32 devices in a mesh: dp: 8 (over y, x, core), ep: 4 (over z).
Axes of the slice: x: 2, y: 2, z: 4, core: 2. Of those that a mesh axis runs over, the one named last changes fastest.
Arguments:
- frames: float32 [2, 8192, 512], P(None, ('dp', 'ep')), may hold values from -6 to 6
- embedding: float32 [2, 8192, 512], P(None, ('dp', 'ep')), may hold values from -6 to 6
- cotangent: float32 [2, 8192, 512], P(None, ('dp', 'ep')), may hold values from -6 to 6
- expert_ids: int32 [2, 2, 8192, 1], P(None, None, ('dp', 'ep')), may hold values from 0 to 3; in each aligned block of 256 rows (0 to 255, 256 to 511, ..., all dimensions but the last counted through in order) at most 128 rows name the same one
- lengths: int32 [2, 8], replicated, may hold values from 256 to 1024, as said below
- norm_gain: float32 [5, 512], replicated, may hold values from 0.5 to 1.5
- norm_bias: float32 [5, 512], replicated, may hold values from -1.8 to 1.8
- router: float32 [2, 512, 4], replicated, may hold values from -0.125 to 0.125
- attention_in: bfloat16 [512, 1536], replicated, may hold values from -0.25 to 0.25
- attention_out: bfloat16 [512, 512], replicated, may hold values from -1 to 1
- slopes: float32 [8], replicated, may hold values from 0.0005 to 0.1
- conv_point: bfloat16 [512, 1024], replicated, may hold values from -0.25 to 0.25
- conv_depth: float32 [15, 512], replicated, may hold values from -1.5 to 1.5
- batch_gain: float32 [512], replicated, may hold values from 0.5 to 1.5
- batch_bias: float32 [512], replicated, may hold values from -1.8 to 1.8
- conv_out: bfloat16 [512, 512], replicated, may hold values from -0.25 to 0.25
- expert_in: bfloat16 [2, 4, 512, 2048], P(None, 'ep'), may hold values from -0.25 to 0.25
- expert_out: bfloat16 [2, 4, 2048, 512], P(None, 'ep'), may hold values from -1.5 to 1.5
Outputs:
- output: float32 [2, 8192, 512], P(None, ('dp', 'ep'))
- frames_grad: float32 [2, 8192, 512], P(None, ('dp', 'ep'))
- norm_gain_grad: float32 [5, 512], replicated
- norm_bias_grad: float32 [5, 512], replicated
- router_grad: float32 [2, 512, 4], replicated
- attention_in_grad: float32 [512, 1536], replicated
- attention_out_grad: float32 [512, 512], replicated
- slopes_grad: float32 [8], replicated
- conv_point_grad: float32 [512, 1024], replicated
- conv_depth_grad: float32 [15, 512], replicated
- batch_gain_grad: float32 [512], replicated
- batch_bias_grad: float32 [512], replicated
- conv_out_grad: float32 [512, 512], replicated
- expert_in_grad: float32 [2, 4, 512, 2048], P(None, 'ep')
- expert_out_grad: float32 [2, 4, 2048, 512], P(None, 'ep')
The draws below stay inside these ranges and needn't reach their ends.
Inputs may be any that keep to these rules, and one draw needn't show every extreme that they name: `expert_ids`: in every aligned block of 256 rows (the frames of one device for one block and micro-batch) no expert is named more than 128 times, a bound that some block reaches. `lengths`: in every micro-batch one utterance, drawn from the seed, is valid in all its frames.
All inputs are finite; a program needn't handle non-finite values.
Results may differ from the reference program's by a relative error of at most 0.0003.
Values sent between devices are 32-bit elements; how exact they have to be, the bound alone decides.
No kernel may reach another device: no remote copies, remote signals or barrier semaphores. Data moves between devices by JAX's collectives and lax.ppermute only.
A program may use at most 384 MiB of HBM per device.

```python
import math
import jax
import jax.numpy as jnp
import numpy as np
from jax import lax

D = 512
FF = 2048
HEADS = 8
HSIZE = 64
KSIZE = 15
MB = 2
T_DEV = 256
EXPERTS = 4
UTT_LEN = 1024
TOKENS = 8192
CAP = 128
N_DP = 8


def draw_lengths(key, part):
    key = jax.random.fold_in(key, 11)
    first, second = jax.random.split(key)
    drawn = jax.random.randint(first, (MB, N_DP), UTT_LEN // 4, UTT_LEN + 1)
    chosen = jax.random.randint(second, (MB, 1), 0, N_DP)
    columns = jnp.arange(N_DP, dtype=jnp.int32)[None, :]
    return jnp.where(columns == chosen, UTT_LEN, drawn).astype(jnp.int32)


def shard_levels(key, extent, shards, low, top_value):
    level = 1.0
    for axis_at, shards_of in shards:
        steps = jax.random.uniform(jax.random.fold_in(jax.random.fold_in(key, 6), axis_at), (shards_of,), jnp.float32, low / len(shards), top_value / len(shards))
        level = level * jnp.repeat(jnp.exp(steps), extent[axis_at] // shards_of).reshape((-1,) + (1,) * (len(extent) - 1 - axis_at))
    return level


def shared_out(key, own, number, rows, count, top, reach, lean):
    ranking = jax.random.permutation(key, count)
    crowded, usual = shares(count, rows * top, reach, lean, True), shares(count, rows * top, reach, lean, False)
    places = jnp.arange(count)

    def named(sizes, turn):
        used = int((sizes > 0).sum())
        fixed = max(1, used // 4)
        shifted = fixed + (places - fixed + turn * (used - fixed)) % max(1, count - fixed)
        return jnp.zeros((count,), jnp.int32).at[ranking[jnp.where(places < fixed, places, shifted)]].set(jnp.asarray(sizes, jnp.int32))

    sizes = jnp.where(number % 4 == 0, named(crowded, number // 4), named(usual, number - number // 4 - 1))
    mixed = jax.random.permutation(jax.random.fold_in(own, 3), count)
    donor, sink = mixed[0:count // 2 * 2:2], mixed[1:count // 2 * 2:2]
    slack = jnp.minimum(sizes[donor] - 1, reach - sizes[sink]) // 2
    slack = jnp.where((donor == ranking[0]) | (sink == ranking[0]) | (sizes[sink] == 0), 0, jnp.maximum(slack, 0))
    shifted = jax.random.randint(jax.random.fold_in(own, 4), (count // 2,), 0, 1 << 20) % (slack + 1)
    sizes = sizes.at[donor].add(-shifted).at[sink].add(shifted)
    labels = jnp.searchsorted(jnp.cumsum(sizes), jnp.arange(rows * top), side="right").astype(jnp.int32)
    grid = labels.reshape(top, rows).T
    grid = grid[jax.random.permutation(jax.random.fold_in(own, 1), rows)]
    turn = jax.random.randint(jax.random.fold_in(own, 2), (rows, 1), 0, top)
    return jnp.take_along_axis(grid, (jnp.arange(top)[None, :] + turn) % top, axis=1)


def shares(number_of, total, bound, slope, full):
    loads = [(1 << 20) // math.isqrt(standing ** slope) + 1 for standing in range(1, number_of + 1)]
    largest = bound if full else min(bound, max(-(-total // number_of), total * loads[0] // sum(loads)))
    least = 1 if total - largest >= number_of - 1 else 0
    given, spare = [largest] + [least] * (number_of - 1), total - largest - least * (number_of - 1)
    while spare > 0:
        free = [i for i in range(1, number_of) if given[i] < largest] or [i for i in range(1, number_of) if given[i] < bound]
        mass, left = sum([loads[i] for i in free]), spare
        for i in free:
            more = min(bound - given[i], max(1, left * loads[i] // mass), spare)
            given[i] = given[i] + more
            spare = spare - more
    return np.array(given)


def normal_values(stream_key, dims, width, limit, pieces=(), kind=jnp.bfloat16):
    level = shard_levels(stream_key, dims, pieces, -0.22, 0.18) if pieces else 1.0
    entries = jax.random.normal(stream_key, dims, jnp.float32) * width * level
    return jnp.minimum(jnp.maximum(entries, -limit), limit).astype(kind)


def setup_inputs(seed: int = 0) -> dict:
    arg_keys = jax.random.split(jax.random.key(seed), 19)
    frames = normal_values(arg_keys[0], (MB, TOKENS, D), 1.0, 6.0, ((1, 32),), jnp.float32)
    embedding = normal_values(arg_keys[1], (MB, TOKENS, D), 1.0, 6.0, ((1, 32),), jnp.float32)
    cotangent = normal_values(arg_keys[2], (MB, TOKENS, D), 1.0, 6.0, ((1, 32),), jnp.float32)
    expert_ids_keys = jax.random.split(jax.random.fold_in(arg_keys[3], 1), 2 * MB * TOKENS // T_DEV)
    expert_ids_turns = jax.random.permutation(jax.random.fold_in(arg_keys[3], 3), 2 * MB * TOKENS // T_DEV)
    expert_ids = jax.vmap(lambda own, number: shared_out(jax.random.fold_in(arg_keys[3], 2), own, number, T_DEV, EXPERTS, 1, CAP, 1))(expert_ids_keys, expert_ids_turns).reshape((2, MB, TOKENS, 1))
    lengths = draw_lengths(jax.random.fold_in(arg_keys[18], 71), 0)
    norm_gain = jnp.clip(1.0 + 0.1 * jax.random.normal(arg_keys[5], (5, D), jnp.float32), 0.5, 1.5)
    norm_bias = normal_values(arg_keys[6], (5, D), 0.3, 1.8, (), jnp.float32)
    router = normal_values(arg_keys[7], (2, D, EXPERTS), (4 * D) ** -0.5, 0.125, (), jnp.float32)
    attention_in = normal_values(arg_keys[8], (D, 3 * D), D ** -0.5, 0.25)
    attention_out = normal_values(arg_keys[9], (D, D), (D // 16) ** -0.5, 1.0)
    slopes = jnp.clip(jnp.exp(jax.random.uniform(arg_keys[10], (HEADS,), jnp.float32, math.log(0.0005), math.log(0.1))), 0.0005, 0.1)
    conv_point = normal_values(arg_keys[11], (D, 2 * D), D ** -0.5, 0.25)
    conv_depth = normal_values(arg_keys[12], (KSIZE, D), KSIZE ** -0.5, 1.5, (), jnp.float32)
    batch_gain = jnp.clip(1.0 + 0.1 * jax.random.normal(arg_keys[13], (D,), jnp.float32), 0.5, 1.5)
    batch_bias = normal_values(arg_keys[14], (D,), 0.3, 1.8, (), jnp.float32)
    conv_out = normal_values(arg_keys[15], (D, D), D ** -0.5, 0.25)
    expert_in = normal_values(arg_keys[16], (2, EXPERTS, D, FF), D ** -0.5, 0.25, ((1, 4),))
    expert_out = normal_values(arg_keys[17], (2, EXPERTS, FF, D), (max(FF // 128, 1)) ** -0.5, 1.5, ((1, 4),))
    return {"frames": frames, "embedding": embedding, "cotangent": cotangent, "expert_ids": expert_ids, "lengths": lengths, "norm_gain": norm_gain, "norm_bias": norm_bias, "router": router, "attention_in": attention_in, "attention_out": attention_out, "slopes": slopes, "conv_point": conv_point, "conv_depth": conv_depth, "batch_gain": batch_gain, "batch_bias": batch_bias, "conv_out": conv_out, "expert_in": expert_in, "expert_out": expert_out}


HIGH = lax.Precision.HIGHEST
EPS = 1e-05
MASKED = -1e+30

@jax.custom_vjp
def low(v):
    return lax.optimization_barrier(v.astype(jnp.bfloat16)).astype(jnp.float32)

@jax.custom_vjp
def low_back(v):
    return v

def low_keep(v):
    return (low(v), None)

def low_pass(kept, grad):
    return (grad,)

def back_keep(v):
    return (v, None)

def back_low(kept, grad):
    return (low(grad),)
low.defvjp(low_keep, low_pass)
low_back.defvjp(back_keep, back_low)

def matmul(left, right):
    return jnp.matmul(left, right, precision=HIGH)

def norm_rows(values, gain, shift):
    center = values - lax.optimization_barrier(jnp.mean(values, axis=-1, keepdims=True))
    spread = lax.optimization_barrier(jnp.mean(center * center, axis=-1, keepdims=True))
    return center * lax.rsqrt(spread + EPS) * gain + shift

def mixture(hidden, embed_rows, ids, gain, shift, router, weight_in, weight_out):
    experts = router.shape[1]
    normed = norm_rows(hidden, gain, shift)
    probs = jax.nn.softmax(matmul(normed + embed_rows, router), axis=-1)
    matches = ids[:, None] == jnp.arange(experts, dtype=jnp.int32)[None, :]
    gate = lax.optimization_barrier(jnp.sum(probs * matches.astype(jnp.float32), axis=-1))
    blocks = hidden.shape[0] // T_DEV
    counted = matches.astype(jnp.int32).reshape(blocks, T_DEV, experts)
    rank = lax.optimization_barrier(jnp.sum((jnp.cumsum(counted, axis=1, dtype=jnp.int32) - 1) * counted, axis=2)).astype(jnp.int32)
    slot = (ids.reshape(blocks, T_DEV) * CAP + rank).astype(jnp.int32)
    block_id = jnp.broadcast_to(jnp.arange(blocks, dtype=jnp.int32)[:, None], (blocks, T_DEV))
    buffer = jnp.zeros((blocks, experts * CAP, D), jnp.float32)
    buffer = buffer.at[block_id, slot].set(normed.reshape(blocks, T_DEV, D))
    buffer = buffer.reshape(blocks, experts, CAP, D)
    pre = jnp.einsum('becd,edf->becf', buffer, weight_in, precision=HIGH)
    result = jnp.einsum('becf,efd->becd', jax.nn.silu(pre), weight_out, precision=HIGH)
    back = result.reshape(blocks, experts * CAP, D)[block_id, slot].reshape(-1, D)
    return hidden + 0.5 * gate[:, None] * back

def attention(hidden, valid, gain, shift, weight_in, weight_out, slopes):
    length = hidden.shape[0]
    packed = matmul(norm_rows(hidden, gain, shift), weight_in)
    query = packed[:, :D].reshape(length, HEADS, HSIZE)
    key = packed[:, D:2 * D].reshape(length, HEADS, HSIZE)
    value = packed[:, 2 * D:].reshape(length, HEADS, HSIZE)
    spots = jnp.arange(length, dtype=jnp.int32)
    distance = jnp.abs(spots[:, None] - spots[None, :]).astype(jnp.float32)
    scores = jnp.einsum('qhc,khc->hqk', query, key, precision=HIGH) / math.sqrt(HSIZE) - slopes[:, None, None] * distance[None]
    scores = jnp.where(valid[None, None, :] > 0.5, scores, MASKED)
    probs = jax.nn.softmax(scores, axis=-1)
    mixed = jnp.einsum('hqk,khc->qhc', probs, value, precision=HIGH).reshape(length, D)
    return matmul(mixed, weight_out)

def conv_front(hidden, valid, gain, shift, point, depth):
    length = hidden.shape[0]
    both = matmul(norm_rows(hidden, gain, shift), point)
    gated = both[:, :D] * jax.nn.sigmoid(both[:, D:]) * valid[:, None]
    half = KSIZE // 2
    padded = jnp.pad(gated, ((half, half), (0, 0)))
    total = depth[0] * padded[0:length]
    for offset in range(1, KSIZE):
        total = total + depth[offset] * padded[offset:offset + length]
    return total

def utterance_front(hidden, embed_rows, ids, valid, weights):
    norm_gain, norm_bias, router, att_in, att_out, slopes, point, depth, batch_gain, batch_bias, project, weight_in, weight_out = weights
    first = mixture(hidden, embed_rows, ids, norm_gain[0], norm_bias[0], router[0], weight_in[0], weight_out[0])
    second = first + attention(first, valid, norm_gain[1], norm_bias[1], att_in, att_out, slopes)
    return (second, conv_front(second, valid, norm_gain[2], norm_bias[2], point, depth))

def utterance_back(second, conv, embed_rows, ids, valid, centre, inverse_dev, weights):
    norm_gain, norm_bias, router, att_in, att_out, slopes, point, depth, batch_gain, batch_bias, project, weight_in, weight_out = weights
    shaped = (conv - centre) * inverse_dev * batch_gain + batch_bias
    third = second + matmul(jax.nn.silu(shaped), project)
    fourth = mixture(third, embed_rows, ids, norm_gain[3], norm_bias[3], router[1], weight_in[1], weight_out[1])
    return norm_rows(fourth, norm_gain[4], norm_bias[4]) * valid[:, None]

def reference(frames, embedding, cotangent, expert_ids, lengths, norm_gain, norm_bias, router, attention_in, attention_out, slopes, conv_point, conv_depth, batch_gain, batch_bias, conv_out, expert_in, expert_out):
    weights = tuple((w.astype(jnp.float32) for w in (norm_gain, norm_bias, router, attention_in, attention_out, slopes, conv_point, conv_depth, batch_gain, batch_bias, conv_out, expert_in, expert_out)))

    def forward(inputs, params):
        results = []
        for step in range(MB):
            valid = (jnp.arange(UTT_LEN, dtype=jnp.int32)[None, :] < lengths[step][:, None]).astype(jnp.float32)
            source = inputs[step].reshape(N_DP, UTT_LEN, D)
            embed_rows = embedding[step].reshape(N_DP, UTT_LEN, D)
            ids_first = expert_ids[0, step, :, 0].reshape(N_DP, UTT_LEN)
            ids_second = expert_ids[1, step, :, 0].reshape(N_DP, UTT_LEN)
            second, conv = lax.map(lambda item: jax.checkpoint(utterance_front)(item[0], item[1], item[2], item[3], params), (source, embed_rows, ids_first, valid))
            count = jnp.sum(lengths[step]).astype(jnp.float32)
            weight_mask = valid[:, :, None]
            centre = lax.optimization_barrier(jnp.sum(conv * weight_mask, axis=(0, 1))) / count
            inverse_dev = lax.rsqrt(lax.optimization_barrier(jnp.sum(conv * conv * weight_mask, axis=(0, 1))) / count - centre * centre + EPS)
            result = lax.map(lambda item: jax.checkpoint(utterance_back)(item[0], item[1], item[2], item[3], item[4], centre, inverse_dev, params), (second, conv, embed_rows, ids_second, valid))
            results.append(result.reshape(TOKENS, D))
        return jnp.stack(results)
    output, pull = jax.vjp(forward, frames.astype(jnp.float32), weights)
    frames_grad, grads = pull(cotangent.astype(jnp.float32))
    return (output, frames_grad, grads[0], grads[1], grads[2], grads[3], grads[4], grads[5], grads[6], grads[7], grads[8], grads[9], grads[10], grads[11], grads[12])
```

```python
import functools

import jax
import jax.numpy as jnp
from jax import lax
from jax.experimental import pallas as pl
from jax.experimental.pallas import tpu as pltpu
from jax.sharding import PartitionSpec as P

HIGH = lax.Precision.HIGH
EPS = 1e-05
FAR = 1e30
LANES = 128


def product(left, right):
    return jnp.matmul(left, right, precision=HIGH)


def after(values, *earlier):
    return lax.optimization_barrier((values,) + earlier)[0]


def swap(values, axis, bit):
    count = lax.axis_size(axis)
    return lax.ppermute(values, axis, [(i, i ^ bit) for i in range(count)])


def bits_of(axis):
    count = lax.axis_size(axis)
    return [(axis, 1 << k) for k in range(count.bit_length() - 1)]


def butterfly(values, steps):
    for axis, bit in steps:
        values = values + swap(values, axis, bit)
    return values


def upper(step):
    axis, bit = step
    return (lax.axis_index(axis) // bit) % 2


def halve(values, step):
    side = upper(step)
    half = values.shape[0] // 2
    keep = lax.dynamic_slice_in_dim(values, side * half, half, 0)
    send = lax.dynamic_slice_in_dim(values, (1 - side) * half, half, 0)
    return keep + swap(send, *step)


def join(values, step):
    side = upper(step)
    other = swap(values, *step)
    half = values.shape[0]
    out = jnp.zeros((2 * half,) + values.shape[1:], values.dtype)
    out = lax.dynamic_update_slice_in_dim(out, values, side * half, 0)
    return lax.dynamic_update_slice_in_dim(out, other, (1 - side) * half, 0)


def reduce_pair(pair, steps, meanwhile):
    first, rest = steps[0], steps[1:]
    orders = [(first,) + tuple(rest), (first,) + tuple(rest[::-1])]
    pair = list(pair)
    for k in range(len(steps)):
        pair = [halve(part, order[k]) for part, order in zip(pair, orders)]
    middle = tuple(pair)
    pair, meanwhile = lax.optimization_barrier((pair, meanwhile))
    for k in range(len(steps) - 1, 0, -1):
        pair = [join(part, order[k]) for part, order in zip(pair, orders)]
    return [(part, swap(part, *first)) for part in pair], upper(first), middle, meanwhile


class Layout:
    def __init__(self, micro, rows, capacity):
        self.micro, self.rows, self.capacity = micro, rows, capacity
        self.ep, self.dp = lax.axis_size("ep"), lax.axis_size("dp")
        self.z, self.d = lax.axis_index("ep"), lax.axis_index("dp")
        self.paired = micro == 2 and self.ep == 4 and self.dp % 2 == 0
        self.core = self.d % 2

    def route(self, low, u, home):
        pairs = []
        for d in range(self.dp):
            for z in range(self.ep):
                there = (d - d % 2 + z // 2) * self.ep + 2 * ((z % 2) ^ u) + (low ^ (d % 2))
                pairs.append((d * self.ep + z, there))
        return [(j, i) for i, j in pairs] if home else pairs

    def piece(self, values, at, count, axis=0):
        return lax.slice_in_dim(values, at * self.capacity, (at + count) * self.capacity, axis=axis)

    def home_slots(self, ids, rank):
        block = jnp.arange(self.micro, dtype=jnp.int32)[:, None]
        if not self.paired:
            return self.work_slots(ids, rank)
        step = ids ^ (2 * block + self.core)
        u = (self.z % 2) ^ (ids // 2)
        return (((step % 2) * 2 + u) * 2 + step // 2) * self.capacity + rank

    def work_slots(self, ids, rank):
        block = jnp.arange(self.micro, dtype=jnp.int32)[:, None]
        step = ids ^ self.z
        groups = self.ep // 2
        inner = block ^ (ids // 2) if self.paired else block
        return ((step % groups * 2 + step // groups) * self.micro + inner) * self.capacity + rank

    def hop(self, values, step):
        return values if step == 0 else swap(values, "ep", step)

    def hops(self, values, group):
        half = values.shape[0] // 2
        return jnp.concatenate(
            [self.hop(values[h * half : (h + 1) * half], group + h * (self.ep // 2)) for h in (0, 1)], axis=0
        )

    def group_of(self, values, group):
        return self.piece(values, group * 2 * self.micro, 2 * self.micro)

    def home_to_expert(self, rows, extra):
        wide = rows.shape[1]
        few = extra.shape[0]
        count = self.micro * self.capacity
        out = []
        last = ()
        for group in range(self.ep // 2):
            got = []
            for u in (0, 1):
                at = (group * 2 + u) * self.micro
                more = self.piece(extra, at, self.micro, 1)
                message = jnp.concatenate(
                    [self.piece(rows, at, self.micro), jnp.pad(more, ((0, 0), (0, wide - count)))], axis=0
                )
                message = after(message, *last)
                if self.paired:
                    got.append(lax.ppermute(message, ("dp", "ep"), self.route(group, u, False)))
                else:
                    got.append(self.hop(message, group + u * (self.ep // 2)))
            last = tuple(got)
            rows_got = [v[:count] for v in got]
            more_got = [v[count:, :count] for v in got]
            if self.paired:
                order = [(u, h) for h in (0, 1) for u in (0, 1)]
                rows_got = [self.piece(rows_got[u], h, 1) for u, h in order]
                more_got = [self.piece(more_got[u], h, 1, 1) for u, h in order]
            out.append((jnp.concatenate(rows_got, axis=0), jnp.concatenate(more_got, axis=1).T))
        return out

    def expert_to_home(self, groups):
        rows_out, more_out = [], []
        count = self.micro * self.capacity
        for group, (rows, more) in enumerate(groups):
            wide = rows.shape[1]
            for u in (0, 1):
                if self.paired:
                    row = jnp.concatenate([self.piece(rows, 2 * h + u, 1) for h in (0, 1)], axis=0)
                    few = jnp.concatenate([self.piece(more, 2 * h + u, 1, 1) for h in (0, 1)], axis=1)
                else:
                    row, few = self.piece(rows, u * self.micro, self.micro), self.piece(more, u * self.micro, self.micro, 1)
                message = jnp.concatenate([row, jnp.pad(few, ((0, 0), (0, wide - count)))], axis=0)
                if self.paired:
                    got = lax.ppermute(message, ("dp", "ep"), self.route(group, u, True))
                else:
                    got = self.hop(message, group + u * (self.ep // 2))
                rows_out.append(got[:count])
                more_out.append(got[count:, :count])
        return jnp.concatenate(rows_out, axis=0), jnp.concatenate(more_out, axis=1)

    def ids_to_work(self, ids):
        if not self.paired:
            return ids
        values = jnp.swapaxes(ids, 1, 2).astype(jnp.float32)
        out = []
        for turn in (0, 1):
            pairs = []
            for d in range(self.dp):
                for z in range(self.ep):
                    m = (z % 2) ^ turn
                    pairs.append((d * self.ep + z, (d - d % 2 + z // 2) * self.ep + 2 * m + d % 2))
            block = lax.dynamic_index_in_dim(values, (self.z % 2) ^ turn, 0, keepdims=False)
            out.append(lax.ppermute(block, ("dp", "ep"), pairs))
        m = self.z // 2
        both = jnp.stack([jnp.where(m == 0, out[0], out[1]), jnp.where(m == 0, out[1], out[0])])
        return jnp.swapaxes(both, 1, 2).astype(jnp.int32)

    def places(self, lengths):
        counts = jnp.sum(lengths, axis=1).astype(jnp.float32)
        if self.paired:
            m = self.z // 2
            place = self.core * 2 * self.rows + jnp.arange(2 * self.rows, dtype=jnp.int32)
            group = self.d - self.core + self.z % 2
            return place, [lengths[m, group]], counts[m][None]
        place = self.z * self.rows + jnp.arange(self.rows, dtype=jnp.int32)
        return place, [lengths[m, self.d] for m in range(self.micro)], counts

    def gather(self, values):
        if self.paired:
            return jnp.concatenate([values, swap(values, "dp", 1)], axis=0)
        return lax.all_gather(values, "ep", axis=0, tiled=True)

    def key_places(self):
        if self.paired:
            base = jnp.arange(2 * self.rows, dtype=jnp.int32)
            return jnp.concatenate([base + self.core * 2 * self.rows, base + (1 - self.core) * 2 * self.rows])
        return jnp.arange(self.ep * self.rows, dtype=jnp.int32)

    def scatter(self, values):
        if self.paired:
            half = values.shape[1] // 2
            return values[:, :half] + swap(values[:, half:], "dp", 1)
        return lax.psum_scatter(values, "ep", scatter_dimension=1, tiled=True)

    def halo(self, values, width):
        length = values.shape[0]
        if self.paired:
            low = self.core == 0
            edge = jnp.where(low, values[length - width :], values[:width])
            other = swap(edge, "dp", 1)
            zero = jnp.zeros_like(other)
            before, after = jnp.where(low, zero, other), jnp.where(low, other, zero)
        else:
            up = [(i, i + 1) for i in range(self.ep - 1)]
            down = [(j, i) for i, j in up]
            before = lax.ppermute(values[length - width :], "ep", up)
            after = lax.ppermute(values[:width], "ep", down)
        return jnp.concatenate([before, values, after], axis=0)

    def batch_total(self, values):
        if self.paired:
            return butterfly(values, bits_of("dp") + [("ep", 1)])
        return butterfly(values, bits_of("dp") + bits_of("ep"))


def norm_rows(values, gain, shift):
    center = values - jnp.mean(values, axis=-1, keepdims=True)
    spread = jnp.mean(center * center, axis=-1, keepdims=True)
    return center * lax.rsqrt(spread + EPS) * gain + shift


def swish_slope(values):
    squash = jax.nn.sigmoid(values)
    return squash * (1.0 + values * (1.0 - squash))


def ranks(ids, experts):
    rows = ids.shape[1]
    onehot = (ids[..., None] == jnp.arange(experts, dtype=jnp.int32)).astype(jnp.float32)
    below = (jnp.arange(rows)[:, None] > jnp.arange(rows)[None, :]).astype(jnp.float32)
    before = jnp.einsum("rs,bse->bre", below, onehot)
    return jnp.sum(before * onehot, axis=2).astype(jnp.int32)


def tables_of(slot, count):
    spots = jnp.arange(count, dtype=jnp.int32)
    flat = slot.reshape(-1)
    return (
        (spots[:, None] == flat[None, :]).astype(jnp.bfloat16),
        (flat[:, None] == spots[None, :]).astype(jnp.bfloat16),
    )


def pick(table, values):
    return jnp.matmul(table.astype(jnp.float32), values, precision=HIGH)


def pick_columns(values, table):
    return jnp.matmul(values, table.astype(jnp.float32), precision=HIGH)


def expert_forward(hidden, extra, own, gain, shift, router, weight_in, weight_out):
    def front(source, gain_now, shift_now, router_now, extra_now):
        normed = norm_rows(source, gain_now, shift_now)
        probs = jax.nn.softmax(product(normed, router_now) + extra_now, axis=-1)
        return (normed, jnp.sum(probs * own, axis=-1))

    (normed, gate), front_pull = jax.vjp(front, hidden, gain, shift, router, extra)
    pre = product(normed, weight_in)
    result = product(jax.nn.silu(pre), weight_out)
    new = hidden + 0.5 * gate[:, None] * result
    return (new, (front_pull, normed, gate, pre, result))


def expert_backward(grad, saved, weight_in, weight_out):
    front_pull, normed, gate, pre, result = saved
    grad_result = 0.5 * gate[:, None] * grad
    grad_gate = 0.5 * jnp.sum(grad * result, axis=1)
    grad_active = jnp.einsum("cd,fd->cf", grad_result, weight_out, precision=HIGH)
    grad_pre = grad_active * swish_slope(pre)
    grad_normed = jnp.einsum("cf,df->cd", grad_pre, weight_in, precision=HIGH)
    grad_hidden, gain_grad, shift_grad, router_grad, extra_grad = front_pull((grad_normed, grad_gate))
    return (grad + grad_hidden, extra_grad, (gain_grad, shift_grad, router_grad), (normed, jax.nn.silu(pre), grad_result, grad_pre))


def expert_weight_grads(kept):
    normed, active, grad_result, grad_pre = kept
    outer = jnp.einsum("cf,cd->fd", active, grad_result, precision=HIGH)
    return jnp.einsum("cd,cf->df", normed, grad_pre, precision=HIGH), outer


def add_up(trees):
    total = trees[0]
    for tree in trees[1:]:
        total = jax.tree.map(jnp.add, total, tree)
    return total


def parted(values):
    head = values.astype(jnp.bfloat16).astype(jnp.float32)
    return head, values - head


def head_lanes(side):
    low = lax.broadcasted_iota(jnp.int32, (1, LANES), 1) < LANES // 2
    turn = lambda v: pltpu.roll(v, LANES // 2, 1)
    at_low = lambda v: v if side == 0 else turn(v)
    at_high = lambda v: turn(v) if side == 0 else v
    both = lambda v, w: jnp.where(low, at_low(v), at_high(w))
    alone = lambda v, rest=0.0: jnp.where(low, at_low(v), rest)
    return both, alone


def dot_nt(left, right):
    return lax.dot_general(left, right, (((1,), (1,)), ((), ())), preferred_element_type=jnp.float32)


def dot_tn(left, right):
    return lax.dot_general(left, right, (((0,), (0,)), ((), ())), preferred_element_type=jnp.float32)


def dot_nn(left, right):
    return lax.dot_general(left, right, (((1,), (0,)), ((), ())), preferred_element_type=jnp.float32)


def narrow(*parts):
    return jnp.concatenate(parts, axis=1).astype(jnp.bfloat16) if len(parts) > 1 else parts[0].astype(jnp.bfloat16)


def attend_kernel(chunk, scale, slopes, dist, q_ref, k_ref, v_ref, out_ref, log_ref, k3, v2, v1, scores):
    pair = pl.program_id(0)
    total = k_ref.shape[0]
    q_hi, q_lo = parted(q_ref[...] * scale)
    k_hi, k_lo = parted(k_ref[...])
    v_hi, v_lo = parted(v_ref[...])
    mixed = []
    for side in (0, 1):
        both, alone = head_lanes(side)
        k3[...] = narrow(both(k_hi, k_hi), alone(k_lo))
        v2[...] = narrow(both(v_hi, v_lo))
        v1[...] = narrow(alone(v_hi))
        q3 = narrow(both(q_hi, q_lo), alone(q_hi))
        slope = slopes[2 * pair + side]
        highest = None
        for at in range(0, total, chunk):
            now = pl.ds(at, chunk)
            score = dot_nt(k3[now], q3) - slope * dist[now]
            scores[now] = score
            top = jnp.max(score, axis=0, keepdims=True)
            highest = top if highest is None else jnp.maximum(highest, top)
        summed, weight = 0.0, 0.0
        for at in range(0, total, chunk):
            now = pl.ds(at, chunk)
            raised = jnp.exp(scores[now] - highest)
            weight = weight + jnp.sum(raised, axis=0, keepdims=True)
            r_hi, r_lo = parted(raised)
            summed = summed + dot_tn(v2[now], narrow(r_hi)) + dot_tn(v1[now], narrow(r_lo))
        mixed.append((summed[: LANES // 2] + summed[LANES // 2 :]) / weight)
        log_ref[0, side : side + 1, :] = highest + jnp.log(weight)
    out_ref[...] = jnp.concatenate(mixed, axis=0).T


def attend_back_kernel(
    chunk, scale, slopes, dist, q_ref, k_ref, v_ref, o_ref, g_ref, log_ref, dq_ref, dkv_ref, ds_ref, k3, v3, k2, k1, hold
):
    pair = pl.program_id(0)
    total = k_ref.shape[0]
    q_hi, q_lo = parted(q_ref[...] * scale)
    k_hi, k_lo = parted(k_ref[...])
    v_hi, v_lo = parted(v_ref[...])
    grad = g_ref[...]
    g_hi, g_lo = parted(grad)
    weighed = grad * o_ref[...]
    lane = lax.broadcasted_iota(jnp.int32, (1, LANES), 1)
    low = lane < LANES // 2
    half = LANES // 2
    grad_query = []
    for side in (0, 1):
        both, alone = head_lanes(side)
        own = low if side == 0 else jnp.logical_not(low)
        centre = -jnp.sum(jnp.where(own, weighed, 0.0), axis=1, keepdims=True)
        c_hi, c_rest = parted(centre)
        c_mid, c_lo = parted(c_rest)
        tail = jnp.where(lane == half, c_hi, jnp.where(lane == half + 1, c_mid, jnp.where(lane == half + 2, c_lo, 0.0)))
        ones = jnp.where(jnp.logical_and(lane >= half, lane < half + 3), 1.0, 0.0)
        k3[...] = narrow(both(k_hi, k_hi), alone(k_lo))
        v3[...] = narrow(both(v_hi, v_hi), alone(v_lo, ones))
        k2[...] = narrow(both(k_hi, k_lo))
        k1[...] = narrow(alone(k_hi))
        q3 = narrow(both(q_hi, q_lo), alone(q_hi))
        q2, q1 = narrow(both(q_hi, q_lo)), narrow(alone(q_hi))
        g3 = narrow(both(g_hi, g_lo), alone(g_hi, tail))
        g2, g1 = narrow(both(g_hi, g_lo)), narrow(alone(g_hi))
        slope = slopes[2 * pair + side]
        logs = log_ref[0, side : side + 1, :]
        slope_grad, query_grad = 0.0, 0.0
        for at in range(0, total, chunk):
            now = pl.ds(at, chunk)
            far = dist[now]
            probs = jnp.exp(dot_nt(k3[now], q3) - slope * far - logs)
            grad_score = probs * dot_nt(v3[now], g3)
            slope_grad = slope_grad + jnp.sum(grad_score * far, axis=0, keepdims=True)
            p_hi, p_lo = parted(probs)
            s_hi, s_lo = parted(grad_score)
            s_hi, s_lo = narrow(s_hi), narrow(s_lo)
            value_grad = dot_nn(narrow(p_hi), g2) + dot_nn(narrow(p_lo), g1)
            key_grad = dot_nn(s_hi, q2) + dot_nn(s_lo, q1)
            query_grad = query_grad + dot_tn(k2[now], s_hi) + dot_tn(k1[now], s_lo)
            value_grad = value_grad + pltpu.roll(value_grad, half, 1)
            key_grad = key_grad + pltpu.roll(key_grad, half, 1)
            if side == 0:
                hold[0, now], hold[1, now] = key_grad, value_grad
            else:
                dkv_ref[0, now] = jnp.where(low, hold[0, now], key_grad)
                dkv_ref[1, now] = jnp.where(low, hold[1, now], value_grad)
        grad_query.append(query_grad[:half] + query_grad[half:])
        ds_ref[0, side : side + 1, :] = slope_grad
    dq_ref[...] = jnp.concatenate(grad_query, axis=0).T * scale


def attend_specs(rows, total, pairs):
    lanes = lambda at: pl.BlockSpec((rows, LANES), lambda i, at=at: (0, at + i))
    wide = lambda at: pl.BlockSpec((total, LANES), lambda i, at=at: (0, at + i))
    return [
        pl.BlockSpec(memory_space=pltpu.SMEM),
        pl.BlockSpec((total, rows), lambda i: (0, 0)),
        lanes(0),
        wide(0),
        wide(pairs),
    ], lanes(0), pl.BlockSpec((1, 8, rows), lambda i: (i, 0, 0))


def attend_params(rows, total, width, passes):
    return dict(
        compiler_params=pltpu.CompilerParams(vmem_limit_bytes=40 * 1024 * 1024),
        cost_estimate=pl.CostEstimate(
            flops=2 * rows * total * width * passes, bytes_accessed=16 * total * width, transcendentals=rows * total * 8
        ),
    )


def attend(packed, both, dist, slopes):
    rows, total = packed.shape[0], both.shape[0]
    width = both.shape[1] // 2
    pairs = width // LANES
    chunk = min(total, 256)
    in_specs, lanes, logs = attend_specs(rows, total, pairs)
    return pl.pallas_call(
        functools.partial(attend_kernel, chunk, (width // slopes.shape[0]) ** -0.5),
        grid=(pairs,),
        in_specs=in_specs,
        out_specs=[lanes, logs],
        out_shape=[
            jax.ShapeDtypeStruct((rows, width), jnp.float32),
            jax.ShapeDtypeStruct((pairs, 8, rows), jnp.float32),
        ],
        scratch_shapes=[
            pltpu.VMEM((total, 2 * LANES), jnp.bfloat16),
            pltpu.VMEM((total, LANES), jnp.bfloat16),
            pltpu.VMEM((total, LANES), jnp.bfloat16),
            pltpu.VMEM((total, rows), jnp.float32),
        ],
        name="attend",
        **attend_params(rows, total, width, 12),
    )(slopes, dist, packed, both, both)


def attend_back(packed, both, dist, slopes, mixed, logs, grad_mixed):
    rows, total = packed.shape[0], both.shape[0]
    width = both.shape[1] // 2
    pairs = width // LANES
    chunk = min(total, 256)
    in_specs, lanes, log_spec = attend_specs(rows, total, pairs)
    dq, dkv, ds = pl.pallas_call(
        functools.partial(attend_back_kernel, chunk, (width // slopes.shape[0]) ** -0.5),
        grid=(pairs,),
        in_specs=in_specs + [lanes, lanes, log_spec],
        out_specs=[lanes, pl.BlockSpec((2, total, LANES), lambda i: (0, 0, i)), log_spec],
        out_shape=[
            jax.ShapeDtypeStruct((rows, width), jnp.float32),
            jax.ShapeDtypeStruct((2, total, width), jnp.float32),
            jax.ShapeDtypeStruct((pairs, 8, rows), jnp.float32),
        ],
        scratch_shapes=[
            pltpu.VMEM((total, 2 * LANES), jnp.bfloat16),
            pltpu.VMEM((total, 2 * LANES), jnp.bfloat16),
            pltpu.VMEM((total, LANES), jnp.bfloat16),
            pltpu.VMEM((total, LANES), jnp.bfloat16),
            pltpu.VMEM((2, total, LANES), jnp.float32),
        ],
        name="attend_back",
        **attend_params(rows, total, width, 30),
    )(slopes, dist, packed, both, both, mixed, grad_mixed, logs)
    return dq, dkv, -jnp.sum(ds[:, :2], axis=2).reshape(-1)


def body(
    frames,
    embedding,
    cotangent,
    expert_ids,
    lengths,
    norm_gain,
    norm_bias,
    router,
    attention_in,
    attention_out,
    slopes,
    conv_point,
    conv_depth,
    batch_gain,
    batch_bias,
    conv_out,
    expert_in,
    expert_out,
):
    packed_weight = attention_in.astype(jnp.float32)
    mixing_weight = attention_out.astype(jnp.float32)
    point_weight = conv_point.astype(jnp.float32)
    project_weight = conv_out.astype(jnp.float32)
    inner_weight = expert_in[:, 0].astype(jnp.float32)
    outer_weight = expert_out[:, 0].astype(jnp.float32)
    micro, rows, width = frames.shape
    experts = router.shape[2]
    heads = slopes.shape[0]
    kernel = conv_depth.shape[0]
    half = kernel // 2
    capacity = 2 * rows // experts
    everyone = bits_of("dp") + bits_of("ep")
    layout = Layout(micro, rows, capacity)
    place, part_lengths, counts = layout.places(lengths)
    key_place = layout.key_places()
    parts = len(part_lengths)
    part_rows = micro * rows // parts
    valid_f = jnp.concatenate([(place < length) for length in part_lengths]).astype(jnp.float32)[:, None]
    to_parts = lambda v: v.reshape((parts, part_rows) + v.shape[1:])
    spread = lambda v: jnp.broadcast_to(v[:, None], (parts, part_rows) + v.shape[1:]).reshape(parts * part_rows, -1)

    slots = experts * micro * capacity
    own = (jnp.arange(experts, dtype=jnp.int32) == layout.z).astype(jnp.float32)[None, :]
    ids = jnp.moveaxis(expert_ids[..., 0], 0, 2)
    rank = [ranks(ids[..., b], experts) for b in (0, 1)]
    home = [tables_of(layout.home_slots(ids[..., b], rank[b]), slots) for b in (0, 1)]
    groups = range(experts // 2)
    home_rows = embedding.reshape(-1, width)
    home_logits = [product(router[b].T, home_rows.T) for b in (0, 1)]
    home_place = layout.z * rows + jnp.arange(rows, dtype=jnp.int32)
    home_valid = (home_place[None, :] < lengths[:, layout.d][:, None]).astype(jnp.float32).reshape(1, -1)
    spare = jnp.zeros((-(experts + 1) % 8, micro * rows), jnp.float32)
    extras = [
        pick_columns(jnp.concatenate([home_logits[b], home_valid, spare], axis=0), home[b][1]) for b in (0, 1)
    ]

    sources = layout.home_to_expert(pick(home[0][0], frames.reshape(-1, width)), extras[0])
    kept_first = []
    back = []
    last = ()
    for group in groups:
        hidden, extra = sources[group]
        new, kept = expert_forward(
            after(hidden, *last),
            extra[:, :experts],
            own,
            norm_gain[0],
            norm_bias[0],
            router[0],
            inner_weight[0],
            outer_weight[0],
        )
        last = (new,)
        kept_first.append(kept)
        back.append(layout.hops(new, group))
    work_ids = layout.ids_to_work(after(ids, sources[-1][0]))
    work = [
        tables_of(layout.work_slots(work_ids[..., b], ranks(work_ids[..., b], experts)), slots) for b in (0, 1)
    ]
    first = pick(work[0][1], jnp.concatenate(back, axis=0))

    def attention_front(values, gain_now, shift_now, weight_now):
        return product(norm_rows(values, gain_now, shift_now), weight_now)

    packed, attention_pull = jax.vjp(attention_front, first, norm_gain[1], norm_bias[1], packed_weight)
    packed, cot_rows = lax.optimization_barrier((packed, cotangent.reshape(-1, width)))
    pulls = layout.home_to_expert(pick(home[1][0], cot_rows), extras[1])
    packed_parts = to_parts(packed)
    apart = jnp.abs(key_place[:, None] - place[None, :]).astype(jnp.float32)
    kept_attention = []
    mixed_parts = []
    for part in range(parts):
        both = layout.gather(packed_parts[part, :, width:])
        dist = jnp.where((key_place < part_lengths[part])[:, None], apart, FAR)
        mixed, logs = attend(packed_parts[part], both, dist, slopes)
        kept_attention.append((both, dist, mixed, logs))
        mixed_parts.append(mixed)
    mixed_all = jnp.concatenate(mixed_parts, axis=0)
    second = first + product(mixed_all, mixing_weight)

    def conv_front(values, gain_now, shift_now, point_now):
        both = product(norm_rows(values, gain_now, shift_now), point_now)
        return both[:, :width] * jax.nn.sigmoid(both[:, width:]) * valid_f

    gated, conv_pull = jax.vjp(conv_front, second, norm_gain[2], norm_bias[2], point_weight)
    padded = [layout.halo(v, half) for v in to_parts(gated)]
    conv_parts = []
    for part in range(parts):
        total = conv_depth[0] * padded[part][0:part_rows]
        for offset in range(1, kernel):
            total = total + conv_depth[offset] * padded[part][offset : offset + part_rows]
        conv_parts.append(total)
    conv = jnp.concatenate(conv_parts, axis=0)
    stats = layout.batch_total(
        jnp.stack([jnp.sum(to_parts(conv * valid_f), axis=1), jnp.sum(to_parts(conv * conv * valid_f), axis=1)], axis=1)
    )
    centre = stats[:, 0] / counts[:, None]
    inverse_dev = lax.rsqrt(stats[:, 1] / counts[:, None] - centre * centre + EPS)
    scaled = (conv - spread(centre)) * spread(inverse_dev)
    shaped = scaled * batch_gain + batch_bias
    swished = jax.nn.silu(shaped)
    third = second + product(swished, project_weight)

    def final(values, gain_now, shift_now, valid_now):
        return norm_rows(values, gain_now, shift_now) * valid_now

    sent = pick(work[1][0], third)
    results, back, kept, small = [], [], [], []
    arrived, last = (), ()
    for group in groups:
        hidden = layout.hops(after(layout.group_of(sent, group), *arrived), group)
        arrived = (hidden,)
        pull_now, extra = pulls[group]
        fourth, saved = expert_forward(
            after(hidden, *last),
            extra[:, :experts],
            own,
            norm_gain[3],
            norm_bias[3],
            router[1],
            inner_weight[1],
            outer_weight[1],
        )
        valid_now = extra[:, experts : experts + 1]
        result, final_pull = jax.vjp(lambda v, g, b: final(v, g, b, valid_now), fourth, norm_gain[4], norm_bias[4])
        grad_fourth, gain_four, shift_four = final_pull(pull_now)
        grad, extra_grad, small_now, kept_now = expert_backward(grad_fourth, saved, inner_weight[1], outer_weight[1])
        last = (grad,)
        results.append((result, jnp.pad(extra_grad.T, ((0, -experts % 8), (0, 0)))))
        kept.append(kept_now)
        small.append(small_now + (gain_four, shift_four))
        back.append(layout.hops(grad, group))
    gain_three, shift_three, router_one, gain_four, shift_four = add_up(small)
    kept, _ = lax.optimization_barrier((kept, back[:-1]))
    inner_one, outer_one = lax.psum(add_up([expert_weight_grads(v) for v in kept]), "dp")
    grad_third = pick(work[1][1], jnp.concatenate(back, axis=0))
    project_grad = product(swished.T, grad_third)
    grad_shaped = product(grad_third, project_weight.T) * swish_slope(shaped)
    sums = jnp.stack(
        [jnp.sum(to_parts(grad_shaped), axis=1), jnp.sum(to_parts(grad_shaped * scaled), axis=1)], axis=1
    )
    totals = layout.batch_total(sums)
    shift_total, gain_total = totals[:, 0], totals[:, 1]
    results, _ = lax.optimization_barrier((results, totals))
    output_slots, logit_slots = layout.expert_to_home(results)
    output = pick(home[1][1], output_slots).reshape(micro, rows, width)
    logit_one = pick_columns(logit_slots[:experts], home[1][0])
    router_one = router_one + product(logit_one, home_rows).T
    grad_conv = (
        batch_gain
        * spread(inverse_dev)
        * (grad_shaped - valid_f * (spread(shift_total) + scaled * spread(gain_total)) / spread(counts[:, None]))
    )
    depth_grad = 0.0
    gated_parts = []
    for part, now in enumerate(to_parts(grad_conv)):
        grad_pad = layout.halo(now, half)
        total = conv_depth[0] * grad_pad[2 * half : 2 * half + part_rows]
        for offset in range(1, kernel):
            total = total + conv_depth[offset] * grad_pad[2 * half - offset : 2 * half - offset + part_rows]
        gated_parts.append(total)
        depth_grad = depth_grad + jnp.stack(
            [jnp.sum(now * padded[part][offset : offset + part_rows], axis=0) for offset in range(kernel)]
        )
    grad_hidden, gain_two, shift_two, point_grad = conv_pull(jnp.concatenate(gated_parts, axis=0))
    grad_second = grad_third + grad_hidden

    mixing_grad = product(mixed_all.T, grad_second)
    grad_mixed = to_parts(product(grad_second, mixing_weight.T))
    packed_back = []
    slope_grad = 0.0
    for part in range(parts):
        both, dist, mixed, logs = kept_attention[part]
        grad_query, grad_both, slope_now = attend_back(
            packed_parts[part], both, dist, slopes, mixed, logs, grad_mixed[part]
        )
        slope_grad = slope_grad + slope_now
        grad_both = layout.scatter(grad_both)
        packed_back.append(jnp.concatenate([grad_query, grad_both[0], grad_both[1]], axis=1))
    grad_hidden, gain_one, shift_one, packed_grad = attention_pull(jnp.concatenate(packed_back, axis=0))
    grad_first = grad_second + grad_hidden
    early = jnp.concatenate(
        [
            jnp.stack([gain_one, gain_two, gain_three, gain_four, shift_one, shift_two, shift_three, shift_four]),
            router_one.T,
            jnp.pad(slope_grad, (0, width - heads))[None],
            depth_grad,
            jnp.sum(sums, axis=0),
        ],
        axis=0,
    )
    few = early.shape[0]
    mixing_grad = jnp.concatenate([mixing_grad, jnp.pad(early, ((0, -few % 8), (0, 0)))], axis=0)
    packed_grad, mixing_grad, project_grad, point_grad = lax.psum(
        after((packed_grad, mixing_grad, project_grad, point_grad), inner_one), ("dp", "ep")
    )
    mixing_grad, early = mixing_grad[:width], mixing_grad[width:]

    sent = pick(work[0][0], grad_first)
    sources, kept, small = [], [], []
    arrived, last = (), ()
    for group in groups:
        grad = layout.hops(after(layout.group_of(sent, group), *arrived), group)
        arrived = (grad,)
        grad, extra_grad, small_now, kept_now = expert_backward(
            after(grad, *last), kept_first[group], inner_weight[0], outer_weight[0]
        )
        last = (grad,)
        sources.append((grad, jnp.pad(extra_grad.T, ((0, -experts % 8), (0, 0)))))
        kept.append(kept_now)
        small.append(small_now)
    gain_zero, shift_zero, router_zero = add_up(small)
    expert_zero = add_up([expert_weight_grads(v) for v in kept])
    dense = (packed_grad, mixing_grad, early, project_grad, point_grad)
    halves_zero, side, middle, dense = reduce_pair(expert_zero, bits_of("dp"), dense)
    packed_grad, mixing_grad, early, project_grad, point_grad = dense
    rows_back, logit_slots = layout.expert_to_home(sources)
    rows_back, logit_slots, inner_one, outer_one, _ = lax.optimization_barrier(
        (rows_back, logit_slots, inner_one, outer_one, middle)
    )
    logit_zero = pick_columns(logit_slots[:experts], home[0][0])
    router_zero = router_zero + product(logit_zero, home_rows).T
    frames_grad = pick(home[0][1], rows_back).reshape(micro, rows, width)
    late = butterfly(
        jnp.concatenate([gain_zero[None], shift_zero[None], router_zero.T], axis=0),
        bits_of("ep") + bits_of("dp"),
    )
    expert_grads = []
    for one, (mine, other) in zip((inner_one, outer_one), halves_zero):
        whole = lax.pad(one[None], 0.0, ((1, 0, 0), (0, 0, 0), (0, 0, 0)))
        half_rows = mine.shape[0]
        whole = lax.dynamic_update_slice(whole, mine[None], (0, side * half_rows, 0))
        expert_grads.append(lax.dynamic_update_slice(whole, other[None], (0, (1 - side) * half_rows, 0))[:, None])

    at = 8 + experts
    gain_grad = jnp.concatenate([late[:1], early[:4]], axis=0)
    shift_grad = jnp.concatenate([late[1:2], early[4:8]], axis=0)
    router_grad = jnp.stack([late[2 : 2 + experts].T, early[8:at].T])
    return (
        output,
        frames_grad,
        gain_grad,
        shift_grad,
        router_grad,
        packed_grad,
        mixing_grad,
        early[at, :heads],
        point_grad,
        early[at + 1 : at + 1 + kernel],
        early[at + 2 + kernel],
        early[at + 1 + kernel],
        project_grad,
        expert_grads[0],
        expert_grads[1],
    )


def solution(mesh):
    rows = P(None, ("dp", "ep"), None)
    whole = P()
    split = P(None, "ep", None, None)
    return jax.shard_map(
        body,
        mesh=mesh,
        in_specs=(rows, rows, rows, P(None, None, ("dp", "ep"), None)) + (whole,) * 12 + (split, split),
        out_specs=(rows, rows) + (whole,) * 11 + (split, split),
        check_vma=False,
    )
```

```python
import functools

import jax
import jax.numpy as jnp
from jax import lax
from jax.experimental import pallas as pl
from jax.experimental.pallas import tpu as pltpu
from jax.sharding import PartitionSpec as P

HIGH = lax.Precision.HIGH
EPS = 1e-05
FAR = 1e30
LANES = 128
BRIEF = pl.CostEstimate(flops=1, bytes_accessed=1, transcendentals=0)


def product(left, right):
    return jnp.matmul(left, right, precision=HIGH)


def after(values, *earlier):
    return lax.optimization_barrier((values,) + earlier)[0]


def swap(values, axis, bit):
    count = lax.axis_size(axis)
    return lax.ppermute(values, axis, [(i, i ^ bit) for i in range(count)])


def bits_of(axis):
    count = lax.axis_size(axis)
    return [(axis, 1 << k) for k in range(count.bit_length() - 1)]


def butterfly(values, steps):
    for axis, bit in steps:
        values = values + swap(values, axis, bit)
    return values


def upper(step):
    axis, bit = step
    return (lax.axis_index(axis) // bit) % 2


def halve(values, step):
    side = upper(step)
    half = values.shape[0] // 2
    keep = lax.dynamic_slice_in_dim(values, side * half, half, 0)
    send = lax.dynamic_slice_in_dim(values, (1 - side) * half, half, 0)
    return keep + swap(send, *step)


def join(values, step):
    side = upper(step)
    other = swap(values, *step)
    half = values.shape[0]
    out = jnp.zeros((2 * half,) + values.shape[1:], values.dtype)
    out = lax.dynamic_update_slice_in_dim(out, values, side * half, 0)
    return lax.dynamic_update_slice_in_dim(out, other, (1 - side) * half, 0)


class DenseSum:
    def __init__(self, pair):
        first, *rest = bits_of("dp")
        far = bits_of("ep")[::-1]
        self.orders = [[first] + rest + far, [first] + rest[::-1] + far]
        self.parts = list(pair)
        count = len(self.orders[0])
        self.ways = [(halve, k) for k in range(count)] + [(join, k) for k in range(count - 1, -1, -1)]

    def step(self, value, count=1):
        for _ in range(count):
            way, k = self.ways.pop(0)
            self.parts = [way(part, order[k]) for part, order in zip(self.parts, self.orders)]
        value, self.parts = lax.optimization_barrier((value, self.parts))
        return value


class Layout:
    def __init__(self, micro, rows, capacity):
        self.micro, self.rows, self.capacity = micro, rows, capacity
        self.ep, self.dp = lax.axis_size("ep"), lax.axis_size("dp")
        self.z, self.d = lax.axis_index("ep"), lax.axis_index("dp")
        self.paired = micro == 2 and self.ep == 4 and self.dp % 2 == 0
        self.core = self.d % 2

    def route(self, low, u, home):
        pairs = []
        for d in range(self.dp):
            for z in range(self.ep):
                there = (d - d % 2 + z // 2) * self.ep + 2 * ((z % 2) ^ u) + (low ^ (d % 2))
                pairs.append((d * self.ep + z, there))
        return [(j, i) for i, j in pairs] if home else pairs

    def piece(self, values, at, count, axis=0):
        return lax.slice_in_dim(values, at * self.capacity, (at + count) * self.capacity, axis=axis)

    def home_slots(self, ids, rank):
        block = jnp.arange(self.micro, dtype=jnp.int32)[:, None]
        if not self.paired:
            return self.work_slots(ids, rank)
        step = ids ^ (2 * block + self.core)
        u = (self.z % 2) ^ (ids // 2)
        return (((step % 2) * 2 + u) * 2 + step // 2) * self.capacity + rank

    def work_slots(self, ids, rank):
        block = jnp.arange(self.micro, dtype=jnp.int32)[:, None]
        step = ids ^ self.z
        groups = self.ep // 2
        inner = block ^ (ids // 2) if self.paired else block
        return ((step % groups * 2 + step // groups) * self.micro + inner) * self.capacity + rank

    def hop(self, values, step):
        return values if step == 0 else swap(values, "ep", step)

    def hops(self, values, group):
        half = values.shape[0] // 2
        return [self.hop(values[h * half : (h + 1) * half], group + h * (self.ep // 2)) for h in (0, 1)]

    def group_of(self, values, group):
        return self.piece(values, group * 2 * self.micro, 2 * self.micro)

    def home_to_expert(self, rows, extra):
        wide = rows.shape[1]
        few = extra.shape[0]
        count = self.micro * self.capacity
        out = []
        last = ()
        for group in range(self.ep // 2):
            got = []
            for u in (0, 1):
                at = (group * 2 + u) * self.micro
                more = self.piece(extra, at, self.micro, 1)
                message = jnp.concatenate(
                    [self.piece(rows, at, self.micro), jnp.pad(more, ((0, 0), (0, wide - count)))], axis=0
                )
                message = after(message, *last)
                if self.paired:
                    got.append(lax.ppermute(message, ("dp", "ep"), self.route(group, u, False)))
                else:
                    got.append(self.hop(message, group + u * (self.ep // 2)))
            last = tuple(got)
            rows_got = [v[:count] for v in got]
            more_got = [v[count:, :count] for v in got]
            if self.paired:
                order = [(u, h) for h in (0, 1) for u in (0, 1)]
                rows_got = [self.piece(rows_got[u], h, 1) for u, h in order]
                more_got = [self.piece(more_got[u], h, 1, 1) for u, h in order]
            out.append((jnp.concatenate(rows_got, axis=0), jnp.concatenate(more_got, axis=1)))
        return out

    def expert_to_home(self, groups):
        messages = []
        for group, (rows, more) in enumerate(groups):
            wide = rows.shape[1]
            for u in (0, 1):
                if self.paired:
                    row = jnp.concatenate([self.piece(rows, 2 * h + u, 1) for h in (0, 1)], axis=0)
                    few = jnp.concatenate([self.piece(more, 2 * h + u, 1, 1) for h in (0, 1)], axis=1)
                else:
                    row, few = self.piece(rows, u * self.micro, self.micro), self.piece(more, u * self.micro, self.micro, 1)
                message = row
                if more.shape[0]:
                    message = jnp.concatenate([row, jnp.pad(few, ((0, 0), (0, wide - few.shape[1])))], axis=0)
                if self.paired:
                    messages.append(lax.ppermute(message, ("dp", "ep"), self.route(group, u, True)))
                else:
                    messages.append(self.hop(message, group + u * (self.ep // 2)))
        return messages

    def opened(self, messages):
        count = self.micro * self.capacity
        return (
            jnp.concatenate([v[:count] for v in messages], axis=0),
            jnp.concatenate([v[count:, :count] for v in messages], axis=1),
        )

    def ids_to_work(self, ids):
        if not self.paired:
            return ids
        values = jnp.swapaxes(ids, 1, 2).astype(jnp.float32)
        out = []
        for turn in (0, 1):
            pairs = []
            for d in range(self.dp):
                for z in range(self.ep):
                    m = (z % 2) ^ turn
                    pairs.append((d * self.ep + z, (d - d % 2 + z // 2) * self.ep + 2 * m + d % 2))
            block = lax.dynamic_index_in_dim(values, (self.z % 2) ^ turn, 0, keepdims=False)
            out.append(lax.ppermute(block, ("dp", "ep"), pairs))
        m = self.z // 2
        both = jnp.stack([jnp.where(m == 0, out[0], out[1]), jnp.where(m == 0, out[1], out[0])])
        return jnp.swapaxes(both, 1, 2).astype(jnp.int32)

    def places(self, lengths):
        counts = jnp.sum(lengths, axis=1).astype(jnp.float32)
        if self.paired:
            m = self.z // 2
            place = self.core * 2 * self.rows + jnp.arange(2 * self.rows, dtype=jnp.int32)
            group = self.d - self.core + self.z % 2
            return place, [lengths[m, group]], counts[m][None]
        place = self.z * self.rows + jnp.arange(self.rows, dtype=jnp.int32)
        return place, [lengths[m, self.d] for m in range(self.micro)], counts

    def gather(self, values):
        if self.paired:
            return jnp.concatenate([values, swap(values, "dp", 1)], axis=0)
        return lax.all_gather(values, "ep", axis=0, tiled=True)

    def key_places(self):
        if self.paired:
            base = jnp.arange(2 * self.rows, dtype=jnp.int32)
            return jnp.concatenate([base + self.core * 2 * self.rows, base + (1 - self.core) * 2 * self.rows])
        return jnp.arange(self.ep * self.rows, dtype=jnp.int32)

    def scatter(self, values):
        if self.paired:
            half = values.shape[1] // 2
            return values[:, :half] + swap(values[:, half:], "dp", 1)
        return lax.psum_scatter(values, "ep", scatter_dimension=1, tiled=True)

    def halo(self, values, width):
        length = values.shape[0]
        if self.paired:
            low = self.core == 0
            edge = jnp.where(low, values[length - width :], values[:width])
            other = swap(edge, "dp", 1)
            zero = jnp.zeros_like(other)
            before, after = jnp.where(low, zero, other), jnp.where(low, other, zero)
        else:
            up = [(i, i + 1) for i in range(self.ep - 1)]
            down = [(j, i) for i, j in up]
            before = lax.ppermute(values[length - width :], "ep", up)
            after = lax.ppermute(values[:width], "ep", down)
        return jnp.concatenate([before, values, after], axis=0)

    def batch_total(self, values):
        if self.paired:
            return butterfly(values, bits_of("dp") + [("ep", 1)])
        return butterfly(values, bits_of("dp") + bits_of("ep"))


def norm_rows(values, gain, shift):
    center = values - jnp.mean(values, axis=-1, keepdims=True)
    spread = jnp.mean(center * center, axis=-1, keepdims=True)
    return center * lax.rsqrt(spread + EPS) * gain + shift


def swish_slope(values):
    squash = jax.nn.sigmoid(values)
    return squash * (1.0 + values * (1.0 - squash))


def ranks(ids, experts):
    rows = ids.shape[1]
    onehot = (ids[..., None] == jnp.arange(experts, dtype=jnp.int32)).astype(jnp.float32)
    below = (jnp.arange(rows)[:, None] > jnp.arange(rows)[None, :]).astype(jnp.float32)
    before = jnp.einsum("rs,bse->bre", below, onehot)
    return jnp.sum(before * onehot, axis=2).astype(jnp.int32)


def tables_of(slot, count):
    spots = jnp.arange(count, dtype=jnp.int32)
    flat = slot.reshape(-1)
    return (
        (spots[:, None] == flat[None, :]).astype(jnp.bfloat16),
        (flat[:, None] == spots[None, :]).astype(jnp.bfloat16),
    )


def pick(table, values):
    return jnp.matmul(table.astype(jnp.float32), values, precision=HIGH)


def pick_columns(values, table):
    return jnp.matmul(values, table.astype(jnp.float32), precision=HIGH)


def product_two(left, right, dot):
    head, rest = parted(left)
    return dot(narrow(head), right) + dot(narrow(rest), right)


def exact_dot(left, right, contract):
    return lax.dot_general(
        left, right, (contract, ((), ())), precision=lax.Precision.HIGHEST, preferred_element_type=jnp.float32
    )


def norm_parts(values):
    center = values - jnp.mean(values, axis=1, keepdims=True)
    scale = lax.rsqrt(jnp.mean(center * center, axis=1, keepdims=True) + EPS)
    return center * scale, scale


def norm_back(grad, gain, normal, scale):
    weighed = grad * gain
    centred = weighed - jnp.mean(weighed, axis=1, keepdims=True)
    return scale * (centred - normal * jnp.mean(weighed * normal, axis=1, keepdims=True))


def gate_parts(hidden, extra, own, norm, router, experts):
    normal, scale = norm_parts(hidden)
    normed = normal * norm[0:1] + norm[1:2]
    lane = lax.broadcasted_iota(jnp.int32, (1, LANES), 1)
    logits = exact_dot(normed, router, ((1,), (0,))) + extra
    logits = jnp.where(lane < experts, logits, -FAR)
    raised = jnp.exp(logits - jnp.max(logits, axis=1, keepdims=True))
    probs = raised / jnp.sum(raised, axis=1, keepdims=True)
    return normal, scale, normed, probs, jnp.sum(probs * own, axis=1, keepdims=True)


def hidden_columns(weight_in):
    wide = min(512, weight_in.shape[1])
    return [pl.ds(at, wide) for at in range(0, weight_in.shape[1], wide)]


def forward_part(hidden, extra, own, norm, router, weight_in, weight_out, pre, experts):
    parts = gate_parts(hidden, extra, own, norm, router, experts)
    result = 0.0
    for now in hidden_columns(weight_in):
        before = product_two(parts[2], weight_in[:, now], dot_nn)
        pre[:, now] = before
        result = result + product_two(before * jax.nn.sigmoid(before), weight_out[now, :], dot_nn)
    return parts, result, hidden + 0.5 * parts[4] * result


def backward_part(grad, result, parts, own, norm, router, weight_in, weight_out, pre, active, grad_pre):
    normal, scale, normed, probs, gate = parts
    grad_result = 0.5 * gate * grad
    grad_gate = 0.5 * jnp.sum(grad * result, axis=1, keepdims=True)
    grad_logits = grad_gate * probs * (own - gate)
    grad_normed = exact_dot(grad_logits, router, ((1,), (1,)))
    for now in hidden_columns(weight_in):
        before = pre[:, now]
        squash = jax.nn.sigmoid(before)
        active[:, now] = before * squash
        slope = squash * (1.0 + before * (1.0 - squash))
        now_grad = product_two(grad_result, weight_out[now, :], dot_nt) * slope
        grad_pre[:, now] = now_grad
        grad_normed = grad_normed + product_two(now_grad, weight_in[:, now], dot_nt)
    sums = [jnp.sum(grad_normed * normal, axis=0, keepdims=True), jnp.sum(grad_normed, axis=0, keepdims=True)]
    return grad + norm_back(grad_normed, norm[0:1], normal, scale), grad_result, grad_logits, sums


def add_rows(out, rows):
    @pl.when(pl.program_id(0) == 0)
    def _():
        out[...] = jnp.zeros_like(out)

    for at, row in enumerate(rows):
        out[at : at + 1, :] += row


def forward_kernel(experts, hidden, extra, own, norm, router, weight_in, weight_out, new, result, pre):
    _, result[...], new[...] = forward_part(
        hidden[...], extra[...], own[...], norm[...], router[...], weight_in, weight_out, pre, experts
    )


def backward_kernel(
    experts, hidden, extra, grad, result, pre, own, norm, router, weight_in, weight_out,
    back, logits, normed, active, grad_result, grad_pre, sums,
):
    parts = gate_parts(hidden[...], extra[...], own[...], norm[...], router[...], experts)
    back[...], grad_result[...], logits[...], rows = backward_part(
        grad[...], result[...], parts, own[...], norm[...], router[...], weight_in, weight_out, pre, active, grad_pre
    )
    normed[...] = parts[2]
    add_rows(sums, rows)


def both_kernel(
    experts, hidden, extra, pull, own, norm, last, router, weight_in, weight_out,
    output, back, logits, normed, active, grad_result, grad_pre, sums, pre,
):
    parts, result, new = forward_part(
        hidden[...], extra[...], own[...], norm[...], router[...], weight_in, weight_out, pre, experts
    )
    lane = lax.broadcasted_iota(jnp.int32, (1, LANES), 1)
    valid = jnp.sum(jnp.where(lane == experts, extra[...], 0.0), axis=1, keepdims=True)
    normal, scale = norm_parts(new)
    output[...] = (normal * last[0:1] + last[1:2]) * valid
    grad = pull[...] * valid
    last_sums = [jnp.sum(grad * normal, axis=0, keepdims=True), jnp.sum(grad, axis=0, keepdims=True)]
    back[...], grad_result[...], logits[...], rows = backward_part(
        norm_back(grad, last[0:1], normal, scale), result, parts, own[...], norm[...], router[...],
        weight_in, weight_out, pre, active, grad_pre,
    )
    normed[...] = parts[2]
    add_rows(sums, rows + last_sums)


def expert_call(kernel, name, experts, by_rows, fixed, widths, sums, hold, products):
    rows, width = by_rows[0].shape
    block = min(256, rows)
    row_spec = lambda wide: pl.BlockSpec((block, wide), lambda i: (i, 0))
    full = lambda v: pl.BlockSpec(v.shape, lambda i: (0, 0))
    out_specs = [row_spec(wide) for wide in widths]
    out_shape = [jax.ShapeDtypeStruct((rows, wide), jnp.float32) for wide in widths]
    if sums:
        out_specs.append(pl.BlockSpec((8, width), lambda i: (0, 0)))
        out_shape.append(jax.ShapeDtypeStruct((8, width), jnp.float32))
    inner = fixed[-2].shape[1]
    return pl.pallas_call(
        functools.partial(kernel, experts),
        grid=(rows // block,),
        in_specs=[row_spec(v.shape[1]) for v in by_rows] + [full(v) for v in fixed],
        out_specs=out_specs,
        out_shape=out_shape,
        scratch_shapes=[pltpu.VMEM((block, inner), jnp.float32)] if hold else [],
        compiler_params=pltpu.CompilerParams(vmem_limit_bytes=48 * 1024 * 1024),
        cost_estimate=BRIEF,
        name=name,
    )(*by_rows, *fixed)


def lanes_of(extra):
    return jnp.pad(extra.T, ((0, 0), (0, LANES - extra.shape[0])))


def weight_kernel(groups, *refs):
    normed, grad_result, active, grad_pre = (refs[k * groups : (k + 1) * groups] for k in range(4))
    inner, outer = refs[4 * groups :]

    def summed(left, right):
        total = 0.0
        for one, two in zip(left, right):
            (a_hi, a_lo), (b_hi, b_lo) = parted(one[...]), parted(two[...])
            a_hi, a_lo, b_hi, b_lo = narrow(a_hi), narrow(a_lo), narrow(b_hi), narrow(b_lo)
            total = total + dot_tn(a_hi, b_hi) + dot_tn(a_lo, b_hi) + dot_tn(a_hi, b_lo)
        return total

    outer[...] = summed(active, grad_result)
    inner[...] = summed(normed, grad_pre)


def expert_weight_grads(kept):
    normed, active, grad_result, grad_pre = zip(*kept)
    rows, width = normed[0].shape
    inner = active[0].shape[1]
    wide = min(512, inner)
    full = pl.BlockSpec((rows, width), lambda i: (0, 0))
    part = pl.BlockSpec((rows, wide), lambda i: (0, i))
    count = len(kept)
    return pl.pallas_call(
        functools.partial(weight_kernel, count),
        grid=(inner // wide,),
        in_specs=[full] * (2 * count) + [part] * (2 * count),
        out_specs=[pl.BlockSpec((width, wide), lambda i: (0, i)), pl.BlockSpec((wide, width), lambda i: (i, 0))],
        out_shape=[
            jax.ShapeDtypeStruct((width, inner), jnp.float32),
            jax.ShapeDtypeStruct((inner, width), jnp.float32),
        ],
        compiler_params=pltpu.CompilerParams(vmem_limit_bytes=48 * 1024 * 1024),
        cost_estimate=pl.CostEstimate(
            flops=12 * count * rows * width * inner, bytes_accessed=16 * count * rows * inner, transcendentals=0
        ),
        name="weights",
    )(*normed, *grad_result, *active, *grad_pre)


def add_up(trees):
    total = trees[0]
    for tree in trees[1:]:
        total = jax.tree.map(jnp.add, total, tree)
    return total


def parted(values):
    head = values.astype(jnp.bfloat16).astype(jnp.float32)
    return head, values - head


def head_lanes(side):
    low = lax.broadcasted_iota(jnp.int32, (1, LANES), 1) < LANES // 2
    turn = lambda v: pltpu.roll(v, LANES // 2, 1)
    at_low = lambda v: v if side == 0 else turn(v)
    at_high = lambda v: turn(v) if side == 0 else v
    both = lambda v, w: jnp.where(low, at_low(v), at_high(w))
    alone = lambda v, rest=0.0: jnp.where(low, at_low(v), rest)
    return both, alone


def dot_nt(left, right):
    return lax.dot_general(left, right, (((1,), (1,)), ((), ())), preferred_element_type=jnp.float32)


def dot_tn(left, right):
    return lax.dot_general(left, right, (((0,), (0,)), ((), ())), preferred_element_type=jnp.float32)


def dot_nn(left, right):
    return lax.dot_general(left, right, (((1,), (0,)), ((), ())), preferred_element_type=jnp.float32)


def narrow(*parts):
    return jnp.concatenate(parts, axis=1).astype(jnp.bfloat16) if len(parts) > 1 else parts[0].astype(jnp.bfloat16)


def attend_kernel(chunk, scale, slopes, dist, q_ref, k_ref, v_ref, out_ref, log_ref, k3, v2, v1, scores):
    pair = pl.program_id(0)
    total = k_ref.shape[0]
    q_hi, q_lo = parted(q_ref[...] * scale)
    k_hi, k_lo = parted(k_ref[...])
    v_hi, v_lo = parted(v_ref[...])
    mixed = []
    for side in (0, 1):
        both, alone = head_lanes(side)
        k3[...] = narrow(both(k_hi, k_hi), alone(k_lo))
        v2[...] = narrow(both(v_hi, v_lo))
        v1[...] = narrow(alone(v_hi))
        q3 = narrow(both(q_hi, q_lo), alone(q_hi))
        slope = slopes[2 * pair + side]
        highest = None
        for at in range(0, total, chunk):
            now = pl.ds(at, chunk)
            score = dot_nt(k3[now], q3) - slope * dist[now]
            scores[now] = score
            top = jnp.max(score, axis=0, keepdims=True)
            highest = top if highest is None else jnp.maximum(highest, top)
        summed, weight = 0.0, 0.0
        for at in range(0, total, chunk):
            now = pl.ds(at, chunk)
            raised = jnp.exp(scores[now] - highest)
            weight = weight + jnp.sum(raised, axis=0, keepdims=True)
            r_hi, r_lo = parted(raised)
            summed = summed + dot_tn(v2[now], narrow(r_hi)) + dot_tn(v1[now], narrow(r_lo))
        mixed.append((summed[: LANES // 2] + summed[LANES // 2 :]) / weight)
        log_ref[0, side : side + 1, :] = highest + jnp.log(weight)
    out_ref[...] = jnp.concatenate(mixed, axis=0).T


def attend_back_kernel(
    chunk, scale, slopes, dist, q_ref, k_ref, v_ref, o_ref, g_ref, log_ref, dq_ref, dkv_ref, ds_ref, k3, v3, k2, k1, hold
):
    pair = pl.program_id(0)
    total = k_ref.shape[0]
    q_hi, q_lo = parted(q_ref[...] * scale)
    k_hi, k_lo = parted(k_ref[...])
    v_hi, v_lo = parted(v_ref[...])
    grad = g_ref[...]
    g_hi, g_lo = parted(grad)
    weighed = grad * o_ref[...]
    lane = lax.broadcasted_iota(jnp.int32, (1, LANES), 1)
    low = lane < LANES // 2
    half = LANES // 2
    grad_query = []
    for side in (0, 1):
        both, alone = head_lanes(side)
        own = low if side == 0 else jnp.logical_not(low)
        centre = -jnp.sum(jnp.where(own, weighed, 0.0), axis=1, keepdims=True)
        c_hi, c_rest = parted(centre)
        c_mid, c_lo = parted(c_rest)
        tail = jnp.where(lane == half, c_hi, jnp.where(lane == half + 1, c_mid, jnp.where(lane == half + 2, c_lo, 0.0)))
        ones = jnp.where(jnp.logical_and(lane >= half, lane < half + 3), 1.0, 0.0)
        k3[...] = narrow(both(k_hi, k_hi), alone(k_lo))
        v3[...] = narrow(both(v_hi, v_hi), alone(v_lo, ones))
        k2[...] = narrow(both(k_hi, k_lo))
        k1[...] = narrow(alone(k_hi))
        q3 = narrow(both(q_hi, q_lo), alone(q_hi))
        q2, q1 = narrow(both(q_hi, q_lo)), narrow(alone(q_hi))
        g3 = narrow(both(g_hi, g_lo), alone(g_hi, tail))
        g2, g1 = narrow(both(g_hi, g_lo)), narrow(alone(g_hi))
        slope = slopes[2 * pair + side]
        logs = log_ref[0, side : side + 1, :]
        slope_grad, query_grad = 0.0, 0.0
        for at in range(0, total, chunk):
            now = pl.ds(at, chunk)
            far = dist[now]
            probs = jnp.exp(dot_nt(k3[now], q3) - slope * far - logs)
            grad_score = probs * dot_nt(v3[now], g3)
            slope_grad = slope_grad + jnp.sum(grad_score * far, axis=0, keepdims=True)
            p_hi, p_lo = parted(probs)
            s_hi, s_lo = parted(grad_score)
            s_hi, s_lo = narrow(s_hi), narrow(s_lo)
            value_grad = dot_nn(narrow(p_hi), g2) + dot_nn(narrow(p_lo), g1)
            key_grad = dot_nn(s_hi, q2) + dot_nn(s_lo, q1)
            query_grad = query_grad + dot_tn(k2[now], s_hi) + dot_tn(k1[now], s_lo)
            value_grad = value_grad + pltpu.roll(value_grad, half, 1)
            key_grad = key_grad + pltpu.roll(key_grad, half, 1)
            if side == 0:
                hold[0, now], hold[1, now] = key_grad, value_grad
            else:
                dkv_ref[0, now] = jnp.where(low, hold[0, now], key_grad)
                dkv_ref[1, now] = jnp.where(low, hold[1, now], value_grad)
        grad_query.append(query_grad[:half] + query_grad[half:])
        ds_ref[0, side : side + 1, :] = slope_grad
    dq_ref[...] = jnp.concatenate(grad_query, axis=0).T * scale


def attend_specs(rows, total, pairs):
    lanes = lambda at: pl.BlockSpec((rows, LANES), lambda i, at=at: (0, at + i))
    wide = lambda at: pl.BlockSpec((total, LANES), lambda i, at=at: (0, at + i))
    return [
        pl.BlockSpec(memory_space=pltpu.SMEM),
        pl.BlockSpec((total, rows), lambda i: (0, 0)),
        lanes(0),
        wide(0),
        wide(pairs),
    ], lanes(0), pl.BlockSpec((1, 8, rows), lambda i: (i, 0, 0))


def attend_params(rows, total, width, passes):
    return dict(
        compiler_params=pltpu.CompilerParams(vmem_limit_bytes=40 * 1024 * 1024),
        cost_estimate=BRIEF,
    )


def attend(packed, both, dist, slopes):
    rows, total = packed.shape[0], both.shape[0]
    width = both.shape[1] // 2
    pairs = width // LANES
    chunk = min(total, 256)
    in_specs, lanes, logs = attend_specs(rows, total, pairs)
    return pl.pallas_call(
        functools.partial(attend_kernel, chunk, (width // slopes.shape[0]) ** -0.5),
        grid=(pairs,),
        in_specs=in_specs,
        out_specs=[lanes, logs],
        out_shape=[
            jax.ShapeDtypeStruct((rows, width), jnp.float32),
            jax.ShapeDtypeStruct((pairs, 8, rows), jnp.float32),
        ],
        scratch_shapes=[
            pltpu.VMEM((total, 2 * LANES), jnp.bfloat16),
            pltpu.VMEM((total, LANES), jnp.bfloat16),
            pltpu.VMEM((total, LANES), jnp.bfloat16),
            pltpu.VMEM((total, rows), jnp.float32),
        ],
        name="attend",
        **attend_params(rows, total, width, 12),
    )(slopes, dist, packed, both, both)


def attend_back(packed, both, dist, slopes, mixed, logs, grad_mixed):
    rows, total = packed.shape[0], both.shape[0]
    width = both.shape[1] // 2
    pairs = width // LANES
    chunk = min(total, 256)
    in_specs, lanes, log_spec = attend_specs(rows, total, pairs)
    dq, dkv, ds = pl.pallas_call(
        functools.partial(attend_back_kernel, chunk, (width // slopes.shape[0]) ** -0.5),
        grid=(pairs,),
        in_specs=in_specs + [lanes, lanes, log_spec],
        out_specs=[lanes, pl.BlockSpec((2, total, LANES), lambda i: (0, 0, i)), log_spec],
        out_shape=[
            jax.ShapeDtypeStruct((rows, width), jnp.float32),
            jax.ShapeDtypeStruct((2, total, width), jnp.float32),
            jax.ShapeDtypeStruct((pairs, 8, rows), jnp.float32),
        ],
        scratch_shapes=[
            pltpu.VMEM((total, 2 * LANES), jnp.bfloat16),
            pltpu.VMEM((total, 2 * LANES), jnp.bfloat16),
            pltpu.VMEM((total, LANES), jnp.bfloat16),
            pltpu.VMEM((total, LANES), jnp.bfloat16),
            pltpu.VMEM((2, total, LANES), jnp.float32),
        ],
        name="attend_back",
        **attend_params(rows, total, width, 30),
    )(slopes, dist, packed, both, both, mixed, grad_mixed, logs)
    return dq, dkv, -jnp.sum(ds[:, :2], axis=2).reshape(-1)


def body(
    frames,
    embedding,
    cotangent,
    expert_ids,
    lengths,
    norm_gain,
    norm_bias,
    router,
    attention_in,
    attention_out,
    slopes,
    conv_point,
    conv_depth,
    batch_gain,
    batch_bias,
    conv_out,
    expert_in,
    expert_out,
):
    packed_weight = attention_in.astype(jnp.float32)
    mixing_weight = attention_out.astype(jnp.float32)
    point_weight = conv_point.astype(jnp.float32)
    project_weight = conv_out.astype(jnp.float32)
    inner_weight = [expert_in[b, 0] for b in (0, 1)]
    outer_weight = [expert_out[b, 0] for b in (0, 1)]
    micro, rows, width = frames.shape
    experts = router.shape[2]
    heads = slopes.shape[0]
    kernel = conv_depth.shape[0]
    half = kernel // 2
    capacity = 2 * rows // experts
    everyone = bits_of("dp") + bits_of("ep")
    layout = Layout(micro, rows, capacity)
    place, part_lengths, counts = layout.places(lengths)
    key_place = layout.key_places()
    parts = len(part_lengths)
    part_rows = micro * rows // parts
    valid_f = jnp.concatenate([(place < length) for length in part_lengths]).astype(jnp.float32)[:, None]
    to_parts = lambda v: v.reshape((parts, part_rows) + v.shape[1:])
    spread = lambda v: jnp.broadcast_to(v[:, None], (parts, part_rows) + v.shape[1:]).reshape(parts * part_rows, -1)

    slots = experts * micro * capacity
    own = (jnp.arange(LANES, dtype=jnp.int32) == layout.z).astype(jnp.float32)[None, :]
    norms = [jnp.stack([norm_gain[i], norm_bias[i]]) for i in range(norm_gain.shape[0])]
    routers = [jnp.pad(router[b], ((0, 0), (0, LANES - experts))) for b in (0, 1)]
    wide = inner_weight[0].shape[1]
    ids = jnp.moveaxis(expert_ids[..., 0], 0, 2)
    rank = [ranks(ids[..., b], experts) for b in (0, 1)]
    home = [tables_of(layout.home_slots(ids[..., b], rank[b]), slots) for b in (0, 1)]
    groups = range(experts // 2)
    home_rows = embedding.reshape(-1, width)
    home_logits = [product(router[b].T, home_rows.T) for b in (0, 1)]
    home_place = layout.z * rows + jnp.arange(rows, dtype=jnp.int32)
    home_valid = (home_place[None, :] < lengths[:, layout.d][:, None]).astype(jnp.float32).reshape(1, -1)
    spare = jnp.zeros((-(experts + 1) % 8, micro * rows), jnp.float32)
    extras = [
        pick_columns(jnp.concatenate([home_logits[b], home_valid, spare], axis=0), home[b][1]) for b in (0, 1)
    ]

    sources = layout.home_to_expert(pick(home[0][0], frames.reshape(-1, width)), extras[0])
    kept_first = []
    back = []
    last = ()
    for group in groups:
        hidden, extra = sources[group]
        hidden, extra = after(hidden, *last), lanes_of(extra)
        fixed = (own, norms[0], routers[0], inner_weight[0], outer_weight[0])
        new, result, pre = expert_call(
            forward_kernel, "forward", experts, (hidden, extra), fixed, (width, width, wide), False, False, 2
        )
        last = (new,)
        kept_first.append(((hidden, extra), (result, pre), fixed))
        back += layout.hops(new, group)
    work_ids = layout.ids_to_work(after(ids, sources[-1][0]))
    work = [
        tables_of(layout.work_slots(work_ids[..., b], ranks(work_ids[..., b], experts)), slots) for b in (0, 1)
    ]
    first = pick(work[0][1], jnp.concatenate(back, axis=0))

    def attention_front(values, gain_now, shift_now, weight_now):
        return product(norm_rows(values, gain_now, shift_now), weight_now)

    packed, attention_pull = jax.vjp(attention_front, first, norm_gain[1], norm_bias[1], packed_weight)
    packed, cot_rows = lax.optimization_barrier((packed, cotangent.reshape(-1, width)))
    pulls = layout.home_to_expert(pick(home[1][0], cot_rows), extras[1])
    packed_parts = to_parts(packed)
    apart = jnp.abs(key_place[:, None] - place[None, :]).astype(jnp.float32)
    kept_attention = []
    mixed_parts = []
    for part in range(parts):
        both = layout.gather(packed_parts[part, :, width:])
        dist = jnp.where((key_place < part_lengths[part])[:, None], apart, FAR)
        mixed, logs = attend(packed_parts[part], both, dist, slopes)
        kept_attention.append((both, dist, mixed, logs))
        mixed_parts.append(mixed)
    mixed_all = jnp.concatenate(mixed_parts, axis=0)
    second = first + product(mixed_all, mixing_weight)

    def conv_front(values, gain_now, shift_now, point_now):
        both = product(norm_rows(values, gain_now, shift_now), point_now)
        return both[:, :width] * jax.nn.sigmoid(both[:, width:]) * valid_f

    gated, conv_pull = jax.vjp(conv_front, second, norm_gain[2], norm_bias[2], point_weight)
    padded = [layout.halo(v, half) for v in to_parts(gated)]
    conv_parts = []
    for part in range(parts):
        total = conv_depth[0] * padded[part][0:part_rows]
        for offset in range(1, kernel):
            total = total + conv_depth[offset] * padded[part][offset : offset + part_rows]
        conv_parts.append(total)
    conv = jnp.concatenate(conv_parts, axis=0)
    stats = layout.batch_total(
        jnp.stack([jnp.sum(to_parts(conv * valid_f), axis=1), jnp.sum(to_parts(conv * conv * valid_f), axis=1)], axis=1)
    )
    centre = stats[:, 0] / counts[:, None]
    inverse_dev = lax.rsqrt(stats[:, 1] / counts[:, None] - centre * centre + EPS)
    scaled = (conv - spread(centre)) * spread(inverse_dev)
    shaped = scaled * batch_gain + batch_bias
    swished = jax.nn.silu(shaped)
    third = second + product(swished, project_weight)

    sent = pick(work[1][0], third)
    results, back, kept, small = [], [], [], []
    arrived, last = (), ()
    for group in groups:
        hidden = layout.hops(after(layout.group_of(sent, group), *arrived), group)
        arrived = tuple(hidden)
        pull_now, extra = pulls[group]
        result, grad, grad_logits, normed, active, grad_result, grad_pre, sums = expert_call(
            both_kernel,
            "both",
            experts,
            (jnp.concatenate(after(hidden, *last), axis=0), lanes_of(extra), pull_now),
            (own, norms[3], norms[4], routers[1], inner_weight[1], outer_weight[1]),
            (width, width, LANES, width, wide, width, wide),
            True,
            True,
            4,
        )
        last = (grad,)
        results.append((result, grad_logits[:, : experts + (-experts % 8)].T))
        kept.append((normed, active, grad_result, grad_pre))
        small.append((sums, product(normed.T, grad_logits[:, :experts])))
        back += layout.hops(grad, group)
    sums, router_one = add_up(small)
    gain_three, shift_three, gain_four, shift_four = (sums[k] for k in range(4))
    kept, _ = lax.optimization_barrier((kept, back[:-2]))
    expert_one = lax.psum(expert_weight_grads(kept), "dp")
    grad_third = pick(work[1][1], jnp.concatenate(back, axis=0))
    project_grad = product(swished.T, grad_third)
    grad_shaped = product(grad_third, project_weight.T) * swish_slope(shaped)
    sums = jnp.stack(
        [jnp.sum(to_parts(grad_shaped), axis=1), jnp.sum(to_parts(grad_shaped * scaled), axis=1)], axis=1
    )
    totals = layout.batch_total(sums)
    shift_total, gain_total = totals[:, 0], totals[:, 1]
    results, _ = lax.optimization_barrier((results, totals))
    output_slots, logit_slots = layout.opened(layout.expert_to_home(results))
    output = pick(home[1][1], output_slots).reshape(micro, rows, width)
    logit_one = pick_columns(logit_slots[:experts], home[1][0])
    router_one = router_one + product(logit_one, home_rows).T
    grad_conv = (
        batch_gain
        * spread(inverse_dev)
        * (grad_shaped - valid_f * (spread(shift_total) + scaled * spread(gain_total)) / spread(counts[:, None]))
    )
    depth_grad = 0.0
    gated_parts = []
    for part, now in enumerate(to_parts(grad_conv)):
        grad_pad = layout.halo(now, half)
        total = conv_depth[0] * grad_pad[2 * half : 2 * half + part_rows]
        for offset in range(1, kernel):
            total = total + conv_depth[offset] * grad_pad[2 * half - offset : 2 * half - offset + part_rows]
        gated_parts.append(total)
        depth_grad = depth_grad + jnp.stack(
            [jnp.sum(now * padded[part][offset : offset + part_rows], axis=0) for offset in range(kernel)]
        )
    grad_hidden, gain_two, shift_two, point_grad = conv_pull(jnp.concatenate(gated_parts, axis=0))
    grad_second = grad_third + grad_hidden

    mixing_grad = product(mixed_all.T, grad_second)
    grad_mixed = to_parts(product(grad_second, mixing_weight.T))
    packed_back = []
    slope_grad = 0.0
    for part in range(parts):
        both, dist, mixed, logs = kept_attention[part]
        grad_query, grad_both, slope_now = attend_back(
            packed_parts[part], both, dist, slopes, mixed, logs, grad_mixed[part]
        )
        slope_grad = slope_grad + slope_now
        grad_both = layout.scatter(grad_both)
        packed_back.append(jnp.concatenate([grad_query, grad_both[0], grad_both[1]], axis=1))
    grad_hidden, gain_one, shift_one, packed_grad = attention_pull(jnp.concatenate(packed_back, axis=0))
    grad_first = grad_second + grad_hidden
    early = jnp.concatenate(
        [
            jnp.stack([gain_one, gain_two, gain_three, gain_four, shift_one, shift_two, shift_three, shift_four]),
            router_one.T,
            jnp.pad(slope_grad, (0, width - heads))[None],
            depth_grad,
            jnp.sum(sums, axis=0),
        ],
        axis=0,
    )
    dense = DenseSum(
        [jnp.concatenate([packed_grad, project_grad], axis=1), jnp.concatenate([mixing_grad, point_grad], axis=1)]
    )
    over_dp, over_ep = len(bits_of("dp")), len(bits_of("ep"))

    sent = pick(work[0][0], grad_first)
    sources, kept, small = [], [], []
    arrived, last = (), ()
    for group in groups:
        grad = layout.hops(after(layout.group_of(sent, group), *arrived), group)
        arrived = tuple(grad)
        grad = after(grad, *last)
        if group == 0:
            grad, expert_one = lax.optimization_barrier((dense.step(grad), expert_one))
        if group == 1:
            grad = dense.step(grad)
        (hidden, extra), saved, fixed = kept_first[group]
        new, grad_logits, normed, active, grad_result, grad_pre, sums = expert_call(
            backward_kernel,
            "backward",
            experts,
            (hidden, extra, jnp.concatenate(grad, axis=0)) + saved,
            fixed,
            (width, LANES, width, wide, width, wide),
            True,
            False,
            2,
        )
        if group == 0:
            new = dense.step(new, over_dp - 2)
        if group == 1:
            new = dense.step(new, over_ep - 1)
        last = (new,)
        sources.append((new, grad_logits[:, : experts + (-experts % 8)].T))
        kept.append((normed, active, grad_result, grad_pre))
        small.append((sums, product(normed.T, grad_logits[:, :experts])))
    sums, router_zero = add_up(small)
    gain_zero, shift_zero = sums[0], sums[1]
    expert_zero = lax.psum(expert_weight_grads(kept), "dp")
    sources = dense.step(sources, over_ep + 1)
    frame_messages = layout.expert_to_home(sources)
    frame_messages = dense.step(frame_messages, over_dp - 1)
    rows_back, logit_slots = layout.opened(frame_messages)
    logit_zero = pick_columns(logit_slots[:experts], home[0][0])
    router_zero = router_zero + product(logit_zero, home_rows).T
    frames_grad = pick(home[0][1], rows_back).reshape(micro, rows, width)
    late = jnp.concatenate([gain_zero[None], shift_zero[None], router_zero.T, early], axis=0)
    late = butterfly(dense.step(late), bits_of("ep") + bits_of("dp"))
    late, early = late[: 2 + experts], late[2 + experts :]
    packed_grad, project_grad = dense.parts[0][:, : 3 * width], dense.parts[0][:, 3 * width :]
    mixing_grad, point_grad = dense.parts[1][:, :width], dense.parts[1][:, width:]
    expert_grads = []
    for zero, one in zip(expert_zero, expert_one):
        whole = lax.optimization_barrier(lax.pad(after(one, late)[None], 0.0, ((1, 0, 0), (0, 0, 0), (0, 0, 0))))
        expert_grads.append(lax.dynamic_update_slice(whole, zero[None], (0, 0, 0))[:, None])

    at = 8 + experts
    gain_grad = jnp.concatenate([late[:1], early[:4]], axis=0)
    shift_grad = jnp.concatenate([late[1:2], early[4:8]], axis=0)
    router_grad = jnp.stack([late[2 : 2 + experts].T, early[8:at].T])
    return (
        output,
        frames_grad,
        gain_grad,
        shift_grad,
        router_grad,
        packed_grad,
        mixing_grad,
        early[at, :heads],
        point_grad,
        early[at + 1 : at + 1 + kernel],
        early[at + 2 + kernel],
        early[at + 1 + kernel],
        project_grad,
        expert_grads[0],
        expert_grads[1],
    )


def solution(mesh):
    rows = P(None, ("dp", "ep"), None)
    whole = P()
    split = P(None, "ep", None, None)
    return jax.shard_map(
        body,
        mesh=mesh,
        in_specs=(rows, rows, rows, P(None, None, ("dp", "ep"), None)) + (whole,) * 12 + (split, split),
        out_specs=(rows, rows) + (whole,) * 11 + (split, split),
        check_vma=False,
    )
```

```python
import functools

import jax
import jax.numpy as jnp
from jax import lax
from jax.experimental import pallas as pl
from jax.experimental.pallas import tpu as pltpu
from jax.sharding import PartitionSpec as P

HIGH = lax.Precision.HIGH
EPS = 1e-05
FAR = 1e30
LANES = 128
BRIEF = pl.CostEstimate(flops=1, bytes_accessed=1, transcendentals=0)


def product(left, right):
    return jnp.matmul(left, right, precision=HIGH)


def after(values, *earlier):
    return lax.optimization_barrier((values,) + earlier)[0]


def swap(values, axis, bit):
    count = lax.axis_size(axis)
    return lax.ppermute(values, axis, [(i, i ^ bit) for i in range(count)])


def bits_of(axis):
    count = lax.axis_size(axis)
    return [(axis, 1 << k) for k in range(count.bit_length() - 1)]


def butterfly(values, steps):
    for axis, bit in steps:
        values = values + swap(values, axis, bit)
    return values


def upper(step):
    axis, bit = step
    return (lax.axis_index(axis) // bit) % 2


def halve(values, step):
    side = upper(step)
    half = values.shape[0] // 2
    keep = lax.dynamic_slice_in_dim(values, side * half, half, 0)
    send = lax.dynamic_slice_in_dim(values, (1 - side) * half, half, 0)
    return keep + swap(send, *step)


def join(values, step):
    side = upper(step)
    other = swap(values, *step)
    half = values.shape[0]
    out = jnp.zeros((2 * half,) + values.shape[1:], values.dtype)
    out = lax.dynamic_update_slice_in_dim(out, values, side * half, 0)
    return lax.dynamic_update_slice_in_dim(out, other, (1 - side) * half, 0)


class DenseSum:
    def __init__(self, pair):
        first, *rest = bits_of("dp")
        far = bits_of("ep")[::-1]
        self.orders = [[first] + rest + far, [first] + rest[::-1] + far]
        self.parts = list(pair)
        count = len(self.orders[0])
        self.ways = [(halve, k) for k in range(count)] + [(join, k) for k in range(count - 1, -1, -1)]

    def step(self, value, count=1):
        for _ in range(count):
            way, k = self.ways.pop(0)
            self.parts = [way(part, order[k]) for part, order in zip(self.parts, self.orders)]
        value, self.parts = lax.optimization_barrier((value, self.parts))
        return value


class Layout:
    def __init__(self, micro, rows, capacity):
        self.micro, self.rows, self.capacity = micro, rows, capacity
        self.ep, self.dp = lax.axis_size("ep"), lax.axis_size("dp")
        self.z, self.d = lax.axis_index("ep"), lax.axis_index("dp")
        self.paired = micro == 2 and self.ep == 4 and self.dp % 2 == 0
        self.core = self.d % 2

    def route(self, low, u, home):
        pairs = []
        for d in range(self.dp):
            for z in range(self.ep):
                there = (d - d % 2 + z // 2) * self.ep + 2 * ((z % 2) ^ u) + (low ^ (d % 2))
                pairs.append((d * self.ep + z, there))
        return [(j, i) for i, j in pairs] if home else pairs

    def piece(self, values, at, count, axis=0):
        return lax.slice_in_dim(values, at * self.capacity, (at + count) * self.capacity, axis=axis)

    def home_slots(self, ids, rank):
        block = jnp.arange(self.micro, dtype=jnp.int32)[:, None]
        if not self.paired:
            return self.work_slots(ids, rank)
        step = ids ^ (2 * block + self.core)
        u = (self.z % 2) ^ (ids // 2)
        return (((step % 2) * 2 + u) * 2 + step // 2) * self.capacity + rank

    def work_slots(self, ids, rank):
        block = jnp.arange(self.micro, dtype=jnp.int32)[:, None]
        step = ids ^ self.z
        groups = self.ep // 2
        inner = block ^ (ids // 2) if self.paired else block
        return ((step % groups * 2 + step // groups) * self.micro + inner) * self.capacity + rank

    def hop(self, values, step):
        return values if step == 0 else swap(values, "ep", step)

    def hops(self, values, group):
        half = values.shape[0] // 2
        return [self.hop(values[h * half : (h + 1) * half], group + h * (self.ep // 2)) for h in (0, 1)]

    def group_of(self, values, group):
        return self.piece(values, group * 2 * self.micro, 2 * self.micro)

    def home_to_expert(self, rows, extra, ahead=()):
        wide = rows.shape[1]
        few = extra.shape[0]
        count = self.micro * self.capacity
        out = []
        last = ()
        for group in range(self.ep // 2):
            got = []
            for u in (0, 1):
                at = (group * 2 + u) * self.micro
                more = self.piece(extra, at, self.micro, 1)
                message = jnp.concatenate(
                    [self.piece(rows, at, self.micro), jnp.pad(more, ((0, 0), (0, wide - count)))], axis=0
                )
                message = after(message, *last)
                if self.paired:
                    got.append(lax.ppermute(message, ("dp", "ep"), self.route(group, u, False)))
                else:
                    got.append(self.hop(message, group + u * (self.ep // 2)))
            last = tuple(got) + tuple(ahead)
            rows_got = [v[:count] for v in got]
            more_got = [v[count:, :count] for v in got]
            if self.paired:
                order = [(u, h) for h in (0, 1) for u in (0, 1)]
                rows_got = [self.piece(rows_got[u], h, 1) for u, h in order]
                more_got = [self.piece(more_got[u], h, 1, 1) for u, h in order]
            out.append((jnp.concatenate(rows_got, axis=0), jnp.concatenate(more_got, axis=1)))
        return out

    def expert_to_home(self, groups):
        messages = []
        for group, (rows, more) in enumerate(groups):
            wide = rows.shape[1]
            for u in (0, 1):
                if self.paired:
                    row = jnp.concatenate([self.piece(rows, 2 * h + u, 1) for h in (0, 1)], axis=0)
                    few = jnp.concatenate([self.piece(more, 2 * h + u, 1, 1) for h in (0, 1)], axis=1)
                else:
                    row, few = self.piece(rows, u * self.micro, self.micro), self.piece(more, u * self.micro, self.micro, 1)
                message = row
                if more.shape[0]:
                    message = jnp.concatenate([row, jnp.pad(few, ((0, 0), (0, wide - few.shape[1])))], axis=0)
                if self.paired:
                    messages.append(lax.ppermute(message, ("dp", "ep"), self.route(group, u, True)))
                else:
                    messages.append(self.hop(message, group + u * (self.ep // 2)))
        return messages

    def opened(self, messages):
        count = self.micro * self.capacity
        return (
            jnp.concatenate([v[:count] for v in messages], axis=0),
            jnp.concatenate([v[count:, :count] for v in messages], axis=1),
        )

    def ids_to_work(self, ids):
        if not self.paired:
            return ids
        values = jnp.swapaxes(ids, 1, 2).astype(jnp.float32)
        out = []
        for turn in (0, 1):
            pairs = []
            for d in range(self.dp):
                for z in range(self.ep):
                    m = (z % 2) ^ turn
                    pairs.append((d * self.ep + z, (d - d % 2 + z // 2) * self.ep + 2 * m + d % 2))
            block = lax.dynamic_index_in_dim(values, (self.z % 2) ^ turn, 0, keepdims=False)
            out.append(lax.ppermute(block, ("dp", "ep"), pairs))
        m = self.z // 2
        both = jnp.stack([jnp.where(m == 0, out[0], out[1]), jnp.where(m == 0, out[1], out[0])])
        return jnp.swapaxes(both, 1, 2).astype(jnp.int32)

    def places(self, lengths):
        counts = jnp.sum(lengths, axis=1).astype(jnp.float32)
        if self.paired:
            m = self.z // 2
            place = self.core * 2 * self.rows + jnp.arange(2 * self.rows, dtype=jnp.int32)
            group = self.d - self.core + self.z % 2
            return place, [lengths[m, group]], counts[m][None]
        place = self.z * self.rows + jnp.arange(self.rows, dtype=jnp.int32)
        return place, [lengths[m, self.d] for m in range(self.micro)], counts

    def gather(self, values):
        if self.paired:
            return jnp.concatenate([values, swap(values, "dp", 1)], axis=0)
        return lax.all_gather(values, "ep", axis=0, tiled=True)

    def key_places(self):
        if self.paired:
            base = jnp.arange(2 * self.rows, dtype=jnp.int32)
            return jnp.concatenate([base + self.core * 2 * self.rows, base + (1 - self.core) * 2 * self.rows])
        return jnp.arange(self.ep * self.rows, dtype=jnp.int32)

    def scatter(self, values):
        if self.paired:
            half = values.shape[1] // 2
            return values[:, :half] + swap(values[:, half:], "dp", 1)
        return lax.psum_scatter(values, "ep", scatter_dimension=1, tiled=True)

    def halo(self, values, width):
        length = values.shape[0]
        if self.paired:
            low = self.core == 0
            edge = jnp.where(low, values[length - width :], values[:width])
            other = swap(edge, "dp", 1)
            zero = jnp.zeros_like(other)
            before, after = jnp.where(low, zero, other), jnp.where(low, other, zero)
        else:
            up = [(i, i + 1) for i in range(self.ep - 1)]
            down = [(j, i) for i, j in up]
            before = lax.ppermute(values[length - width :], "ep", up)
            after = lax.ppermute(values[:width], "ep", down)
        return jnp.concatenate([before, values, after], axis=0)

    def batch_total(self, values):
        if self.paired:
            return butterfly(values, bits_of("dp") + [("ep", 1)])
        return butterfly(values, bits_of("dp") + bits_of("ep"))


def norm_rows(values, gain, shift):
    center = values - jnp.mean(values, axis=-1, keepdims=True)
    spread = jnp.mean(center * center, axis=-1, keepdims=True)
    return center * lax.rsqrt(spread + EPS) * gain + shift


def swish_slope(values):
    squash = jax.nn.sigmoid(values)
    return squash * (1.0 + values * (1.0 - squash))


def ranks(ids, experts):
    rows = ids.shape[1]
    onehot = (ids[..., None] == jnp.arange(experts, dtype=jnp.int32)).astype(jnp.float32)
    below = (jnp.arange(rows)[:, None] > jnp.arange(rows)[None, :]).astype(jnp.float32)
    before = jnp.einsum("rs,bse->bre", below, onehot)
    return jnp.sum(before * onehot, axis=2).astype(jnp.int32)


def tables_of(slot, count):
    spots = jnp.arange(count, dtype=jnp.int32)
    flat = slot.reshape(-1)
    return (
        (spots[:, None] == flat[None, :]).astype(jnp.bfloat16),
        (flat[:, None] == spots[None, :]).astype(jnp.bfloat16),
    )


def pick(table, values):
    return jnp.matmul(table.astype(jnp.float32), values, precision=HIGH)


def pick_columns(values, table):
    return jnp.matmul(values, table.astype(jnp.float32), precision=HIGH)


def product_two(left, right, dot):
    head, rest = parted(left)
    return dot(narrow(head), right) + dot(narrow(rest), right)


def exact_dot(left, right, contract):
    return lax.dot_general(
        left, right, (contract, ((), ())), precision=lax.Precision.HIGHEST, preferred_element_type=jnp.float32
    )


def norm_parts(values):
    center = values - jnp.mean(values, axis=1, keepdims=True)
    scale = lax.rsqrt(jnp.mean(center * center, axis=1, keepdims=True) + EPS)
    return center * scale, scale


def norm_back(grad, gain, normal, scale):
    weighed = grad * gain
    centred = weighed - jnp.mean(weighed, axis=1, keepdims=True)
    return scale * (centred - normal * jnp.mean(weighed * normal, axis=1, keepdims=True))


def gate_parts(hidden, extra, own, norm, router, experts):
    normal, scale = norm_parts(hidden)
    normed = normal * norm[0:1] + norm[1:2]
    lane = lax.broadcasted_iota(jnp.int32, (1, LANES), 1)
    logits = exact_dot(normed, router, ((1,), (0,))) + extra
    logits = jnp.where(lane < experts, logits, -FAR)
    raised = jnp.exp(logits - jnp.max(logits, axis=1, keepdims=True))
    probs = raised / jnp.sum(raised, axis=1, keepdims=True)
    return normal, scale, normed, probs, jnp.sum(probs * own, axis=1, keepdims=True)


def hidden_columns(weight_in):
    wide = min(512, weight_in.shape[1])
    return [pl.ds(at, wide) for at in range(0, weight_in.shape[1], wide)]


def forward_part(hidden, extra, own, norm, router, weight_in, weight_out, pre, experts):
    parts = gate_parts(hidden, extra, own, norm, router, experts)
    result = 0.0
    for now in hidden_columns(weight_in):
        before = product_two(parts[2], weight_in[:, now], dot_nn)
        pre[:, now] = before
        result = result + product_two(before * jax.nn.sigmoid(before), weight_out[now, :], dot_nn)
    return parts, result, hidden + 0.5 * parts[4] * result


def backward_part(grad, result, parts, own, norm, router, weight_in, weight_out, pre, active, grad_pre):
    normal, scale, normed, probs, gate = parts
    grad_result = 0.5 * gate * grad
    grad_gate = 0.5 * jnp.sum(grad * result, axis=1, keepdims=True)
    grad_logits = grad_gate * probs * (own - gate)
    grad_normed = exact_dot(grad_logits, router, ((1,), (1,)))
    for now in hidden_columns(weight_in):
        before = pre[:, now]
        squash = jax.nn.sigmoid(before)
        active[:, now] = before * squash
        slope = squash * (1.0 + before * (1.0 - squash))
        now_grad = product_two(grad_result, weight_out[now, :], dot_nt) * slope
        grad_pre[:, now] = now_grad
        grad_normed = grad_normed + product_two(now_grad, weight_in[:, now], dot_nt)
    sums = [jnp.sum(grad_normed * normal, axis=0, keepdims=True), jnp.sum(grad_normed, axis=0, keepdims=True)]
    return grad + norm_back(grad_normed, norm[0:1], normal, scale), grad_result, grad_logits, sums


def add_rows(out, rows):
    @pl.when(pl.program_id(0) == 0)
    def _():
        out[...] = jnp.zeros_like(out)

    for at, row in enumerate(rows):
        out[at : at + 1, :] += row


def forward_kernel(experts, hidden, extra, own, norm, router, weight_in, weight_out, new, result, pre):
    _, result[...], new[...] = forward_part(
        hidden[...], extra[...], own[...], norm[...], router[...], weight_in, weight_out, pre, experts
    )


def backward_kernel(
    experts, hidden, extra, grad, result, pre, own, norm, router, weight_in, weight_out,
    back, logits, normed, active, grad_result, grad_pre, sums,
):
    parts = gate_parts(hidden[...], extra[...], own[...], norm[...], router[...], experts)
    back[...], grad_result[...], logits[...], rows = backward_part(
        grad[...], result[...], parts, own[...], norm[...], router[...], weight_in, weight_out, pre, active, grad_pre
    )
    normed[...] = parts[2]
    add_rows(sums, rows)


def both_kernel(
    experts, hidden, extra, pull, own, norm, last, router, weight_in, weight_out,
    output, back, logits, normed, active, grad_result, grad_pre, sums, pre,
):
    parts, result, new = forward_part(
        hidden[...], extra[...], own[...], norm[...], router[...], weight_in, weight_out, pre, experts
    )
    lane = lax.broadcasted_iota(jnp.int32, (1, LANES), 1)
    valid = jnp.sum(jnp.where(lane == experts, extra[...], 0.0), axis=1, keepdims=True)
    normal, scale = norm_parts(new)
    output[...] = (normal * last[0:1] + last[1:2]) * valid
    grad = pull[...] * valid
    last_sums = [jnp.sum(grad * normal, axis=0, keepdims=True), jnp.sum(grad, axis=0, keepdims=True)]
    back[...], grad_result[...], logits[...], rows = backward_part(
        norm_back(grad, last[0:1], normal, scale), result, parts, own[...], norm[...], router[...],
        weight_in, weight_out, pre, active, grad_pre,
    )
    normed[...] = parts[2]
    add_rows(sums, rows + last_sums)


def expert_call(kernel, name, experts, by_rows, fixed, widths, sums, hold, products):
    rows, width = by_rows[0].shape
    block = min(256, rows)
    row_spec = lambda wide: pl.BlockSpec((block, wide), lambda i: (i, 0))
    full = lambda v: pl.BlockSpec(v.shape, lambda i: (0, 0))
    out_specs = [row_spec(wide) for wide in widths]
    out_shape = [jax.ShapeDtypeStruct((rows, wide), jnp.float32) for wide in widths]
    if sums:
        out_specs.append(pl.BlockSpec((8, width), lambda i: (0, 0)))
        out_shape.append(jax.ShapeDtypeStruct((8, width), jnp.float32))
    inner = fixed[-2].shape[1]
    return pl.pallas_call(
        functools.partial(kernel, experts),
        grid=(rows // block,),
        in_specs=[row_spec(v.shape[1]) for v in by_rows] + [full(v) for v in fixed],
        out_specs=out_specs,
        out_shape=out_shape,
        scratch_shapes=[pltpu.VMEM((block, inner), jnp.float32)] if hold else [],
        compiler_params=pltpu.CompilerParams(vmem_limit_bytes=48 * 1024 * 1024),
        cost_estimate=BRIEF,
        name=name,
    )(*by_rows, *fixed)


def lanes_of(extra):
    return jnp.pad(extra.T, ((0, 0), (0, LANES - extra.shape[0])))


def weight_kernel(groups, *refs):
    normed, grad_result, active, grad_pre = (refs[k * groups : (k + 1) * groups] for k in range(4))
    inner, outer = refs[4 * groups :]

    def summed(left, right):
        total = 0.0
        for one, two in zip(left, right):
            (a_hi, a_lo), (b_hi, b_lo) = parted(one[...]), parted(two[...])
            a_hi, a_lo, b_hi, b_lo = narrow(a_hi), narrow(a_lo), narrow(b_hi), narrow(b_lo)
            total = total + dot_tn(a_hi, b_hi) + dot_tn(a_lo, b_hi) + dot_tn(a_hi, b_lo)
        return total

    outer[...] = summed(active, grad_result)
    inner[...] = summed(normed, grad_pre)


def expert_weight_grads(kept):
    normed, active, grad_result, grad_pre = zip(*kept)
    rows, width = normed[0].shape
    inner = active[0].shape[1]
    wide = min(512, inner)
    full = pl.BlockSpec((rows, width), lambda i: (0, 0))
    part = pl.BlockSpec((rows, wide), lambda i: (0, i))
    count = len(kept)
    return pl.pallas_call(
        functools.partial(weight_kernel, count),
        grid=(inner // wide,),
        in_specs=[full] * (2 * count) + [part] * (2 * count),
        out_specs=[pl.BlockSpec((width, wide), lambda i: (0, i)), pl.BlockSpec((wide, width), lambda i: (i, 0))],
        out_shape=[
            jax.ShapeDtypeStruct((width, inner), jnp.float32),
            jax.ShapeDtypeStruct((inner, width), jnp.float32),
        ],
        compiler_params=pltpu.CompilerParams(vmem_limit_bytes=48 * 1024 * 1024),
        cost_estimate=pl.CostEstimate(
            flops=12 * count * rows * width * inner, bytes_accessed=16 * count * rows * inner, transcendentals=0
        ),
        name="weights",
    )(*normed, *grad_result, *active, *grad_pre)


def add_up(trees):
    total = trees[0]
    for tree in trees[1:]:
        total = jax.tree.map(jnp.add, total, tree)
    return total


def parted(values):
    head = values.astype(jnp.bfloat16).astype(jnp.float32)
    return head, values - head


def head_lanes(side):
    low = lax.broadcasted_iota(jnp.int32, (1, LANES), 1) < LANES // 2
    turn = lambda v: pltpu.roll(v, LANES // 2, 1)
    at_low = lambda v: v if side == 0 else turn(v)
    at_high = lambda v: turn(v) if side == 0 else v
    both = lambda v, w: jnp.where(low, at_low(v), at_high(w))
    alone = lambda v, rest=0.0: jnp.where(low, at_low(v), rest)
    return both, alone


def dot_nt(left, right):
    return lax.dot_general(left, right, (((1,), (1,)), ((), ())), preferred_element_type=jnp.float32)


def dot_tn(left, right):
    return lax.dot_general(left, right, (((0,), (0,)), ((), ())), preferred_element_type=jnp.float32)


def dot_nn(left, right):
    return lax.dot_general(left, right, (((1,), (0,)), ((), ())), preferred_element_type=jnp.float32)


def narrow(*parts):
    return jnp.concatenate(parts, axis=1).astype(jnp.bfloat16) if len(parts) > 1 else parts[0].astype(jnp.bfloat16)


def attend_kernel(chunk, scale, slopes, dist, q_ref, k_ref, v_ref, out_ref, log_ref, k3, v2, v1, scores):
    pair = pl.program_id(0)
    total = k_ref.shape[0]
    q_hi, q_lo = parted(q_ref[...] * scale)
    k_hi, k_lo = parted(k_ref[...])
    v_hi, v_lo = parted(v_ref[...])
    mixed = []
    for side in (0, 1):
        both, alone = head_lanes(side)
        k3[...] = narrow(both(k_hi, k_hi), alone(k_lo))
        v2[...] = narrow(both(v_hi, v_lo))
        v1[...] = narrow(alone(v_hi))
        q3 = narrow(both(q_hi, q_lo), alone(q_hi))
        slope = slopes[2 * pair + side]
        highest = None
        for at in range(0, total, chunk):
            now = pl.ds(at, chunk)
            score = dot_nt(k3[now], q3) - slope * dist[now]
            scores[now] = score
            top = jnp.max(score, axis=0, keepdims=True)
            highest = top if highest is None else jnp.maximum(highest, top)
        summed, weight = 0.0, 0.0
        for at in range(0, total, chunk):
            now = pl.ds(at, chunk)
            raised = jnp.exp(scores[now] - highest)
            weight = weight + jnp.sum(raised, axis=0, keepdims=True)
            r_hi, r_lo = parted(raised)
            summed = summed + dot_tn(v2[now], narrow(r_hi)) + dot_tn(v1[now], narrow(r_lo))
        mixed.append((summed[: LANES // 2] + summed[LANES // 2 :]) / weight)
        log_ref[0, side : side + 1, :] = highest + jnp.log(weight)
    out_ref[...] = jnp.concatenate(mixed, axis=0).T


def attend_back_kernel(
    chunk, scale, slopes, dist, q_ref, k_ref, v_ref, o_ref, g_ref, log_ref, dq_ref, dkv_ref, ds_ref, k3, v3, k2, k1, hold
):
    pair = pl.program_id(0)
    total = k_ref.shape[0]
    q_hi, q_lo = parted(q_ref[...] * scale)
    k_hi, k_lo = parted(k_ref[...])
    v_hi, v_lo = parted(v_ref[...])
    grad = g_ref[...]
    g_hi, g_lo = parted(grad)
    weighed = grad * o_ref[...]
    lane = lax.broadcasted_iota(jnp.int32, (1, LANES), 1)
    low = lane < LANES // 2
    half = LANES // 2
    grad_query = []
    for side in (0, 1):
        both, alone = head_lanes(side)
        own = low if side == 0 else jnp.logical_not(low)
        centre = -jnp.sum(jnp.where(own, weighed, 0.0), axis=1, keepdims=True)
        c_hi, c_rest = parted(centre)
        c_mid, c_lo = parted(c_rest)
        tail = jnp.where(lane == half, c_hi, jnp.where(lane == half + 1, c_mid, jnp.where(lane == half + 2, c_lo, 0.0)))
        ones = jnp.where(jnp.logical_and(lane >= half, lane < half + 3), 1.0, 0.0)
        k3[...] = narrow(both(k_hi, k_hi), alone(k_lo))
        v3[...] = narrow(both(v_hi, v_hi), alone(v_lo, ones))
        k2[...] = narrow(both(k_hi, k_lo))
        k1[...] = narrow(alone(k_hi))
        q3 = narrow(both(q_hi, q_lo), alone(q_hi))
        q2, q1 = narrow(both(q_hi, q_lo)), narrow(alone(q_hi))
        g3 = narrow(both(g_hi, g_lo), alone(g_hi, tail))
        g2, g1 = narrow(both(g_hi, g_lo)), narrow(alone(g_hi))
        slope = slopes[2 * pair + side]
        logs = log_ref[0, side : side + 1, :]
        slope_grad, query_grad = 0.0, 0.0
        for at in range(0, total, chunk):
            now = pl.ds(at, chunk)
            far = dist[now]
            probs = jnp.exp(dot_nt(k3[now], q3) - slope * far - logs)
            grad_score = probs * dot_nt(v3[now], g3)
            slope_grad = slope_grad + jnp.sum(grad_score * far, axis=0, keepdims=True)
            p_hi, p_lo = parted(probs)
            s_hi, s_lo = parted(grad_score)
            s_hi, s_lo = narrow(s_hi), narrow(s_lo)
            value_grad = dot_nn(narrow(p_hi), g2) + dot_nn(narrow(p_lo), g1)
            key_grad = dot_nn(s_hi, q2) + dot_nn(s_lo, q1)
            query_grad = query_grad + dot_tn(k2[now], s_hi) + dot_tn(k1[now], s_lo)
            value_grad = value_grad + pltpu.roll(value_grad, half, 1)
            key_grad = key_grad + pltpu.roll(key_grad, half, 1)
            if side == 0:
                hold[0, now], hold[1, now] = key_grad, value_grad
            else:
                dkv_ref[0, now] = jnp.where(low, hold[0, now], key_grad)
                dkv_ref[1, now] = jnp.where(low, hold[1, now], value_grad)
        grad_query.append(query_grad[:half] + query_grad[half:])
        ds_ref[0, side : side + 1, :] = slope_grad
    dq_ref[...] = jnp.concatenate(grad_query, axis=0).T * scale


def attend_specs(rows, total, pairs):
    lanes = lambda at: pl.BlockSpec((rows, LANES), lambda i, at=at: (0, at + i))
    wide = lambda at: pl.BlockSpec((total, LANES), lambda i, at=at: (0, at + i))
    return [
        pl.BlockSpec(memory_space=pltpu.SMEM),
        pl.BlockSpec((total, rows), lambda i: (0, 0)),
        lanes(0),
        wide(0),
        wide(pairs),
    ], lanes(0), pl.BlockSpec((1, 8, rows), lambda i: (i, 0, 0))


def attend_params(rows, total, width, passes):
    return dict(
        compiler_params=pltpu.CompilerParams(vmem_limit_bytes=40 * 1024 * 1024),
        cost_estimate=BRIEF,
    )


def attend(packed, both, dist, slopes):
    rows, total = packed.shape[0], both.shape[0]
    width = both.shape[1] // 2
    pairs = width // LANES
    chunk = min(total, 256)
    in_specs, lanes, logs = attend_specs(rows, total, pairs)
    return pl.pallas_call(
        functools.partial(attend_kernel, chunk, (width // slopes.shape[0]) ** -0.5),
        grid=(pairs,),
        in_specs=in_specs,
        out_specs=[lanes, logs],
        out_shape=[
            jax.ShapeDtypeStruct((rows, width), jnp.float32),
            jax.ShapeDtypeStruct((pairs, 8, rows), jnp.float32),
        ],
        scratch_shapes=[
            pltpu.VMEM((total, 2 * LANES), jnp.bfloat16),
            pltpu.VMEM((total, LANES), jnp.bfloat16),
            pltpu.VMEM((total, LANES), jnp.bfloat16),
            pltpu.VMEM((total, rows), jnp.float32),
        ],
        name="attend",
        **attend_params(rows, total, width, 12),
    )(slopes, dist, packed, both, both)


def attend_back(packed, both, dist, slopes, mixed, logs, grad_mixed):
    rows, total = packed.shape[0], both.shape[0]
    width = both.shape[1] // 2
    pairs = width // LANES
    chunk = min(total, 256)
    in_specs, lanes, log_spec = attend_specs(rows, total, pairs)
    dq, dkv, ds = pl.pallas_call(
        functools.partial(attend_back_kernel, chunk, (width // slopes.shape[0]) ** -0.5),
        grid=(pairs,),
        in_specs=in_specs + [lanes, lanes, log_spec],
        out_specs=[lanes, pl.BlockSpec((2, total, LANES), lambda i: (0, 0, i)), log_spec],
        out_shape=[
            jax.ShapeDtypeStruct((rows, width), jnp.float32),
            jax.ShapeDtypeStruct((2, total, width), jnp.float32),
            jax.ShapeDtypeStruct((pairs, 8, rows), jnp.float32),
        ],
        scratch_shapes=[
            pltpu.VMEM((total, 2 * LANES), jnp.bfloat16),
            pltpu.VMEM((total, 2 * LANES), jnp.bfloat16),
            pltpu.VMEM((total, LANES), jnp.bfloat16),
            pltpu.VMEM((total, LANES), jnp.bfloat16),
            pltpu.VMEM((2, total, LANES), jnp.float32),
        ],
        name="attend_back",
        **attend_params(rows, total, width, 30),
    )(slopes, dist, packed, both, both, mixed, grad_mixed, logs)
    return dq, dkv, -jnp.sum(ds[:, :2], axis=2).reshape(-1)


def body(
    frames,
    embedding,
    cotangent,
    expert_ids,
    lengths,
    norm_gain,
    norm_bias,
    router,
    attention_in,
    attention_out,
    slopes,
    conv_point,
    conv_depth,
    batch_gain,
    batch_bias,
    conv_out,
    expert_in,
    expert_out,
):
    packed_weight = attention_in.astype(jnp.float32)
    mixing_weight = attention_out.astype(jnp.float32)
    point_weight = conv_point.astype(jnp.float32)
    project_weight = conv_out.astype(jnp.float32)
    inner_weight = [expert_in[b, 0] for b in (0, 1)]
    outer_weight = [expert_out[b, 0] for b in (0, 1)]
    micro, rows, width = frames.shape
    experts = router.shape[2]
    heads = slopes.shape[0]
    kernel = conv_depth.shape[0]
    half = kernel // 2
    capacity = 2 * rows // experts
    everyone = bits_of("dp") + bits_of("ep")
    layout = Layout(micro, rows, capacity)
    place, part_lengths, counts = layout.places(lengths)
    key_place = layout.key_places()
    parts = len(part_lengths)
    part_rows = micro * rows // parts
    valid_f = jnp.concatenate([(place < length) for length in part_lengths]).astype(jnp.float32)[:, None]
    to_parts = lambda v: v.reshape((parts, part_rows) + v.shape[1:])
    spread = lambda v: jnp.broadcast_to(v[:, None], (parts, part_rows) + v.shape[1:]).reshape(parts * part_rows, -1)

    slots = experts * micro * capacity
    own = (jnp.arange(LANES, dtype=jnp.int32) == layout.z).astype(jnp.float32)[None, :]
    norms = [jnp.stack([norm_gain[i], norm_bias[i]]) for i in range(norm_gain.shape[0])]
    routers = [jnp.pad(router[b], ((0, 0), (0, LANES - experts))) for b in (0, 1)]
    wide = inner_weight[0].shape[1]
    ids = jnp.moveaxis(expert_ids[..., 0], 0, 2)
    rank = [ranks(ids[..., b], experts) for b in (0, 1)]
    home = [tables_of(layout.home_slots(ids[..., b], rank[b]), slots) for b in (0, 1)]
    groups = range(experts // 2)
    home_rows = embedding.reshape(-1, width)
    home_logits = [product(router[b].T, home_rows.T) for b in (0, 1)]
    home_place = layout.z * rows + jnp.arange(rows, dtype=jnp.int32)
    home_valid = (home_place[None, :] < lengths[:, layout.d][:, None]).astype(jnp.float32).reshape(1, -1)
    spare = jnp.zeros((-(experts + 1) % 8, micro * rows), jnp.float32)
    extras = [
        pick_columns(jnp.concatenate([home_logits[b], home_valid, spare], axis=0), home[b][1]) for b in (0, 1)
    ]

    work_ids = layout.ids_to_work(ids)
    sources = layout.home_to_expert(pick(home[0][0], frames.reshape(-1, width)), extras[0], (work_ids,))
    kept_first = []
    back = []
    last = ()
    for group in groups:
        hidden, extra = sources[group]
        hidden, extra = after(hidden, *last), lanes_of(extra)
        fixed = (own, norms[0], routers[0], inner_weight[0], outer_weight[0])
        new, result, pre = expert_call(
            forward_kernel, "forward", experts, (hidden, extra), fixed, (width, width, wide), False, False, 2
        )
        last = (new,)
        kept_first.append(((hidden, extra), (result, pre), fixed))
        back += layout.hops(new, group)
    work = [
        tables_of(layout.work_slots(work_ids[..., b], ranks(work_ids[..., b], experts)), slots) for b in (0, 1)
    ]
    first = pick(work[0][1], jnp.concatenate(back, axis=0))

    def attention_front(values, gain_now, shift_now, weight_now):
        return product(norm_rows(values, gain_now, shift_now), weight_now)

    packed, attention_pull = jax.vjp(attention_front, first, norm_gain[1], norm_bias[1], packed_weight)
    packed, cot_rows = lax.optimization_barrier((packed, cotangent.reshape(-1, width)))
    pulls = layout.home_to_expert(pick(home[1][0], cot_rows), extras[1])
    packed_parts = to_parts(packed)
    apart = jnp.abs(key_place[:, None] - place[None, :]).astype(jnp.float32)
    kept_attention = []
    mixed_parts = []
    for part in range(parts):
        both = layout.gather(packed_parts[part, :, width:])
        dist = jnp.where((key_place < part_lengths[part])[:, None], apart, FAR)
        mixed, logs = attend(packed_parts[part], both, dist, slopes)
        kept_attention.append((both, dist, mixed, logs))
        mixed_parts.append(mixed)
    mixed_all = jnp.concatenate(mixed_parts, axis=0)
    second = first + product(mixed_all, mixing_weight)

    def conv_front(values, gain_now, shift_now, point_now):
        both = product(norm_rows(values, gain_now, shift_now), point_now)
        return both[:, :width] * jax.nn.sigmoid(both[:, width:]) * valid_f

    gated, conv_pull = jax.vjp(conv_front, second, norm_gain[2], norm_bias[2], point_weight)
    padded = [layout.halo(v, half) for v in to_parts(gated)]
    conv_parts = []
    for part in range(parts):
        total = conv_depth[0] * padded[part][0:part_rows]
        for offset in range(1, kernel):
            total = total + conv_depth[offset] * padded[part][offset : offset + part_rows]
        conv_parts.append(total)
    conv = jnp.concatenate(conv_parts, axis=0)
    stats = layout.batch_total(
        jnp.stack([jnp.sum(to_parts(conv * valid_f), axis=1), jnp.sum(to_parts(conv * conv * valid_f), axis=1)], axis=1)
    )
    centre = stats[:, 0] / counts[:, None]
    inverse_dev = lax.rsqrt(stats[:, 1] / counts[:, None] - centre * centre + EPS)
    scaled = (conv - spread(centre)) * spread(inverse_dev)
    shaped = scaled * batch_gain + batch_bias
    swished = jax.nn.silu(shaped)
    third = second + product(swished, project_weight)

    sent = pick(work[1][0], third)
    results, back, kept, small = [], [], [], []
    arrived, last = (), ()
    for group in groups:
        hidden = layout.hops(after(layout.group_of(sent, group), *arrived), group)
        arrived = tuple(hidden)
        pull_now, extra = pulls[group]
        result, grad, grad_logits, normed, active, grad_result, grad_pre, sums = expert_call(
            both_kernel,
            "both",
            experts,
            (jnp.concatenate(after(hidden, *last), axis=0), lanes_of(extra), pull_now),
            (own, norms[3], norms[4], routers[1], inner_weight[1], outer_weight[1]),
            (width, width, LANES, width, wide, width, wide),
            True,
            True,
            4,
        )
        last = (grad,)
        results.append((result, grad_logits[:, : experts + (-experts % 8)].T))
        kept.append((normed, active, grad_result, grad_pre))
        small.append((sums, product(normed.T, grad_logits[:, :experts])))
        back += layout.hops(grad, group)
    sums, router_one = add_up(small)
    gain_three, shift_three, gain_four, shift_four = (sums[k] for k in range(4))
    kept, _ = lax.optimization_barrier((kept, back[:-2]))
    expert_one = lax.psum(expert_weight_grads(kept), "dp")
    grad_third = pick(work[1][1], jnp.concatenate(back, axis=0))
    project_grad = product(swished.T, grad_third)
    grad_shaped = product(grad_third, project_weight.T) * swish_slope(shaped)
    sums = jnp.stack(
        [jnp.sum(to_parts(grad_shaped), axis=1), jnp.sum(to_parts(grad_shaped * scaled), axis=1)], axis=1
    )
    totals = layout.batch_total(sums)
    shift_total, gain_total = totals[:, 0], totals[:, 1]
    results, _ = lax.optimization_barrier((results, totals))
    output_slots, logit_slots = layout.opened(layout.expert_to_home(results))
    output = pick(home[1][1], output_slots).reshape(micro, rows, width)
    logit_one = pick_columns(logit_slots[:experts], home[1][0])
    router_one = router_one + product(logit_one, home_rows).T
    grad_conv = (
        batch_gain
        * spread(inverse_dev)
        * (grad_shaped - valid_f * (spread(shift_total) + scaled * spread(gain_total)) / spread(counts[:, None]))
    )
    depth_grad = 0.0
    gated_parts = []
    for part, now in enumerate(to_parts(grad_conv)):
        grad_pad = layout.halo(now, half)
        total = conv_depth[0] * grad_pad[2 * half : 2 * half + part_rows]
        for offset in range(1, kernel):
            total = total + conv_depth[offset] * grad_pad[2 * half - offset : 2 * half - offset + part_rows]
        gated_parts.append(total)
        depth_grad = depth_grad + jnp.stack(
            [jnp.sum(now * padded[part][offset : offset + part_rows], axis=0) for offset in range(kernel)]
        )
    grad_hidden, gain_two, shift_two, point_grad = conv_pull(jnp.concatenate(gated_parts, axis=0))
    grad_second = grad_third + grad_hidden

    mixing_grad = product(mixed_all.T, grad_second)
    grad_mixed = to_parts(product(grad_second, mixing_weight.T))
    packed_back = []
    slope_grad = 0.0
    for part in range(parts):
        both, dist, mixed, logs = kept_attention[part]
        grad_query, grad_both, slope_now = attend_back(
            packed_parts[part], both, dist, slopes, mixed, logs, grad_mixed[part]
        )
        slope_grad = slope_grad + slope_now
        grad_both = layout.scatter(grad_both)
        packed_back.append(jnp.concatenate([grad_query, grad_both[0], grad_both[1]], axis=1))
    grad_hidden, gain_one, shift_one, packed_grad = attention_pull(jnp.concatenate(packed_back, axis=0))
    grad_first = grad_second + grad_hidden
    early = jnp.concatenate(
        [
            jnp.stack([gain_one, gain_two, gain_three, gain_four, shift_one, shift_two, shift_three, shift_four]),
            router_one.T,
            jnp.pad(slope_grad, (0, width - heads))[None],
            depth_grad,
            jnp.sum(sums, axis=0),
        ],
        axis=0,
    )
    dense = DenseSum(
        [jnp.concatenate([packed_grad, project_grad], axis=1), jnp.concatenate([mixing_grad, point_grad], axis=1)]
    )
    over_dp, over_ep = len(bits_of("dp")), len(bits_of("ep"))

    sent = pick(work[0][0], grad_first)
    sources, kept, small = [], [], []
    arrived, last = (), ()
    for group in groups:
        grad = layout.hops(after(layout.group_of(sent, group), *arrived), group)
        arrived = tuple(grad)
        grad = after(grad, *last)
        if group == 0:
            grad, expert_one = lax.optimization_barrier((grad, expert_one))
        (hidden, extra), saved, fixed = kept_first[group]
        new, grad_logits, normed, active, grad_result, grad_pre, sums = expert_call(
            backward_kernel,
            "backward",
            experts,
            (hidden, extra, jnp.concatenate(grad, axis=0)) + saved,
            fixed,
            (width, LANES, width, wide, width, wide),
            True,
            False,
            2,
        )
        if group == 0:
            new = dense.step(new)
        if group == 1:
            new = dense.step(new, over_dp - 2)
        last = (new,)
        sources.append((new, grad_logits[:, : experts + (-experts % 8)].T))
        kept.append((normed, active, grad_result, grad_pre))
        small.append((sums, product(normed.T, grad_logits[:, :experts])))
    sums, router_zero = add_up(small)
    gain_zero, shift_zero = sums[0], sums[1]
    expert_zero = lax.psum(expert_weight_grads(kept), "dp")
    sources = dense.step(sources, 2 * over_ep + 1)
    frame_messages = layout.expert_to_home(sources)
    wholes = [lax.pad(one[None], 0.0, ((1, 0, 0), (0, 0, 0), (0, 0, 0))) for one in expert_one]
    frame_messages, wholes = dense.step((frame_messages, wholes), over_dp - 1)
    rows_back, logit_slots = layout.opened(frame_messages)
    logit_zero = pick_columns(logit_slots[:experts], home[0][0])
    router_zero = router_zero + product(logit_zero, home_rows).T
    frames_grad = pick(home[0][1], rows_back).reshape(micro, rows, width)
    late = jnp.concatenate([gain_zero[None], shift_zero[None], router_zero.T, early], axis=0)
    late = butterfly(dense.step(late), bits_of("ep") + bits_of("dp"))
    late, early = late[: 2 + experts], late[2 + experts :]
    packed_grad, project_grad = dense.parts[0][:, : 3 * width], dense.parts[0][:, 3 * width :]
    mixing_grad, point_grad = dense.parts[1][:, :width], dense.parts[1][:, width:]
    expert_grads = []
    for zero, whole in zip(expert_zero, wholes):
        expert_grads.append(lax.dynamic_update_slice(whole, zero[None], (0, 0, 0))[:, None])

    at = 8 + experts
    gain_grad = jnp.concatenate([late[:1], early[:4]], axis=0)
    shift_grad = jnp.concatenate([late[1:2], early[4:8]], axis=0)
    router_grad = jnp.stack([late[2 : 2 + experts].T, early[8:at].T])
    return (
        output,
        frames_grad,
        gain_grad,
        shift_grad,
        router_grad,
        packed_grad,
        mixing_grad,
        early[at, :heads],
        point_grad,
        early[at + 1 : at + 1 + kernel],
        early[at + 2 + kernel],
        early[at + 1 + kernel],
        project_grad,
        expert_grads[0],
        expert_grads[1],
    )


def solution(mesh):
    rows = P(None, ("dp", "ep"), None)
    whole = P()
    split = P(None, "ep", None, None)
    return jax.shard_map(
        body,
        mesh=mesh,
        in_specs=(rows, rows, rows, P(None, None, ("dp", "ep"), None)) + (whole,) * 12 + (split, split),
        out_specs=(rows, rows) + (whole,) * 11 + (split, split),
        check_vma=False,
    )
```

```python
import functools

import jax
import jax.numpy as jnp
from jax import lax
from jax.experimental import pallas as pl
from jax.experimental.pallas import tpu as pltpu
from jax.sharding import PartitionSpec as P

HIGH = lax.Precision.HIGH
EPS = 1e-05
FAR = 1e30
LANES = 128
BRIEF = pl.CostEstimate(flops=1, bytes_accessed=1, transcendentals=0)


def product(left, right):
    return jnp.matmul(left, right, precision=HIGH)


def after(values, *earlier):
    return lax.optimization_barrier((values,) + earlier)[0]


def swap(values, axis, bit):
    count = lax.axis_size(axis)
    return lax.ppermute(values, axis, [(i, i ^ bit) for i in range(count)])


def bits_of(axis):
    count = lax.axis_size(axis)
    return [(axis, 1 << k) for k in range(count.bit_length() - 1)]


def butterfly(values, steps):
    for axis, bit in steps:
        values = values + swap(values, axis, bit)
    return values


def upper(step):
    axis, bit = step
    return (lax.axis_index(axis) // bit) % 2


def halve(values, step):
    side = upper(step)
    half = values.shape[0] // 2
    keep = lax.dynamic_slice_in_dim(values, side * half, half, 0)
    send = lax.dynamic_slice_in_dim(values, (1 - side) * half, half, 0)
    return keep + swap(send, *step)


def join(values, step):
    side = upper(step)
    other = swap(values, *step)
    half = values.shape[0]
    out = jnp.zeros((2 * half,) + values.shape[1:], values.dtype)
    out = lax.dynamic_update_slice_in_dim(out, values, side * half, 0)
    return lax.dynamic_update_slice_in_dim(out, other, (1 - side) * half, 0)


class DenseSum:
    def __init__(self, pair):
        first, *rest = bits_of("dp")
        far = bits_of("ep")[::-1]
        self.orders = [[first] + rest + far, [first] + rest[::-1] + far]
        self.parts = list(pair)
        count = len(self.orders[0])
        self.ways = [(halve, k) for k in range(count)] + [(join, k) for k in range(count - 1, -1, -1)]

    def step(self, value, count=1):
        for _ in range(count):
            way, k = self.ways.pop(0)
            self.parts = [way(part, order[k]) for part, order in zip(self.parts, self.orders)]
        value, self.parts = lax.optimization_barrier((value, self.parts))
        return value


class Layout:
    def __init__(self, micro, rows, capacity):
        self.micro, self.rows, self.capacity = micro, rows, capacity
        self.ep, self.dp = lax.axis_size("ep"), lax.axis_size("dp")
        self.z, self.d = lax.axis_index("ep"), lax.axis_index("dp")
        self.paired = micro == 2 and self.ep == 4 and self.dp % 2 == 0
        self.core = self.d % 2

    def route(self, low, u, home):
        pairs = []
        for d in range(self.dp):
            for z in range(self.ep):
                there = (d - d % 2 + z // 2) * self.ep + 2 * ((z % 2) ^ u) + (low ^ (d % 2))
                pairs.append((d * self.ep + z, there))
        return [(j, i) for i, j in pairs] if home else pairs

    def piece(self, values, at, count, axis=0):
        return lax.slice_in_dim(values, at * self.capacity, (at + count) * self.capacity, axis=axis)

    def home_slots(self, ids, rank):
        block = jnp.arange(self.micro, dtype=jnp.int32)[:, None]
        if not self.paired:
            return self.work_slots(ids, rank)
        step = ids ^ (2 * block + self.core)
        u = (self.z % 2) ^ (ids // 2)
        return (((step % 2) * 2 + u) * 2 + step // 2) * self.capacity + rank

    def work_slots(self, ids, rank):
        block = jnp.arange(self.micro, dtype=jnp.int32)[:, None]
        step = ids ^ self.z
        groups = self.ep // 2
        inner = block ^ (ids // 2) if self.paired else block
        return ((step % groups * 2 + step // groups) * self.micro + inner) * self.capacity + rank

    def hop(self, values, step):
        return values if step == 0 else swap(values, "ep", step)

    def hops(self, values, group):
        half = values.shape[0] // 2
        return [self.hop(values[h * half : (h + 1) * half], group + h * (self.ep // 2)) for h in (0, 1)]

    def group_of(self, values, group):
        return self.piece(values, group * 2 * self.micro, 2 * self.micro)

    def home_to_expert(self, rows, extra, ahead=()):
        wide = rows.shape[1]
        few = extra.shape[0]
        count = self.micro * self.capacity
        out = []
        last = ()
        for group in range(self.ep // 2):
            got = []
            for u in (0, 1):
                at = (group * 2 + u) * self.micro
                more = self.piece(extra, at, self.micro, 1)
                message = jnp.concatenate(
                    [self.piece(rows, at, self.micro), jnp.pad(more, ((0, 0), (0, wide - count)))], axis=0
                )
                message = after(message, *last)
                if self.paired:
                    got.append(lax.ppermute(message, ("dp", "ep"), self.route(group, u, False)))
                else:
                    got.append(self.hop(message, group + u * (self.ep // 2)))
            last = tuple(got) + tuple(ahead)
            rows_got = [v[:count] for v in got]
            more_got = [v[count:, :count] for v in got]
            if self.paired:
                order = [(u, h) for h in (0, 1) for u in (0, 1)]
                rows_got = [self.piece(rows_got[u], h, 1) for u, h in order]
                more_got = [self.piece(more_got[u], h, 1, 1) for u, h in order]
            out.append((jnp.concatenate(rows_got, axis=0), jnp.concatenate(more_got, axis=1)))
        return out

    def expert_to_home(self, groups):
        messages = []
        for group, (rows, more) in enumerate(groups):
            wide = rows.shape[1]
            for u in (0, 1):
                if self.paired:
                    row = jnp.concatenate([self.piece(rows, 2 * h + u, 1) for h in (0, 1)], axis=0)
                    few = jnp.concatenate([self.piece(more, 2 * h + u, 1, 1) for h in (0, 1)], axis=1)
                else:
                    row, few = self.piece(rows, u * self.micro, self.micro), self.piece(more, u * self.micro, self.micro, 1)
                message = row
                if more.shape[0]:
                    message = row
                if more.shape[0]:
                    message = jnp.concatenate([row, jnp.pad(few, ((0, 0), (0, wide - few.shape[1])))], axis=0)
                if self.paired:
                    messages.append(lax.ppermute(message, ("dp", "ep"), self.route(group, u, True)))
                else:
                    messages.append(self.hop(message, group + u * (self.ep // 2)))
        return messages

    def opened(self, messages):
        count = self.micro * self.capacity
        return (
            jnp.concatenate([v[:count] for v in messages], axis=0),
            jnp.concatenate([v[count:, :count] for v in messages], axis=1),
        )

    def ids_to_work(self, ids):
        if not self.paired:
            return ids
        values = jnp.swapaxes(ids, 1, 2).astype(jnp.float32)
        out = []
        for turn in (0, 1):
            pairs = []
            for d in range(self.dp):
                for z in range(self.ep):
                    m = (z % 2) ^ turn
                    pairs.append((d * self.ep + z, (d - d % 2 + z // 2) * self.ep + 2 * m + d % 2))
            block = lax.dynamic_index_in_dim(values, (self.z % 2) ^ turn, 0, keepdims=False)
            out.append(lax.ppermute(block, ("dp", "ep"), pairs))
        m = self.z // 2
        both = jnp.stack([jnp.where(m == 0, out[0], out[1]), jnp.where(m == 0, out[1], out[0])])
        return jnp.swapaxes(both, 1, 2).astype(jnp.int32)

    def places(self, lengths):
        counts = jnp.sum(lengths, axis=1).astype(jnp.float32)
        if self.paired:
            m = self.z // 2
            place = self.core * 2 * self.rows + jnp.arange(2 * self.rows, dtype=jnp.int32)
            group = self.d - self.core + self.z % 2
            return place, [lengths[m, group]], counts[m][None]
        place = self.z * self.rows + jnp.arange(self.rows, dtype=jnp.int32)
        return place, [lengths[m, self.d] for m in range(self.micro)], counts

    def gather(self, values):
        if self.paired:
            return jnp.concatenate([values, swap(values, "dp", 1)], axis=0)
        return lax.all_gather(values, "ep", axis=0, tiled=True)

    def key_places(self):
        if self.paired:
            base = jnp.arange(2 * self.rows, dtype=jnp.int32)
            return jnp.concatenate([base + self.core * 2 * self.rows, base + (1 - self.core) * 2 * self.rows])
        return jnp.arange(self.ep * self.rows, dtype=jnp.int32)

    def scatter(self, values):
        if self.paired:
            half = values.shape[1] // 2
            return values[:, :half] + swap(values[:, half:], "dp", 1)
        return lax.psum_scatter(values, "ep", scatter_dimension=1, tiled=True)

    def halo(self, values, width):
        length = values.shape[0]
        if self.paired:
            low = self.core == 0
            edge = jnp.where(low, values[length - width :], values[:width])
            other = swap(edge, "dp", 1)
            zero = jnp.zeros_like(other)
            before, after = jnp.where(low, zero, other), jnp.where(low, other, zero)
        else:
            up = [(i, i + 1) for i in range(self.ep - 1)]
            down = [(j, i) for i, j in up]
            before = lax.ppermute(values[length - width :], "ep", up)
            after = lax.ppermute(values[:width], "ep", down)
        return jnp.concatenate([before, values, after], axis=0)

    def batch_total(self, values):
        if self.paired:
            return butterfly(values, bits_of("dp") + [("ep", 1)])
        return butterfly(values, bits_of("dp") + bits_of("ep"))


def norm_rows(values, gain, shift):
    center = values - jnp.mean(values, axis=-1, keepdims=True)
    spread = jnp.mean(center * center, axis=-1, keepdims=True)
    return center * lax.rsqrt(spread + EPS) * gain + shift


def swish_slope(values):
    squash = jax.nn.sigmoid(values)
    return squash * (1.0 + values * (1.0 - squash))


def ranks(ids, experts):
    rows = ids.shape[1]
    onehot = (ids[..., None] == jnp.arange(experts, dtype=jnp.int32)).astype(jnp.float32)
    below = (jnp.arange(rows)[:, None] > jnp.arange(rows)[None, :]).astype(jnp.float32)
    before = jnp.einsum("rs,bse->bre", below, onehot)
    return jnp.sum(before * onehot, axis=2).astype(jnp.int32)


def tables_of(slot, count):
    spots = jnp.arange(count, dtype=jnp.int32)
    flat = slot.reshape(-1)
    return (
        (spots[:, None] == flat[None, :]).astype(jnp.bfloat16),
        (flat[:, None] == spots[None, :]).astype(jnp.bfloat16),
    )


def pick(table, values):
    return jnp.matmul(table.astype(jnp.float32), values, precision=HIGH)


def pick_columns(values, table):
    return jnp.matmul(values, table.astype(jnp.float32), precision=HIGH)


def product_two(left, right, dot):
    head, rest = parted(left)
    return dot(narrow(head), right) + dot(narrow(rest), right)


def exact_dot(left, right, contract):
    return lax.dot_general(
        left, right, (contract, ((), ())), precision=lax.Precision.HIGHEST, preferred_element_type=jnp.float32
    )


def norm_parts(values):
    center = values - jnp.mean(values, axis=1, keepdims=True)
    scale = lax.rsqrt(jnp.mean(center * center, axis=1, keepdims=True) + EPS)
    return center * scale, scale


def norm_back(grad, gain, normal, scale):
    weighed = grad * gain
    centred = weighed - jnp.mean(weighed, axis=1, keepdims=True)
    return scale * (centred - normal * jnp.mean(weighed * normal, axis=1, keepdims=True))


def gate_parts(hidden, extra, own, norm, router, experts):
    normal, scale = norm_parts(hidden)
    normed = normal * norm[0:1] + norm[1:2]
    lane = lax.broadcasted_iota(jnp.int32, (1, LANES), 1)
    logits = exact_dot(normed, router, ((1,), (0,))) + extra
    logits = jnp.where(lane < experts, logits, -FAR)
    raised = jnp.exp(logits - jnp.max(logits, axis=1, keepdims=True))
    probs = raised / jnp.sum(raised, axis=1, keepdims=True)
    return normal, scale, normed, probs, jnp.sum(probs * own, axis=1, keepdims=True)


def hidden_columns(weight_in):
    wide = min(512, weight_in.shape[1])
    return [pl.ds(at, wide) for at in range(0, weight_in.shape[1], wide)]


def forward_part(hidden, extra, own, norm, router, weight_in, weight_out, pre, experts):
    parts = gate_parts(hidden, extra, own, norm, router, experts)
    result = 0.0
    for now in hidden_columns(weight_in):
        before = product_two(parts[2], weight_in[:, now], dot_nn)
        pre[:, now] = before
        result = result + product_two(before * jax.nn.sigmoid(before), weight_out[now, :], dot_nn)
    return parts, result, hidden + 0.5 * parts[4] * result


def backward_part(grad, result, parts, own, norm, router, weight_in, weight_out, pre, active, grad_pre):
    normal, scale, normed, probs, gate = parts
    grad_result = 0.5 * gate * grad
    grad_gate = 0.5 * jnp.sum(grad * result, axis=1, keepdims=True)
    grad_logits = grad_gate * probs * (own - gate)
    grad_normed = exact_dot(grad_logits, router, ((1,), (1,)))
    for now in hidden_columns(weight_in):
        before = pre[:, now]
        squash = jax.nn.sigmoid(before)
        active[:, now] = before * squash
        slope = squash * (1.0 + before * (1.0 - squash))
        now_grad = product_two(grad_result, weight_out[now, :], dot_nt) * slope
        grad_pre[:, now] = now_grad
        grad_normed = grad_normed + product_two(now_grad, weight_in[:, now], dot_nt)
    sums = [jnp.sum(grad_normed * normal, axis=0, keepdims=True), jnp.sum(grad_normed, axis=0, keepdims=True)]
    return grad + norm_back(grad_normed, norm[0:1], normal, scale), grad_result, grad_logits, sums


def add_rows(out, rows):
    @pl.when(pl.program_id(0) == 0)
    def _():
        out[...] = jnp.zeros_like(out)

    for at, row in enumerate(rows):
        out[at : at + 1, :] += row


def forward_kernel(experts, hidden, extra, own, norm, router, weight_in, weight_out, new, result, pre):
    _, result[...], new[...] = forward_part(
        hidden[...], extra[...], own[...], norm[...], router[...], weight_in, weight_out, pre, experts
    )


def backward_kernel(
    experts, hidden, extra, grad, result, pre, own, norm, router, weight_in, weight_out,
    back, logits, normed, active, grad_result, grad_pre, sums,
):
    parts = gate_parts(hidden[...], extra[...], own[...], norm[...], router[...], experts)
    back[...], grad_result[...], logits[...], rows = backward_part(
        grad[...], result[...], parts, own[...], norm[...], router[...], weight_in, weight_out, pre, active, grad_pre
    )
    normed[...] = parts[2]
    add_rows(sums, rows)


def both_kernel(
    experts, hidden, extra, pull, own, norm, last, router, weight_in, weight_out,
    output, back, logits, normed, active, grad_result, grad_pre, sums, pre,
):
    parts, result, new = forward_part(
        hidden[...], extra[...], own[...], norm[...], router[...], weight_in, weight_out, pre, experts
    )
    lane = lax.broadcasted_iota(jnp.int32, (1, LANES), 1)
    valid = jnp.sum(jnp.where(lane == experts, extra[...], 0.0), axis=1, keepdims=True)
    normal, scale = norm_parts(new)
    output[...] = (normal * last[0:1] + last[1:2]) * valid
    grad = pull[...] * valid
    last_sums = [jnp.sum(grad * normal, axis=0, keepdims=True), jnp.sum(grad, axis=0, keepdims=True)]
    back[...], grad_result[...], logits[...], rows = backward_part(
        norm_back(grad, last[0:1], normal, scale), result, parts, own[...], norm[...], router[...],
        weight_in, weight_out, pre, active, grad_pre,
    )
    normed[...] = parts[2]
    add_rows(sums, rows + last_sums)


def expert_call(kernel, name, experts, by_rows, fixed, widths, sums, hold, products):
    rows, width = by_rows[0].shape
    block = min(256, rows)
    row_spec = lambda wide: pl.BlockSpec((block, wide), lambda i: (i, 0))
    full = lambda v: pl.BlockSpec(v.shape, lambda i: (0, 0))
    out_specs = [row_spec(wide) for wide in widths]
    out_shape = [jax.ShapeDtypeStruct((rows, wide), jnp.float32) for wide in widths]
    if sums:
        out_specs.append(pl.BlockSpec((8, width), lambda i: (0, 0)))
        out_shape.append(jax.ShapeDtypeStruct((8, width), jnp.float32))
    inner = fixed[-2].shape[1]
    return pl.pallas_call(
        functools.partial(kernel, experts),
        grid=(rows // block,),
        in_specs=[row_spec(v.shape[1]) for v in by_rows] + [full(v) for v in fixed],
        out_specs=out_specs,
        out_shape=out_shape,
        scratch_shapes=[pltpu.VMEM((block, inner), jnp.float32)] if hold else [],
        compiler_params=pltpu.CompilerParams(vmem_limit_bytes=48 * 1024 * 1024),
        cost_estimate=BRIEF,
        name=name,
    )(*by_rows, *fixed)


def lanes_of(extra):
    return jnp.pad(extra.T, ((0, 0), (0, LANES - extra.shape[0])))


def weight_kernel(groups, *refs):
    normed, grad_result, active, grad_pre = (refs[k * groups : (k + 1) * groups] for k in range(4))
    inner, outer = refs[4 * groups :]

    def summed(left, right):
        total = 0.0
        for one, two in zip(left, right):
            (a_hi, a_lo), (b_hi, b_lo) = parted(one[...]), parted(two[...])
            a_hi, a_lo, b_hi, b_lo = narrow(a_hi), narrow(a_lo), narrow(b_hi), narrow(b_lo)
            total = total + dot_tn(a_hi, b_hi) + dot_tn(a_lo, b_hi) + dot_tn(a_hi, b_lo)
        return total

    outer[...] = summed(active, grad_result)
    inner[...] = summed(normed, grad_pre)


def expert_weight_grads(kept, brief):
    normed, active, grad_result, grad_pre = zip(*kept)
    rows, width = normed[0].shape
    inner = active[0].shape[1]
    wide = min(512, inner)
    full = pl.BlockSpec((rows, width), lambda i: (0, 0))
    part = pl.BlockSpec((rows, wide), lambda i: (0, i))
    count = len(kept)
    return pl.pallas_call(
        functools.partial(weight_kernel, count),
        grid=(inner // wide,),
        in_specs=[full] * (2 * count) + [part] * (2 * count),
        out_specs=[pl.BlockSpec((width, wide), lambda i: (0, i)), pl.BlockSpec((wide, width), lambda i: (i, 0))],
        out_shape=[
            jax.ShapeDtypeStruct((width, inner), jnp.float32),
            jax.ShapeDtypeStruct((inner, width), jnp.float32),
        ],
        compiler_params=pltpu.CompilerParams(vmem_limit_bytes=48 * 1024 * 1024),
        cost_estimate=BRIEF if brief else pl.CostEstimate(
            flops=12 * count * rows * width * inner, bytes_accessed=16 * count * rows * inner, transcendentals=0
        ),
        name="weights",
    )(*normed, *grad_result, *active, *grad_pre)


def add_up(trees):
    total = trees[0]
    for tree in trees[1:]:
        total = jax.tree.map(jnp.add, total, tree)
    return total


def parted(values):
    head = values.astype(jnp.bfloat16).astype(jnp.float32)
    return head, values - head


def head_lanes(side):
    low = lax.broadcasted_iota(jnp.int32, (1, LANES), 1) < LANES // 2
    turn = lambda v: pltpu.roll(v, LANES // 2, 1)
    at_low = lambda v: v if side == 0 else turn(v)
    at_high = lambda v: turn(v) if side == 0 else v
    both = lambda v, w: jnp.where(low, at_low(v), at_high(w))
    alone = lambda v, rest=0.0: jnp.where(low, at_low(v), rest)
    return both, alone


def dot_nt(left, right):
    return lax.dot_general(left, right, (((1,), (1,)), ((), ())), preferred_element_type=jnp.float32)


def dot_tn(left, right):
    return lax.dot_general(left, right, (((0,), (0,)), ((), ())), preferred_element_type=jnp.float32)


def dot_nn(left, right):
    return lax.dot_general(left, right, (((1,), (0,)), ((), ())), preferred_element_type=jnp.float32)


def narrow(*parts):
    return jnp.concatenate(parts, axis=1).astype(jnp.bfloat16) if len(parts) > 1 else parts[0].astype(jnp.bfloat16)


def attend_kernel(chunk, scale, slopes, dist, q_ref, k_ref, v_ref, out_ref, log_ref, k3, v2, v1, scores):
    pair = pl.program_id(0)
    total = k_ref.shape[0]
    q_hi, q_lo = parted(q_ref[...] * scale)
    k_hi, k_lo = parted(k_ref[...])
    v_hi, v_lo = parted(v_ref[...])
    mixed = []
    for side in (0, 1):
        both, alone = head_lanes(side)
        k3[...] = narrow(both(k_hi, k_hi), alone(k_lo))
        v2[...] = narrow(both(v_hi, v_lo))
        v1[...] = narrow(alone(v_hi))
        q3 = narrow(both(q_hi, q_lo), alone(q_hi))
        slope = slopes[2 * pair + side]
        highest = None
        for at in range(0, total, chunk):
            now = pl.ds(at, chunk)
            score = dot_nt(k3[now], q3) - slope * dist[now]
            scores[now] = score
            top = jnp.max(score, axis=0, keepdims=True)
            highest = top if highest is None else jnp.maximum(highest, top)
        summed, weight = 0.0, 0.0
        for at in range(0, total, chunk):
            now = pl.ds(at, chunk)
            raised = jnp.exp(scores[now] - highest)
            weight = weight + jnp.sum(raised, axis=0, keepdims=True)
            r_hi, r_lo = parted(raised)
            summed = summed + dot_tn(v2[now], narrow(r_hi)) + dot_tn(v1[now], narrow(r_lo))
        mixed.append((summed[: LANES // 2] + summed[LANES // 2 :]) / weight)
        log_ref[0, side : side + 1, :] = highest + jnp.log(weight)
    out_ref[...] = jnp.concatenate(mixed, axis=0).T


def attend_back_kernel(
    chunk, scale, slopes, dist, q_ref, k_ref, v_ref, o_ref, g_ref, log_ref, dq_ref, dkv_ref, ds_ref, k3, v3, k2, k1, hold
):
    pair = pl.program_id(0)
    total = k_ref.shape[0]
    q_hi, q_lo = parted(q_ref[...] * scale)
    k_hi, k_lo = parted(k_ref[...])
    v_hi, v_lo = parted(v_ref[...])
    grad = g_ref[...]
    g_hi, g_lo = parted(grad)
    weighed = grad * o_ref[...]
    lane = lax.broadcasted_iota(jnp.int32, (1, LANES), 1)
    low = lane < LANES // 2
    half = LANES // 2
    grad_query = []
    for side in (0, 1):
        both, alone = head_lanes(side)
        own = low if side == 0 else jnp.logical_not(low)
        centre = -jnp.sum(jnp.where(own, weighed, 0.0), axis=1, keepdims=True)
        c_hi, c_rest = parted(centre)
        c_mid, c_lo = parted(c_rest)
        tail = jnp.where(lane == half, c_hi, jnp.where(lane == half + 1, c_mid, jnp.where(lane == half + 2, c_lo, 0.0)))
        ones = jnp.where(jnp.logical_and(lane >= half, lane < half + 3), 1.0, 0.0)
        k3[...] = narrow(both(k_hi, k_hi), alone(k_lo))
        v3[...] = narrow(both(v_hi, v_hi), alone(v_lo, ones))
        k2[...] = narrow(both(k_hi, k_lo))
        k1[...] = narrow(alone(k_hi))
        q3 = narrow(both(q_hi, q_lo), alone(q_hi))
        q2, q1 = narrow(both(q_hi, q_lo)), narrow(alone(q_hi))
        g3 = narrow(both(g_hi, g_lo), alone(g_hi, tail))
        g2, g1 = narrow(both(g_hi, g_lo)), narrow(alone(g_hi))
        slope = slopes[2 * pair + side]
        logs = log_ref[0, side : side + 1, :]
        slope_grad, query_grad = 0.0, 0.0
        for at in range(0, total, chunk):
            now = pl.ds(at, chunk)
            far = dist[now]
            probs = jnp.exp(dot_nt(k3[now], q3) - slope * far - logs)
            grad_score = probs * dot_nt(v3[now], g3)
            slope_grad = slope_grad + jnp.sum(grad_score * far, axis=0, keepdims=True)
            p_hi, p_lo = parted(probs)
            s_hi, s_lo = parted(grad_score)
            s_hi, s_lo = narrow(s_hi), narrow(s_lo)
            value_grad = dot_nn(narrow(p_hi), g2) + dot_nn(narrow(p_lo), g1)
            key_grad = dot_nn(s_hi, q2) + dot_nn(s_lo, q1)
            query_grad = query_grad + dot_tn(k2[now], s_hi) + dot_tn(k1[now], s_lo)
            value_grad = value_grad + pltpu.roll(value_grad, half, 1)
            key_grad = key_grad + pltpu.roll(key_grad, half, 1)
            if side == 0:
                hold[0, now], hold[1, now] = key_grad, value_grad
            else:
                dkv_ref[0, now] = jnp.where(low, hold[0, now], key_grad)
                dkv_ref[1, now] = jnp.where(low, hold[1, now], value_grad)
        grad_query.append(query_grad[:half] + query_grad[half:])
        ds_ref[0, side : side + 1, :] = slope_grad
    dq_ref[...] = jnp.concatenate(grad_query, axis=0).T * scale


def attend_specs(rows, total, pairs):
    lanes = lambda at: pl.BlockSpec((rows, LANES), lambda i, at=at: (0, at + i))
    wide = lambda at: pl.BlockSpec((total, LANES), lambda i, at=at: (0, at + i))
    return [
        pl.BlockSpec(memory_space=pltpu.SMEM),
        pl.BlockSpec((total, rows), lambda i: (0, 0)),
        lanes(0),
        wide(0),
        wide(pairs),
    ], lanes(0), pl.BlockSpec((1, 8, rows), lambda i: (i, 0, 0))


def attend_params(rows, total, width, passes):
    return dict(
        compiler_params=pltpu.CompilerParams(vmem_limit_bytes=40 * 1024 * 1024),
        cost_estimate=BRIEF,
    )


def attend(packed, both, dist, slopes):
    rows, total = packed.shape[0], both.shape[0]
    width = both.shape[1] // 2
    pairs = width // LANES
    chunk = min(total, 256)
    in_specs, lanes, logs = attend_specs(rows, total, pairs)
    return pl.pallas_call(
        functools.partial(attend_kernel, chunk, (width // slopes.shape[0]) ** -0.5),
        grid=(pairs,),
        in_specs=in_specs,
        out_specs=[lanes, logs],
        out_shape=[
            jax.ShapeDtypeStruct((rows, width), jnp.float32),
            jax.ShapeDtypeStruct((pairs, 8, rows), jnp.float32),
        ],
        scratch_shapes=[
            pltpu.VMEM((total, 2 * LANES), jnp.bfloat16),
            pltpu.VMEM((total, LANES), jnp.bfloat16),
            pltpu.VMEM((total, LANES), jnp.bfloat16),
            pltpu.VMEM((total, rows), jnp.float32),
        ],
        name="attend",
        **attend_params(rows, total, width, 12),
    )(slopes, dist, packed, both, both)


def attend_back(packed, both, dist, slopes, mixed, logs, grad_mixed):
    rows, total = packed.shape[0], both.shape[0]
    width = both.shape[1] // 2
    pairs = width // LANES
    chunk = min(total, 256)
    in_specs, lanes, log_spec = attend_specs(rows, total, pairs)
    dq, dkv, ds = pl.pallas_call(
        functools.partial(attend_back_kernel, chunk, (width // slopes.shape[0]) ** -0.5),
        grid=(pairs,),
        in_specs=in_specs + [lanes, lanes, log_spec],
        out_specs=[lanes, pl.BlockSpec((2, total, LANES), lambda i: (0, 0, i)), log_spec],
        out_shape=[
            jax.ShapeDtypeStruct((rows, width), jnp.float32),
            jax.ShapeDtypeStruct((2, total, width), jnp.float32),
            jax.ShapeDtypeStruct((pairs, 8, rows), jnp.float32),
        ],
        scratch_shapes=[
            pltpu.VMEM((total, 2 * LANES), jnp.bfloat16),
            pltpu.VMEM((total, 2 * LANES), jnp.bfloat16),
            pltpu.VMEM((total, LANES), jnp.bfloat16),
            pltpu.VMEM((total, LANES), jnp.bfloat16),
            pltpu.VMEM((2, total, LANES), jnp.float32),
        ],
        name="attend_back",
        **attend_params(rows, total, width, 30),
    )(slopes, dist, packed, both, both, mixed, grad_mixed, logs)
    return dq, dkv, -jnp.sum(ds[:, :2], axis=2).reshape(-1)


def body(
    frames,
    embedding,
    cotangent,
    expert_ids,
    lengths,
    norm_gain,
    norm_bias,
    router,
    attention_in,
    attention_out,
    slopes,
    conv_point,
    conv_depth,
    batch_gain,
    batch_bias,
    conv_out,
    expert_in,
    expert_out,
):
    packed_weight = attention_in.astype(jnp.float32)
    mixing_weight = attention_out.astype(jnp.float32)
    point_weight = conv_point.astype(jnp.float32)
    project_weight = conv_out.astype(jnp.float32)
    inner_weight = [expert_in[b, 0] for b in (0, 1)]
    outer_weight = [expert_out[b, 0] for b in (0, 1)]
    micro, rows, width = frames.shape
    experts = router.shape[2]
    heads = slopes.shape[0]
    kernel = conv_depth.shape[0]
    half = kernel // 2
    capacity = 2 * rows // experts
    everyone = bits_of("dp") + bits_of("ep")
    layout = Layout(micro, rows, capacity)
    place, part_lengths, counts = layout.places(lengths)
    key_place = layout.key_places()
    parts = len(part_lengths)
    part_rows = micro * rows // parts
    valid_f = jnp.concatenate([(place < length) for length in part_lengths]).astype(jnp.float32)[:, None]
    to_parts = lambda v: v.reshape((parts, part_rows) + v.shape[1:])
    spread = lambda v: jnp.broadcast_to(v[:, None], (parts, part_rows) + v.shape[1:]).reshape(parts * part_rows, -1)

    slots = experts * micro * capacity
    own = (jnp.arange(LANES, dtype=jnp.int32) == layout.z).astype(jnp.float32)[None, :]
    norms = [jnp.stack([norm_gain[i], norm_bias[i]]) for i in range(norm_gain.shape[0])]
    routers = [jnp.pad(router[b], ((0, 0), (0, LANES - experts))) for b in (0, 1)]
    wide = inner_weight[0].shape[1]
    ids = jnp.moveaxis(expert_ids[..., 0], 0, 2)
    rank = [ranks(ids[..., b], experts) for b in (0, 1)]
    home = [tables_of(layout.home_slots(ids[..., b], rank[b]), slots) for b in (0, 1)]
    groups = range(experts // 2)
    home_rows = embedding.reshape(-1, width)
    home_logits = [product(router[b].T, home_rows.T) for b in (0, 1)]
    home_place = layout.z * rows + jnp.arange(rows, dtype=jnp.int32)
    home_valid = (home_place[None, :] < lengths[:, layout.d][:, None]).astype(jnp.float32).reshape(1, -1)
    spare = jnp.zeros((-(experts + 1) % 8, micro * rows), jnp.float32)
    extras = [
        pick_columns(jnp.concatenate([home_logits[b], home_valid, spare], axis=0), home[b][1]) for b in (0, 1)
    ]

    work_ids = layout.ids_to_work(ids)
    sources = layout.home_to_expert(pick(home[0][0], frames.reshape(-1, width)), extras[0], (work_ids,))
    kept_first = []
    back = []
    last = ()
    for group in groups:
        hidden, extra = sources[group]
        hidden, extra = after(hidden, *last), lanes_of(extra)
        fixed = (own, norms[0], routers[0], inner_weight[0], outer_weight[0])
        new, result, pre = expert_call(
            forward_kernel, "forward", experts, (hidden, extra), fixed, (width, width, wide), False, False, 2
        )
        last = (new,)
        kept_first.append(((hidden, extra), (result, pre), fixed))
        back += layout.hops(new, group)
    work = [
        tables_of(layout.work_slots(work_ids[..., b], ranks(work_ids[..., b], experts)), slots) for b in (0, 1)
    ]
    first = pick(work[0][1], jnp.concatenate(back, axis=0))

    def attention_front(values, gain_now, shift_now, weight_now):
        return product(norm_rows(values, gain_now, shift_now), weight_now)

    packed, attention_pull = jax.vjp(attention_front, first, norm_gain[1], norm_bias[1], packed_weight)
    packed, cot_rows = lax.optimization_barrier((packed, cotangent.reshape(-1, width)))
    pulls = layout.home_to_expert(pick(home[1][0], cot_rows), extras[1])
    packed_parts = to_parts(packed)
    apart = jnp.abs(key_place[:, None] - place[None, :]).astype(jnp.float32)
    kept_attention = []
    mixed_parts = []
    for part in range(parts):
        both = layout.gather(packed_parts[part, :, width:])
        dist = jnp.where((key_place < part_lengths[part])[:, None], apart, FAR)
        mixed, logs = attend(packed_parts[part], both, dist, slopes)
        kept_attention.append((both, dist, mixed, logs))
        mixed_parts.append(mixed)
    mixed_all = jnp.concatenate(mixed_parts, axis=0)
    second = first + product(mixed_all, mixing_weight)

    def conv_front(values, gain_now, shift_now, point_now):
        both = product(norm_rows(values, gain_now, shift_now), point_now)
        return both[:, :width] * jax.nn.sigmoid(both[:, width:]) * valid_f

    gated, conv_pull = jax.vjp(conv_front, second, norm_gain[2], norm_bias[2], point_weight)
    padded = [layout.halo(v, half) for v in to_parts(gated)]
    conv_parts = []
    for part in range(parts):
        total = conv_depth[0] * padded[part][0:part_rows]
        for offset in range(1, kernel):
            total = total + conv_depth[offset] * padded[part][offset : offset + part_rows]
        conv_parts.append(total)
    conv = jnp.concatenate(conv_parts, axis=0)
    stats = layout.batch_total(
        jnp.stack([jnp.sum(to_parts(conv * valid_f), axis=1), jnp.sum(to_parts(conv * conv * valid_f), axis=1)], axis=1)
    )
    centre = stats[:, 0] / counts[:, None]
    inverse_dev = lax.rsqrt(stats[:, 1] / counts[:, None] - centre * centre + EPS)
    scaled = (conv - spread(centre)) * spread(inverse_dev)
    shaped = scaled * batch_gain + batch_bias
    swished = jax.nn.silu(shaped)
    third = second + product(swished, project_weight)

    sent = pick(work[1][0], third)
    results, back, kept, small = [], [], [], []
    arrived, last = (), ()
    for group in groups:
        hidden = layout.hops(after(layout.group_of(sent, group), *arrived), group)
        arrived = tuple(hidden)
        pull_now, extra = pulls[group]
        result, grad, grad_logits, normed, active, grad_result, grad_pre, sums = expert_call(
            both_kernel,
            "both",
            experts,
            (jnp.concatenate(after(hidden, *last), axis=0), lanes_of(extra), pull_now),
            (own, norms[3], norms[4], routers[1], inner_weight[1], outer_weight[1]),
            (width, width, LANES, width, wide, width, wide),
            True,
            True,
            4,
        )
        last = (grad,)
        results.append((result, grad_logits[:, : experts + (-experts % 8)].T))
        kept.append((normed, active, grad_result, grad_pre))
        small.append((sums, product(normed.T, grad_logits[:, :experts])))
        back += layout.hops(grad, group)
    sums, router_one = add_up(small)
    gain_three, shift_three, gain_four, shift_four = (sums[k] for k in range(4))
    kept, _ = lax.optimization_barrier((kept, back[:-2]))
    expert_one = lax.psum(expert_weight_grads(kept, False), "dp")
    grad_third = pick(work[1][1], jnp.concatenate(back, axis=0))
    project_grad = product(swished.T, grad_third)
    grad_shaped = product(grad_third, project_weight.T) * swish_slope(shaped)
    sums = jnp.stack(
        [jnp.sum(to_parts(grad_shaped), axis=1), jnp.sum(to_parts(grad_shaped * scaled), axis=1)], axis=1
    )
    totals = layout.batch_total(sums)
    shift_total, gain_total = totals[:, 0], totals[:, 1]
    results, _ = lax.optimization_barrier((results, totals))
    output_slots, logit_slots = layout.opened(layout.expert_to_home(results))
    output = pick(home[1][1], output_slots).reshape(micro, rows, width)
    logit_one = pick_columns(logit_slots[:experts], home[1][0])
    router_one = router_one + product(logit_one, home_rows).T
    grad_conv = (
        batch_gain
        * spread(inverse_dev)
        * (grad_shaped - valid_f * (spread(shift_total) + scaled * spread(gain_total)) / spread(counts[:, None]))
    )
    depth_grad = 0.0
    gated_parts = []
    for part, now in enumerate(to_parts(grad_conv)):
        grad_pad = layout.halo(now, half)
        total = conv_depth[0] * grad_pad[2 * half : 2 * half + part_rows]
        for offset in range(1, kernel):
            total = total + conv_depth[offset] * grad_pad[2 * half - offset : 2 * half - offset + part_rows]
        gated_parts.append(total)
        depth_grad = depth_grad + jnp.stack(
            [jnp.sum(now * padded[part][offset : offset + part_rows], axis=0) for offset in range(kernel)]
        )
    grad_hidden, gain_two, shift_two, point_grad = conv_pull(jnp.concatenate(gated_parts, axis=0))
    grad_second = grad_third + grad_hidden

    mixing_grad = product(mixed_all.T, grad_second)
    grad_mixed = to_parts(product(grad_second, mixing_weight.T))
    packed_back = []
    slope_grad = 0.0
    for part in range(parts):
        both, dist, mixed, logs = kept_attention[part]
        grad_query, grad_both, slope_now = attend_back(
            packed_parts[part], both, dist, slopes, mixed, logs, grad_mixed[part]
        )
        slope_grad = slope_grad + slope_now
        grad_both = layout.scatter(grad_both)
        packed_back.append(jnp.concatenate([grad_query, grad_both[0], grad_both[1]], axis=1))
    grad_hidden, gain_one, shift_one, packed_grad = attention_pull(jnp.concatenate(packed_back, axis=0))
    grad_first = grad_second + grad_hidden
    early = jnp.concatenate(
        [
            jnp.stack([gain_one, gain_two, gain_three, gain_four, shift_one, shift_two, shift_three, shift_four]),
            router_one.T,
            jnp.pad(slope_grad, (0, width - heads))[None],
            depth_grad,
            jnp.sum(sums, axis=0),
        ],
        axis=0,
    )
    dense = DenseSum(
        [jnp.concatenate([packed_grad, project_grad], axis=1), jnp.concatenate([mixing_grad, point_grad], axis=1)]
    )
    over_dp, over_ep = len(bits_of("dp")), len(bits_of("ep"))

    sent = pick(work[0][0], grad_first)
    sources, kept, small = [], [], []
    arrived, last = (), ()
    for group in groups:
        grad = layout.hops(after(layout.group_of(sent, group), *arrived), group)
        arrived = tuple(grad)
        grad = after(grad, *last)
        if group == 0:
            grad, expert_one = lax.optimization_barrier((grad, expert_one))
        (hidden, extra), saved, fixed = kept_first[group]
        new, grad_logits, normed, active, grad_result, grad_pre, sums = expert_call(
            backward_kernel,
            "backward",
            experts,
            (hidden, extra, jnp.concatenate(grad, axis=0)) + saved,
            fixed,
            (width, LANES, width, wide, width, wide),
            True,
            False,
            2,
        )
        if group == 0:
            new = dense.step(new)
        if group == 1:
            new = dense.step(new, over_dp - 2)
        last = (new,)
        sources.append((new, grad_logits[:, : experts + (-experts % 8)].T))
        kept.append((normed, active, grad_result, grad_pre))
        small.append((sums, product(normed.T, grad_logits[:, :experts])))
    sums, router_zero = add_up(small)
    gain_zero, shift_zero = sums[0], sums[1]
    expert_zero = expert_weight_grads(kept, True)
    sources, dense.parts = after((sources, dense.parts), *expert_zero)
    expert_zero = lax.psum(expert_zero, "dp")
    logit_slots = jnp.concatenate(layout.expert_to_home([(more.T, more[:0]) for _, more in sources]), axis=0).T
    logit_zero = pick_columns(logit_slots[:experts], home[0][0])
    router_zero = router_zero + product(logit_zero, home_rows).T
    late = jnp.concatenate([gain_zero[None], shift_zero[None], router_zero.T, early], axis=0)
    ahead = 2 * over_ep + 1
    for step in bits_of("ep") + bits_of("dp"):
        late = late + swap(late, *step)
        if ahead:
            late = dense.step(late)
            ahead -= 1
    frame_rows, late = dense.step(([v for v, _ in sources], late), ahead) if ahead else lax.optimization_barrier(
        ([v for v, _ in sources], late)
    )
    frame_messages = layout.expert_to_home([(v, jnp.zeros((0, v.shape[0]), v.dtype)) for v in frame_rows])
    wholes = [lax.pad(one[None], 0.0, ((1, 0, 0), (0, 0, 0), (0, 0, 0))) for one in expert_one]
    frame_messages, wholes = dense.step((frame_messages, wholes), over_dp - 1)
    frames_grad = pick(home[0][1], jnp.concatenate(frame_messages, axis=0)).reshape(micro, rows, width)
    late = dense.step(late)
    late, early = late[: 2 + experts], late[2 + experts :]
    packed_grad, project_grad = dense.parts[0][:, : 3 * width], dense.parts[0][:, 3 * width :]
    mixing_grad, point_grad = dense.parts[1][:, :width], dense.parts[1][:, width:]
    expert_grads = []
    for zero, whole in zip(expert_zero, wholes):
        expert_grads.append(lax.dynamic_update_slice(whole, zero[None], (0, 0, 0))[:, None])

    at = 8 + experts
    gain_grad = jnp.concatenate([late[:1], early[:4]], axis=0)
    shift_grad = jnp.concatenate([late[1:2], early[4:8]], axis=0)
    router_grad = jnp.stack([late[2 : 2 + experts].T, early[8:at].T])
    return (
        output,
        frames_grad,
        gain_grad,
        shift_grad,
        router_grad,
        packed_grad,
        mixing_grad,
        early[at, :heads],
        point_grad,
        early[at + 1 : at + 1 + kernel],
        early[at + 2 + kernel],
        early[at + 1 + kernel],
        project_grad,
        expert_grads[0],
        expert_grads[1],
    )


def solution(mesh):
    rows = P(None, ("dp", "ep"), None)
    whole = P()
    split = P(None, "ep", None, None)
    return jax.shard_map(
        body,
        mesh=mesh,
        in_specs=(rows, rows, rows, P(None, None, ("dp", "ep"), None)) + (whole,) * 12 + (split, split),
        out_specs=(rows, rows) + (whole,) * 11 + (split, split),
        check_vma=False,
    )
```

```python
import functools

import jax
import jax.numpy as jnp
from jax import lax
from jax.experimental import pallas as pl
from jax.experimental.pallas import tpu as pltpu
from jax.sharding import PartitionSpec as P

HIGH = lax.Precision.HIGH
EPS = 1e-05
FAR = 1e30
LANES = 128
BRIEF = pl.CostEstimate(flops=1, bytes_accessed=1, transcendentals=0)


def product(left, right):
    return jnp.matmul(left, right, precision=HIGH)


def after(values, *earlier):
    return lax.optimization_barrier((values,) + earlier)[0]


def swap(values, axis, bit):
    count = lax.axis_size(axis)
    return lax.ppermute(values, axis, [(i, i ^ bit) for i in range(count)])


def bits_of(axis):
    count = lax.axis_size(axis)
    return [(axis, 1 << k) for k in range(count.bit_length() - 1)]


def butterfly(values, steps):
    for axis, bit in steps:
        values = values + swap(values, axis, bit)
    return values


def upper(step):
    axis, bit = step
    return (lax.axis_index(axis) // bit) % 2


def halve(values, step):
    side = upper(step)
    half = values.shape[0] // 2
    keep = lax.dynamic_slice_in_dim(values, side * half, half, 0)
    send = lax.dynamic_slice_in_dim(values, (1 - side) * half, half, 0)
    return keep + swap(send, *step)


def join(values, step):
    side = upper(step)
    other = swap(values, *step)
    half = values.shape[0]
    out = jnp.zeros((2 * half,) + values.shape[1:], values.dtype)
    out = lax.dynamic_update_slice_in_dim(out, values, side * half, 0)
    return lax.dynamic_update_slice_in_dim(out, other, (1 - side) * half, 0)


class DenseSum:
    def __init__(self, pair):
        first, *rest = bits_of("dp")
        far = bits_of("ep")[::-1]
        self.orders = [[first] + rest + far, [first] + rest[::-1] + far]
        self.parts = list(pair)
        count = len(self.orders[0])
        self.ways = [(halve, k) for k in range(count)] + [(join, k) for k in range(count - 1, -1, -1)]

    def step(self, value, count=1):
        for _ in range(count):
            way, k = self.ways.pop(0)
            self.parts = [way(part, order[k]) for part, order in zip(self.parts, self.orders)]
        value, self.parts = lax.optimization_barrier((value, self.parts))
        return value


class Layout:
    def __init__(self, micro, rows, capacity):
        self.micro, self.rows, self.capacity = micro, rows, capacity
        self.ep, self.dp = lax.axis_size("ep"), lax.axis_size("dp")
        self.z, self.d = lax.axis_index("ep"), lax.axis_index("dp")
        self.paired = micro == 2 and self.ep == 4 and self.dp % 2 == 0
        self.core = self.d % 2

    def route(self, low, u, home):
        pairs = []
        for d in range(self.dp):
            for z in range(self.ep):
                there = (d - d % 2 + z // 2) * self.ep + 2 * ((z % 2) ^ u) + (low ^ (d % 2))
                pairs.append((d * self.ep + z, there))
        return [(j, i) for i, j in pairs] if home else pairs

    def piece(self, values, at, count, axis=0):
        return lax.slice_in_dim(values, at * self.capacity, (at + count) * self.capacity, axis=axis)

    def home_slots(self, ids, rank):
        block = jnp.arange(self.micro, dtype=jnp.int32)[:, None]
        if not self.paired:
            return self.work_slots(ids, rank)
        step = ids ^ (2 * block + self.core)
        u = (self.z % 2) ^ (ids // 2)
        return (((step % 2) * 2 + u) * 2 + step // 2) * self.capacity + rank

    def work_slots(self, ids, rank):
        block = jnp.arange(self.micro, dtype=jnp.int32)[:, None]
        step = ids ^ self.z
        groups = self.ep // 2
        inner = block ^ (ids // 2) if self.paired else block
        return ((step % groups * 2 + step // groups) * self.micro + inner) * self.capacity + rank

    def hop(self, values, step):
        return values if step == 0 else swap(values, "ep", step)

    def hops(self, values, group):
        half = values.shape[0] // 2
        return [self.hop(values[h * half : (h + 1) * half], group + h * (self.ep // 2)) for h in (0, 1)]

    def group_of(self, values, group):
        return self.piece(values, group * 2 * self.micro, 2 * self.micro)

    def home_to_expert(self, rows, extra, ahead=()):
        wide = rows.shape[1]
        few = extra.shape[0]
        count = self.micro * self.capacity
        out = []
        last = ()
        for group in range(self.ep // 2):
            got = []
            for u in (0, 1):
                at = (group * 2 + u) * self.micro
                more = self.piece(extra, at, self.micro, 1)
                message = jnp.concatenate(
                    [self.piece(rows, at, self.micro), jnp.pad(more, ((0, 0), (0, wide - count)))], axis=0
                )
                message = after(message, *last)
                if self.paired:
                    got.append(lax.ppermute(message, ("dp", "ep"), self.route(group, u, False)))
                else:
                    got.append(self.hop(message, group + u * (self.ep // 2)))
            last = tuple(got) + tuple(ahead)
            rows_got = [v[:count] for v in got]
            more_got = [v[count:, :count] for v in got]
            if self.paired:
                order = [(u, h) for h in (0, 1) for u in (0, 1)]
                rows_got = [self.piece(rows_got[u], h, 1) for u, h in order]
                more_got = [self.piece(more_got[u], h, 1, 1) for u, h in order]
            out.append((jnp.concatenate(rows_got, axis=0), jnp.concatenate(more_got, axis=1)))
        return out

    def expert_to_home(self, groups):
        messages = []
        for group, (rows, more) in enumerate(groups):
            wide = rows.shape[1]
            for u in (0, 1):
                if self.paired:
                    row = jnp.concatenate([self.piece(rows, 2 * h + u, 1) for h in (0, 1)], axis=0)
                    few = jnp.concatenate([self.piece(more, 2 * h + u, 1, 1) for h in (0, 1)], axis=1)
                else:
                    row, few = self.piece(rows, u * self.micro, self.micro), self.piece(more, u * self.micro, self.micro, 1)
                message = row
                if more.shape[0]:
                    message = jnp.concatenate([row, jnp.pad(few, ((0, 0), (0, wide - few.shape[1])))], axis=0)
                if self.paired:
                    messages.append(lax.ppermute(message, ("dp", "ep"), self.route(group, u, True)))
                else:
                    messages.append(self.hop(message, group + u * (self.ep // 2)))
        return messages

    def opened(self, messages):
        count = self.micro * self.capacity
        return (
            jnp.concatenate([v[:count] for v in messages], axis=0),
            jnp.concatenate([v[count:, :count] for v in messages], axis=1),
        )

    def ids_to_work(self, ids):
        if not self.paired:
            return ids
        values = jnp.swapaxes(ids, 1, 2).astype(jnp.float32)
        out = []
        for turn in (0, 1):
            pairs = []
            for d in range(self.dp):
                for z in range(self.ep):
                    m = (z % 2) ^ turn
                    pairs.append((d * self.ep + z, (d - d % 2 + z // 2) * self.ep + 2 * m + d % 2))
            block = lax.dynamic_index_in_dim(values, (self.z % 2) ^ turn, 0, keepdims=False)
            out.append(lax.ppermute(block, ("dp", "ep"), pairs))
        m = self.z // 2
        both = jnp.stack([jnp.where(m == 0, out[0], out[1]), jnp.where(m == 0, out[1], out[0])])
        return jnp.swapaxes(both, 1, 2).astype(jnp.int32)

    def places(self, lengths):
        counts = jnp.sum(lengths, axis=1).astype(jnp.float32)
        if self.paired:
            m = self.z // 2
            place = self.core * 2 * self.rows + jnp.arange(2 * self.rows, dtype=jnp.int32)
            group = self.d - self.core + self.z % 2
            return place, [lengths[m, group]], counts[m][None]
        place = self.z * self.rows + jnp.arange(self.rows, dtype=jnp.int32)
        return place, [lengths[m, self.d] for m in range(self.micro)], counts

    def gather(self, values):
        if self.paired:
            return jnp.concatenate([values, swap(values, "dp", 1)], axis=0)
        return lax.all_gather(values, "ep", axis=0, tiled=True)

    def key_places(self):
        if self.paired:
            base = jnp.arange(2 * self.rows, dtype=jnp.int32)
            return jnp.concatenate([base + self.core * 2 * self.rows, base + (1 - self.core) * 2 * self.rows])
        return jnp.arange(self.ep * self.rows, dtype=jnp.int32)

    def scatter(self, values):
        if self.paired:
            half = values.shape[1] // 2
            return values[:, :half] + swap(values[:, half:], "dp", 1)
        return lax.psum_scatter(values, "ep", scatter_dimension=1, tiled=True)

    def halo(self, values, width):
        length = values.shape[0]
        if self.paired:
            low = self.core == 0
            edge = jnp.where(low, values[length - width :], values[:width])
            other = swap(edge, "dp", 1)
            zero = jnp.zeros_like(other)
            before, after = jnp.where(low, zero, other), jnp.where(low, other, zero)
        else:
            up = [(i, i + 1) for i in range(self.ep - 1)]
            down = [(j, i) for i, j in up]
            before = lax.ppermute(values[length - width :], "ep", up)
            after = lax.ppermute(values[:width], "ep", down)
        return jnp.concatenate([before, values, after], axis=0)

    def batch_total(self, values):
        if self.paired:
            return butterfly(values, bits_of("dp") + [("ep", 1)])
        return butterfly(values, bits_of("dp") + bits_of("ep"))


def norm_rows(values, gain, shift):
    center = values - jnp.mean(values, axis=-1, keepdims=True)
    spread = jnp.mean(center * center, axis=-1, keepdims=True)
    return center * lax.rsqrt(spread + EPS) * gain + shift


def swish_slope(values):
    squash = jax.nn.sigmoid(values)
    return squash * (1.0 + values * (1.0 - squash))


def ranks(ids, experts):
    rows = ids.shape[1]
    onehot = (ids[..., None] == jnp.arange(experts, dtype=jnp.int32)).astype(jnp.float32)
    below = (jnp.arange(rows)[:, None] > jnp.arange(rows)[None, :]).astype(jnp.float32)
    before = jnp.einsum("rs,bse->bre", below, onehot)
    return jnp.sum(before * onehot, axis=2).astype(jnp.int32)


def tables_of(slot, count):
    spots = jnp.arange(count, dtype=jnp.int32)
    flat = slot.reshape(-1)
    return (
        (spots[:, None] == flat[None, :]).astype(jnp.bfloat16),
        (flat[:, None] == spots[None, :]).astype(jnp.bfloat16),
    )


def pick(table, values):
    return jnp.matmul(table.astype(jnp.float32), values, precision=HIGH)


def pick_columns(values, table):
    return jnp.matmul(values, table.astype(jnp.float32), precision=HIGH)


def product_two(left, right, dot):
    head, rest = parted(left)
    return dot(narrow(head), right) + dot(narrow(rest), right)


def exact_dot(left, right, contract):
    return lax.dot_general(
        left, right, (contract, ((), ())), precision=lax.Precision.HIGHEST, preferred_element_type=jnp.float32
    )


def norm_parts(values):
    center = values - jnp.mean(values, axis=1, keepdims=True)
    scale = lax.rsqrt(jnp.mean(center * center, axis=1, keepdims=True) + EPS)
    return center * scale, scale


def norm_back(grad, gain, normal, scale):
    weighed = grad * gain
    centred = weighed - jnp.mean(weighed, axis=1, keepdims=True)
    return scale * (centred - normal * jnp.mean(weighed * normal, axis=1, keepdims=True))


def gate_parts(hidden, extra, own, norm, router, experts):
    normal, scale = norm_parts(hidden)
    normed = normal * norm[0:1] + norm[1:2]
    lane = lax.broadcasted_iota(jnp.int32, (1, LANES), 1)
    logits = exact_dot(normed, router, ((1,), (0,))) + extra
    logits = jnp.where(lane < experts, logits, -FAR)
    raised = jnp.exp(logits - jnp.max(logits, axis=1, keepdims=True))
    probs = raised / jnp.sum(raised, axis=1, keepdims=True)
    return normal, scale, normed, probs, jnp.sum(probs * own, axis=1, keepdims=True)


def hidden_columns(weight_in):
    wide = min(512, weight_in.shape[1])
    return [pl.ds(at, wide) for at in range(0, weight_in.shape[1], wide)]


def forward_part(hidden, extra, own, norm, router, weight_in, weight_out, pre, experts):
    parts = gate_parts(hidden, extra, own, norm, router, experts)
    result = 0.0
    for now in hidden_columns(weight_in):
        before = product_two(parts[2], weight_in[:, now], dot_nn)
        pre[:, now] = before
        result = result + product_two(before * jax.nn.sigmoid(before), weight_out[now, :], dot_nn)
    return parts, result, hidden + 0.5 * parts[4] * result


def backward_part(grad, result, parts, own, norm, router, weight_in, weight_out, pre, active, grad_pre):
    normal, scale, normed, probs, gate = parts
    grad_result = 0.5 * gate * grad
    grad_gate = 0.5 * jnp.sum(grad * result, axis=1, keepdims=True)
    grad_logits = grad_gate * probs * (own - gate)
    grad_normed = exact_dot(grad_logits, router, ((1,), (1,)))
    for now in hidden_columns(weight_in):
        before = pre[:, now]
        squash = jax.nn.sigmoid(before)
        active[:, now] = before * squash
        slope = squash * (1.0 + before * (1.0 - squash))
        now_grad = product_two(grad_result, weight_out[now, :], dot_nt) * slope
        grad_pre[:, now] = now_grad
        grad_normed = grad_normed + product_two(now_grad, weight_in[:, now], dot_nt)
    sums = [jnp.sum(grad_normed * normal, axis=0, keepdims=True), jnp.sum(grad_normed, axis=0, keepdims=True)]
    return grad + norm_back(grad_normed, norm[0:1], normal, scale), grad_result, grad_logits, sums


def add_rows(out, rows):
    @pl.when(pl.program_id(0) == 0)
    def _():
        out[...] = jnp.zeros_like(out)

    for at, row in enumerate(rows):
        out[at : at + 1, :] += row


def forward_kernel(experts, hidden, extra, own, norm, router, weight_in, weight_out, new, result, pre):
    _, result[...], new[...] = forward_part(
        hidden[...], extra[...], own[...], norm[...], router[...], weight_in, weight_out, pre, experts
    )


def backward_kernel(
    experts, hidden, extra, grad, result, pre, own, norm, router, weight_in, weight_out,
    back, logits, normed, active, grad_result, grad_pre, sums,
):
    parts = gate_parts(hidden[...], extra[...], own[...], norm[...], router[...], experts)
    back[...], grad_result[...], logits[...], rows = backward_part(
        grad[...], result[...], parts, own[...], norm[...], router[...], weight_in, weight_out, pre, active, grad_pre
    )
    normed[...] = parts[2]
    add_rows(sums, rows)


def both_kernel(
    experts, hidden, extra, pull, own, norm, last, router, weight_in, weight_out,
    output, back, logits, normed, active, grad_result, grad_pre, sums, pre,
):
    parts, result, new = forward_part(
        hidden[...], extra[...], own[...], norm[...], router[...], weight_in, weight_out, pre, experts
    )
    lane = lax.broadcasted_iota(jnp.int32, (1, LANES), 1)
    valid = jnp.sum(jnp.where(lane == experts, extra[...], 0.0), axis=1, keepdims=True)
    normal, scale = norm_parts(new)
    output[...] = (normal * last[0:1] + last[1:2]) * valid
    grad = pull[...] * valid
    last_sums = [jnp.sum(grad * normal, axis=0, keepdims=True), jnp.sum(grad, axis=0, keepdims=True)]
    back[...], grad_result[...], logits[...], rows = backward_part(
        norm_back(grad, last[0:1], normal, scale), result, parts, own[...], norm[...], router[...],
        weight_in, weight_out, pre, active, grad_pre,
    )
    normed[...] = parts[2]
    add_rows(sums, rows + last_sums)


def expert_call(kernel, name, experts, by_rows, fixed, widths, sums, hold, products):
    rows, width = by_rows[0].shape
    block = min(256, rows)
    row_spec = lambda wide: pl.BlockSpec((block, wide), lambda i: (i, 0))
    full = lambda v: pl.BlockSpec(v.shape, lambda i: (0, 0))
    out_specs = [row_spec(wide) for wide in widths]
    out_shape = [jax.ShapeDtypeStruct((rows, wide), jnp.float32) for wide in widths]
    if sums:
        out_specs.append(pl.BlockSpec((8, width), lambda i: (0, 0)))
        out_shape.append(jax.ShapeDtypeStruct((8, width), jnp.float32))
    inner = fixed[-2].shape[1]
    return pl.pallas_call(
        functools.partial(kernel, experts),
        grid=(rows // block,),
        in_specs=[row_spec(v.shape[1]) for v in by_rows] + [full(v) for v in fixed],
        out_specs=out_specs,
        out_shape=out_shape,
        scratch_shapes=[pltpu.VMEM((block, inner), jnp.float32)] if hold else [],
        compiler_params=pltpu.CompilerParams(vmem_limit_bytes=48 * 1024 * 1024),
        cost_estimate=BRIEF,
        name=name,
    )(*by_rows, *fixed)


def lanes_of(extra):
    return jnp.pad(extra.T, ((0, 0), (0, LANES - extra.shape[0])))


def weight_kernel(groups, *refs):
    normed, grad_result, active, grad_pre = (refs[k * groups : (k + 1) * groups] for k in range(4))
    inner, outer = refs[4 * groups :]

    def summed(left, right):
        total = 0.0
        for one, two in zip(left, right):
            (a_hi, a_lo), (b_hi, b_lo) = parted(one[...]), parted(two[...])
            a_hi, a_lo, b_hi, b_lo = narrow(a_hi), narrow(a_lo), narrow(b_hi), narrow(b_lo)
            total = total + dot_tn(a_hi, b_hi) + dot_tn(a_lo, b_hi) + dot_tn(a_hi, b_lo)
        return total

    outer[...] = summed(active, grad_result)
    inner[...] = summed(normed, grad_pre)


def expert_weight_grads(kept):
    normed, active, grad_result, grad_pre = zip(*kept)
    rows, width = normed[0].shape
    inner = active[0].shape[1]
    wide = min(512, inner)
    full = pl.BlockSpec((rows, width), lambda i: (0, 0))
    part = pl.BlockSpec((rows, wide), lambda i: (0, i))
    count = len(kept)
    return pl.pallas_call(
        functools.partial(weight_kernel, count),
        grid=(inner // wide,),
        in_specs=[full] * (2 * count) + [part] * (2 * count),
        out_specs=[pl.BlockSpec((width, wide), lambda i: (0, i)), pl.BlockSpec((wide, width), lambda i: (i, 0))],
        out_shape=[
            jax.ShapeDtypeStruct((width, inner), jnp.float32),
            jax.ShapeDtypeStruct((inner, width), jnp.float32),
        ],
        compiler_params=pltpu.CompilerParams(vmem_limit_bytes=48 * 1024 * 1024),
        cost_estimate=pl.CostEstimate(
            flops=12 * count * rows * width * inner, bytes_accessed=16 * count * rows * inner, transcendentals=0
        ),
        name="weights",
    )(*normed, *grad_result, *active, *grad_pre)


def add_up(trees):
    total = trees[0]
    for tree in trees[1:]:
        total = jax.tree.map(jnp.add, total, tree)
    return total


def parted(values):
    head = values.astype(jnp.bfloat16).astype(jnp.float32)
    return head, values - head


def head_lanes(side):
    low = lax.broadcasted_iota(jnp.int32, (1, LANES), 1) < LANES // 2
    turn = lambda v: pltpu.roll(v, LANES // 2, 1)
    at_low = lambda v: v if side == 0 else turn(v)
    at_high = lambda v: turn(v) if side == 0 else v
    both = lambda v, w: jnp.where(low, at_low(v), at_high(w))
    alone = lambda v, rest=0.0: jnp.where(low, at_low(v), rest)
    return both, alone


def dot_nt(left, right):
    return lax.dot_general(left, right, (((1,), (1,)), ((), ())), preferred_element_type=jnp.float32)


def dot_tn(left, right):
    return lax.dot_general(left, right, (((0,), (0,)), ((), ())), preferred_element_type=jnp.float32)


def dot_nn(left, right):
    return lax.dot_general(left, right, (((1,), (0,)), ((), ())), preferred_element_type=jnp.float32)


def narrow(*parts):
    return jnp.concatenate(parts, axis=1).astype(jnp.bfloat16) if len(parts) > 1 else parts[0].astype(jnp.bfloat16)


def attend_kernel(chunk, scale, slopes, dist, q_ref, k_ref, v_ref, out_ref, log_ref, k3, v2, v1, scores):
    pair = pl.program_id(0)
    total = k_ref.shape[0]
    q_hi, q_lo = parted(q_ref[...] * scale)
    k_hi, k_lo = parted(k_ref[...])
    v_hi, v_lo = parted(v_ref[...])
    mixed = []
    for side in (0, 1):
        both, alone = head_lanes(side)
        k3[...] = narrow(both(k_hi, k_hi), alone(k_lo))
        v2[...] = narrow(both(v_hi, v_lo))
        v1[...] = narrow(alone(v_hi))
        q3 = narrow(both(q_hi, q_lo), alone(q_hi))
        slope = slopes[2 * pair + side]
        highest = None
        for at in range(0, total, chunk):
            now = pl.ds(at, chunk)
            score = dot_nt(k3[now], q3) - slope * dist[now]
            scores[now] = score
            top = jnp.max(score, axis=0, keepdims=True)
            highest = top if highest is None else jnp.maximum(highest, top)
        summed, weight = 0.0, 0.0
        for at in range(0, total, chunk):
            now = pl.ds(at, chunk)
            raised = jnp.exp(scores[now] - highest)
            weight = weight + jnp.sum(raised, axis=0, keepdims=True)
            r_hi, r_lo = parted(raised)
            summed = summed + dot_tn(v2[now], narrow(r_hi)) + dot_tn(v1[now], narrow(r_lo))
        mixed.append((summed[: LANES // 2] + summed[LANES // 2 :]) / weight)
        log_ref[0, side : side + 1, :] = highest + jnp.log(weight)
    out_ref[...] = jnp.concatenate(mixed, axis=0).T


def attend_back_kernel(
    chunk, scale, slopes, dist, q_ref, k_ref, v_ref, o_ref, g_ref, log_ref, dq_ref, dkv_ref, ds_ref, k3, v3, k2, k1, hold
):
    pair = pl.program_id(0)
    total = k_ref.shape[0]
    q_hi, q_lo = parted(q_ref[...] * scale)
    k_hi, k_lo = parted(k_ref[...])
    v_hi, v_lo = parted(v_ref[...])
    grad = g_ref[...]
    g_hi, g_lo = parted(grad)
    weighed = grad * o_ref[...]
    lane = lax.broadcasted_iota(jnp.int32, (1, LANES), 1)
    low = lane < LANES // 2
    half = LANES // 2
    grad_query = []
    for side in (0, 1):
        both, alone = head_lanes(side)
        own = low if side == 0 else jnp.logical_not(low)
        centre = -jnp.sum(jnp.where(own, weighed, 0.0), axis=1, keepdims=True)
        c_hi, c_rest = parted(centre)
        c_mid, c_lo = parted(c_rest)
        tail = jnp.where(lane == half, c_hi, jnp.where(lane == half + 1, c_mid, jnp.where(lane == half + 2, c_lo, 0.0)))
        ones = jnp.where(jnp.logical_and(lane >= half, lane < half + 3), 1.0, 0.0)
        k3[...] = narrow(both(k_hi, k_hi), alone(k_lo))
        v3[...] = narrow(both(v_hi, v_hi), alone(v_lo, ones))
        k2[...] = narrow(both(k_hi, k_lo))
        k1[...] = narrow(alone(k_hi))
        q3 = narrow(both(q_hi, q_lo), alone(q_hi))
        q2, q1 = narrow(both(q_hi, q_lo)), narrow(alone(q_hi))
        g3 = narrow(both(g_hi, g_lo), alone(g_hi, tail))
        g2, g1 = narrow(both(g_hi, g_lo)), narrow(alone(g_hi))
        slope = slopes[2 * pair + side]
        logs = log_ref[0, side : side + 1, :]
        slope_grad, query_grad = 0.0, 0.0
        for at in range(0, total, chunk):
            now = pl.ds(at, chunk)
            far = dist[now]
            probs = jnp.exp(dot_nt(k3[now], q3) - slope * far - logs)
            grad_score = probs * dot_nt(v3[now], g3)
            slope_grad = slope_grad + jnp.sum(grad_score * far, axis=0, keepdims=True)
            p_hi, p_lo = parted(probs)
            s_hi, s_lo = parted(grad_score)
            s_hi, s_lo = narrow(s_hi), narrow(s_lo)
            value_grad = dot_nn(narrow(p_hi), g2) + dot_nn(narrow(p_lo), g1)
            key_grad = dot_nn(s_hi, q2) + dot_nn(s_lo, q1)
            query_grad = query_grad + dot_tn(k2[now], s_hi) + dot_tn(k1[now], s_lo)
            value_grad = value_grad + pltpu.roll(value_grad, half, 1)
            key_grad = key_grad + pltpu.roll(key_grad, half, 1)
            if side == 0:
                hold[0, now], hold[1, now] = key_grad, value_grad
            else:
                dkv_ref[0, now] = jnp.where(low, hold[0, now], key_grad)
                dkv_ref[1, now] = jnp.where(low, hold[1, now], value_grad)
        grad_query.append(query_grad[:half] + query_grad[half:])
        ds_ref[0, side : side + 1, :] = slope_grad
    dq_ref[...] = jnp.concatenate(grad_query, axis=0).T * scale


def attend_specs(rows, total, pairs):
    lanes = lambda at: pl.BlockSpec((rows, LANES), lambda i, at=at: (0, at + i))
    wide = lambda at: pl.BlockSpec((total, LANES), lambda i, at=at: (0, at + i))
    return [
        pl.BlockSpec(memory_space=pltpu.SMEM),
        pl.BlockSpec((total, rows), lambda i: (0, 0)),
        lanes(0),
        wide(0),
        wide(pairs),
    ], lanes(0), pl.BlockSpec((1, 8, rows), lambda i: (i, 0, 0))


def attend_params(rows, total, width, passes):
    return dict(
        compiler_params=pltpu.CompilerParams(vmem_limit_bytes=40 * 1024 * 1024),
        cost_estimate=BRIEF,
    )


def attend(packed, both, dist, slopes):
    rows, total = packed.shape[0], both.shape[0]
    width = both.shape[1] // 2
    pairs = width // LANES
    chunk = min(total, 256)
    in_specs, lanes, logs = attend_specs(rows, total, pairs)
    return pl.pallas_call(
        functools.partial(attend_kernel, chunk, (width // slopes.shape[0]) ** -0.5),
        grid=(pairs,),
        in_specs=in_specs,
        out_specs=[lanes, logs],
        out_shape=[
            jax.ShapeDtypeStruct((rows, width), jnp.float32),
            jax.ShapeDtypeStruct((pairs, 8, rows), jnp.float32),
        ],
        scratch_shapes=[
            pltpu.VMEM((total, 2 * LANES), jnp.bfloat16),
            pltpu.VMEM((total, LANES), jnp.bfloat16),
            pltpu.VMEM((total, LANES), jnp.bfloat16),
            pltpu.VMEM((total, rows), jnp.float32),
        ],
        name="attend",
        **attend_params(rows, total, width, 12),
    )(slopes, dist, packed, both, both)


def attend_back(packed, both, dist, slopes, mixed, logs, grad_mixed):
    rows, total = packed.shape[0], both.shape[0]
    width = both.shape[1] // 2
    pairs = width // LANES
    chunk = min(total, 256)
    in_specs, lanes, log_spec = attend_specs(rows, total, pairs)
    dq, dkv, ds = pl.pallas_call(
        functools.partial(attend_back_kernel, chunk, (width // slopes.shape[0]) ** -0.5),
        grid=(pairs,),
        in_specs=in_specs + [lanes, lanes, log_spec],
        out_specs=[lanes, pl.BlockSpec((2, total, LANES), lambda i: (0, 0, i)), log_spec],
        out_shape=[
            jax.ShapeDtypeStruct((rows, width), jnp.float32),
            jax.ShapeDtypeStruct((2, total, width), jnp.float32),
            jax.ShapeDtypeStruct((pairs, 8, rows), jnp.float32),
        ],
        scratch_shapes=[
            pltpu.VMEM((total, 2 * LANES), jnp.bfloat16),
            pltpu.VMEM((total, 2 * LANES), jnp.bfloat16),
            pltpu.VMEM((total, LANES), jnp.bfloat16),
            pltpu.VMEM((total, LANES), jnp.bfloat16),
            pltpu.VMEM((2, total, LANES), jnp.float32),
        ],
        name="attend_back",
        **attend_params(rows, total, width, 30),
    )(slopes, dist, packed, both, both, mixed, grad_mixed, logs)
    return dq, dkv, -jnp.sum(ds[:, :2], axis=2).reshape(-1)


def body(
    frames,
    embedding,
    cotangent,
    expert_ids,
    lengths,
    norm_gain,
    norm_bias,
    router,
    attention_in,
    attention_out,
    slopes,
    conv_point,
    conv_depth,
    batch_gain,
    batch_bias,
    conv_out,
    expert_in,
    expert_out,
):
    packed_weight = attention_in.astype(jnp.float32)
    mixing_weight = attention_out.astype(jnp.float32)
    point_weight = conv_point.astype(jnp.float32)
    project_weight = conv_out.astype(jnp.float32)
    inner_weight = [expert_in[b, 0] for b in (0, 1)]
    outer_weight = [expert_out[b, 0] for b in (0, 1)]
    micro, rows, width = frames.shape
    experts = router.shape[2]
    heads = slopes.shape[0]
    kernel = conv_depth.shape[0]
    half = kernel // 2
    capacity = 2 * rows // experts
    everyone = bits_of("dp") + bits_of("ep")
    layout = Layout(micro, rows, capacity)
    place, part_lengths, counts = layout.places(lengths)
    key_place = layout.key_places()
    parts = len(part_lengths)
    part_rows = micro * rows // parts
    valid_f = jnp.concatenate([(place < length) for length in part_lengths]).astype(jnp.float32)[:, None]
    to_parts = lambda v: v.reshape((parts, part_rows) + v.shape[1:])
    spread = lambda v: jnp.broadcast_to(v[:, None], (parts, part_rows) + v.shape[1:]).reshape(parts * part_rows, -1)

    slots = experts * micro * capacity
    own = (jnp.arange(LANES, dtype=jnp.int32) == layout.z).astype(jnp.float32)[None, :]
    norms = [jnp.stack([norm_gain[i], norm_bias[i]]) for i in range(norm_gain.shape[0])]
    routers = [jnp.pad(router[b], ((0, 0), (0, LANES - experts))) for b in (0, 1)]
    wide = inner_weight[0].shape[1]
    ids = jnp.moveaxis(expert_ids[..., 0], 0, 2)
    rank = [ranks(ids[..., b], experts) for b in (0, 1)]
    home = [tables_of(layout.home_slots(ids[..., b], rank[b]), slots) for b in (0, 1)]
    groups = range(experts // 2)
    home_rows = embedding.reshape(-1, width)
    home_logits = [product(router[b].T, home_rows.T) for b in (0, 1)]
    home_place = layout.z * rows + jnp.arange(rows, dtype=jnp.int32)
    home_valid = (home_place[None, :] < lengths[:, layout.d][:, None]).astype(jnp.float32).reshape(1, -1)
    spare = jnp.zeros((-(experts + 1) % 8, micro * rows), jnp.float32)
    extras = [
        pick_columns(jnp.concatenate([home_logits[b], home_valid, spare], axis=0), home[b][1]) for b in (0, 1)
    ]

    work_ids = layout.ids_to_work(ids)
    sources = layout.home_to_expert(pick(home[0][0], frames.reshape(-1, width)), extras[0], (work_ids,))
    kept_first = []
    back = []
    last = ()
    for group in groups:
        hidden, extra = sources[group]
        hidden, extra = after(hidden, *last), lanes_of(extra)
        fixed = (own, norms[0], routers[0], inner_weight[0], outer_weight[0])
        new, result, pre = expert_call(
            forward_kernel, "forward", experts, (hidden, extra), fixed, (width, width, wide), False, False, 2
        )
        last = (new,)
        kept_first.append(((hidden, extra), (result, pre), fixed))
        back += layout.hops(new, group)
    work = [
        tables_of(layout.work_slots(work_ids[..., b], ranks(work_ids[..., b], experts)), slots) for b in (0, 1)
    ]
    first = pick(work[0][1], jnp.concatenate(back, axis=0))

    def attention_front(values, gain_now, shift_now, weight_now):
        return product(norm_rows(values, gain_now, shift_now), weight_now)

    packed, attention_pull = jax.vjp(attention_front, first, norm_gain[1], norm_bias[1], packed_weight)
    packed, cot_rows = lax.optimization_barrier((packed, cotangent.reshape(-1, width)))
    pulls = layout.home_to_expert(pick(home[1][0], cot_rows), extras[1])
    packed_parts = to_parts(packed)
    apart = jnp.abs(key_place[:, None] - place[None, :]).astype(jnp.float32)
    kept_attention = []
    mixed_parts = []
    for part in range(parts):
        both = layout.gather(packed_parts[part, :, width:])
        dist = jnp.where((key_place < part_lengths[part])[:, None], apart, FAR)
        mixed, logs = attend(packed_parts[part], both, dist, slopes)
        kept_attention.append((both, dist, mixed, logs))
        mixed_parts.append(mixed)
    mixed_all = jnp.concatenate(mixed_parts, axis=0)
    second = first + product(mixed_all, mixing_weight)

    def conv_front(values, gain_now, shift_now, point_now):
        both = product(norm_rows(values, gain_now, shift_now), point_now)
        return both[:, :width] * jax.nn.sigmoid(both[:, width:]) * valid_f

    gated, conv_pull = jax.vjp(conv_front, second, norm_gain[2], norm_bias[2], point_weight)
    padded = [layout.halo(v, half) for v in to_parts(gated)]
    conv_parts = []
    for part in range(parts):
        total = conv_depth[0] * padded[part][0:part_rows]
        for offset in range(1, kernel):
            total = total + conv_depth[offset] * padded[part][offset : offset + part_rows]
        conv_parts.append(total)
    conv = jnp.concatenate(conv_parts, axis=0)
    stats = layout.batch_total(
        jnp.stack([jnp.sum(to_parts(conv * valid_f), axis=1), jnp.sum(to_parts(conv * conv * valid_f), axis=1)], axis=1)
    )
    centre = stats[:, 0] / counts[:, None]
    inverse_dev = lax.rsqrt(stats[:, 1] / counts[:, None] - centre * centre + EPS)
    scaled = (conv - spread(centre)) * spread(inverse_dev)
    shaped = scaled * batch_gain + batch_bias
    swished = jax.nn.silu(shaped)
    third = second + product(swished, project_weight)

    sent = pick(work[1][0], third)
    results, back, kept, small = [], [], [], []
    arrived, last = (), ()
    for group in groups:
        hidden = layout.hops(after(layout.group_of(sent, group), *arrived), group)
        arrived = tuple(hidden)
        pull_now, extra = pulls[group]
        result, grad, grad_logits, normed, active, grad_result, grad_pre, sums = expert_call(
            both_kernel,
            "both",
            experts,
            (jnp.concatenate(after(hidden, *last), axis=0), lanes_of(extra), pull_now),
            (own, norms[3], norms[4], routers[1], inner_weight[1], outer_weight[1]),
            (width, width, LANES, width, wide, width, wide),
            True,
            True,
            4,
        )
        last = (grad,)
        results.append((result, grad_logits[:, : experts + (-experts % 8)].T))
        kept.append((normed, active, grad_result, grad_pre))
        small.append((sums, product(normed.T, grad_logits[:, :experts])))
        back += layout.hops(grad, group)
    sums, router_one = add_up(small)
    gain_three, shift_three, gain_four, shift_four = (sums[k] for k in range(4))
    kept, _ = lax.optimization_barrier((kept, back[:-2]))
    expert_one = lax.psum(expert_weight_grads(kept), "dp")
    grad_third = pick(work[1][1], jnp.concatenate(back, axis=0))
    project_grad = product(swished.T, grad_third)
    grad_shaped = product(grad_third, project_weight.T) * swish_slope(shaped)
    sums = jnp.stack(
        [jnp.sum(to_parts(grad_shaped), axis=1), jnp.sum(to_parts(grad_shaped * scaled), axis=1)], axis=1
    )
    totals = layout.batch_total(sums)
    shift_total, gain_total = totals[:, 0], totals[:, 1]
    results, _ = lax.optimization_barrier((results, totals))
    output_slots, logit_slots = layout.opened(layout.expert_to_home(results))
    output = pick(home[1][1], output_slots).reshape(micro, rows, width)
    logit_one = pick_columns(logit_slots[:experts], home[1][0])
    router_one = router_one + product(logit_one, home_rows).T
    grad_conv = (
        batch_gain
        * spread(inverse_dev)
        * (grad_shaped - valid_f * (spread(shift_total) + scaled * spread(gain_total)) / spread(counts[:, None]))
    )
    depth_grad = 0.0
    gated_parts = []
    for part, now in enumerate(to_parts(grad_conv)):
        grad_pad = layout.halo(now, half)
        total = conv_depth[0] * grad_pad[2 * half : 2 * half + part_rows]
        for offset in range(1, kernel):
            total = total + conv_depth[offset] * grad_pad[2 * half - offset : 2 * half - offset + part_rows]
        gated_parts.append(total)
        depth_grad = depth_grad + jnp.stack(
            [jnp.sum(now * padded[part][offset : offset + part_rows], axis=0) for offset in range(kernel)]
        )
    grad_hidden, gain_two, shift_two, point_grad = conv_pull(jnp.concatenate(gated_parts, axis=0))
    grad_second = grad_third + grad_hidden

    mixing_grad = product(mixed_all.T, grad_second)
    grad_mixed = to_parts(product(grad_second, mixing_weight.T))
    packed_back = []
    slope_grad = 0.0
    for part in range(parts):
        both, dist, mixed, logs = kept_attention[part]
        grad_query, grad_both, slope_now = attend_back(
            packed_parts[part], both, dist, slopes, mixed, logs, grad_mixed[part]
        )
        slope_grad = slope_grad + slope_now
        grad_both = layout.scatter(grad_both)
        packed_back.append(jnp.concatenate([grad_query, grad_both[0], grad_both[1]], axis=1))
    grad_hidden, gain_one, shift_one, packed_grad = attention_pull(jnp.concatenate(packed_back, axis=0))
    grad_first = grad_second + grad_hidden
    early = jnp.concatenate(
        [
            jnp.stack([gain_one, gain_two, gain_three, gain_four, shift_one, shift_two, shift_three, shift_four]),
            router_one.T,
            jnp.pad(slope_grad, (0, width - heads))[None],
            depth_grad,
            jnp.sum(sums, axis=0),
        ],
        axis=0,
    )
    dense = DenseSum(
        [jnp.concatenate([packed_grad, project_grad], axis=1), jnp.concatenate([mixing_grad, point_grad], axis=1)]
    )
    over_dp, over_ep = len(bits_of("dp")), len(bits_of("ep"))

    sent = pick(work[0][0], grad_first)
    sources, kept, small = [], [], []
    arrived, last = (), ()
    for group in groups:
        grad = layout.hops(after(layout.group_of(sent, group), *arrived), group)
        arrived = tuple(grad)
        grad = after(grad, *last)
        if group == 0:
            grad, expert_one = lax.optimization_barrier((dense.step(grad), expert_one))
        if group == 1:
            grad = dense.step(grad)
        (hidden, extra), saved, fixed = kept_first[group]
        new, grad_logits, normed, active, grad_result, grad_pre, sums = expert_call(
            backward_kernel,
            "backward",
            experts,
            (hidden, extra, jnp.concatenate(grad, axis=0)) + saved,
            fixed,
            (width, LANES, width, wide, width, wide),
            True,
            False,
            2,
        )
        if group == 0:
            new = dense.step(new, over_dp - 2)
        if group == 1:
            new = dense.step(new, over_ep - 1)
        last = (new,)
        sources.append((new, grad_logits[:, : experts + (-experts % 8)].T))
        kept.append((normed, active, grad_result, grad_pre))
        small.append((sums, product(normed.T, grad_logits[:, :experts])))
    sums, router_zero = add_up(small)
    gain_zero, shift_zero = sums[0], sums[1]
    expert_zero = lax.psum(expert_weight_grads(kept), "dp")
    sources = dense.step(sources, over_ep + 1)
    frame_messages = layout.expert_to_home(sources)
    wholes = [lax.pad(one[None], 0.0, ((1, 0, 0), (0, 0, 0), (0, 0, 0))) for one in expert_one]
    frame_messages, wholes = dense.step((frame_messages, wholes), over_dp - 1)
    rows_back, logit_slots = layout.opened(frame_messages)
    logit_zero = pick_columns(logit_slots[:experts], home[0][0])
    router_zero = router_zero + product(logit_zero, home_rows).T
    frames_grad = pick(home[0][1], rows_back).reshape(micro, rows, width)
    late = jnp.concatenate([gain_zero[None], shift_zero[None], router_zero.T, early], axis=0)
    late = butterfly(dense.step(late), bits_of("ep") + bits_of("dp"))
    late, early = late[: 2 + experts], late[2 + experts :]
    packed_grad, project_grad = dense.parts[0][:, : 3 * width], dense.parts[0][:, 3 * width :]
    mixing_grad, point_grad = dense.parts[1][:, :width], dense.parts[1][:, width:]
    expert_grads = []
    for zero, whole in zip(expert_zero, wholes):
        expert_grads.append(lax.dynamic_update_slice(whole, zero[None], (0, 0, 0))[:, None])

    at = 8 + experts
    gain_grad = jnp.concatenate([late[:1], early[:4]], axis=0)
    shift_grad = jnp.concatenate([late[1:2], early[4:8]], axis=0)
    router_grad = jnp.stack([late[2 : 2 + experts].T, early[8:at].T])
    return (
        output,
        frames_grad,
        gain_grad,
        shift_grad,
        router_grad,
        packed_grad,
        mixing_grad,
        early[at, :heads],
        point_grad,
        early[at + 1 : at + 1 + kernel],
        early[at + 2 + kernel],
        early[at + 1 + kernel],
        project_grad,
        expert_grads[0],
        expert_grads[1],
    )


def solution(mesh):
    rows = P(None, ("dp", "ep"), None)
    whole = P()
    split = P(None, "ep", None, None)
    return jax.shard_map(
        body,
        mesh=mesh,
        in_specs=(rows, rows, rows, P(None, None, ("dp", "ep"), None)) + (whole,) * 12 + (split, split),
        out_specs=(rows, rows) + (whole,) * 11 + (split, split),
        check_vma=False,
    )
```

```python
import functools

import jax
import jax.numpy as jnp
from jax import lax
from jax.experimental import pallas as pl
from jax.experimental.pallas import tpu as pltpu
from jax.sharding import PartitionSpec as P

HIGH = lax.Precision.HIGH
EPS = 1e-05
FAR = 1e30
LANES = 128
BRIEF = pl.CostEstimate(flops=1, bytes_accessed=1, transcendentals=0)


def product(left, right):
    return jnp.matmul(left, right, precision=HIGH)


def after(values, *earlier):
    return lax.optimization_barrier((values,) + earlier)[0]


def swap(values, axis, bit):
    count = lax.axis_size(axis)
    return lax.ppermute(values, axis, [(i, i ^ bit) for i in range(count)])


def bits_of(axis):
    count = lax.axis_size(axis)
    return [(axis, 1 << k) for k in range(count.bit_length() - 1)]


def butterfly(values, steps):
    for axis, bit in steps:
        values = values + swap(values, axis, bit)
    return values


def upper(step):
    axis, bit = step
    return (lax.axis_index(axis) // bit) % 2


def halve(values, step):
    side = upper(step)
    half = values.shape[0] // 2
    keep = lax.dynamic_slice_in_dim(values, side * half, half, 0)
    send = lax.dynamic_slice_in_dim(values, (1 - side) * half, half, 0)
    return keep + swap(send, *step)


def join(values, step):
    side = upper(step)
    other = swap(values, *step)
    half = values.shape[0]
    out = jnp.zeros((2 * half,) + values.shape[1:], values.dtype)
    out = lax.dynamic_update_slice_in_dim(out, values, side * half, 0)
    return lax.dynamic_update_slice_in_dim(out, other, (1 - side) * half, 0)


class DenseSum:
    def __init__(self, pair):
        first, *rest = bits_of("dp")
        far = bits_of("ep")[::-1]
        self.orders = [[first] + rest + far, [first] + rest[::-1] + far]
        self.parts = list(pair)
        count = len(self.orders[0])
        self.ways = [(halve, k) for k in range(count)] + [(join, k) for k in range(count - 1, -1, -1)]

    def step(self, value, count=1):
        for _ in range(count):
            way, k = self.ways.pop(0)
            self.parts = [way(part, order[k]) for part, order in zip(self.parts, self.orders)]
        value, self.parts = lax.optimization_barrier((value, self.parts))
        return value


class Layout:
    def __init__(self, micro, rows, capacity):
        self.micro, self.rows, self.capacity = micro, rows, capacity
        self.ep, self.dp = lax.axis_size("ep"), lax.axis_size("dp")
        self.z, self.d = lax.axis_index("ep"), lax.axis_index("dp")
        self.paired = micro == 2 and self.ep == 4 and self.dp % 2 == 0
        self.core = self.d % 2

    def route(self, low, u, home):
        pairs = []
        for d in range(self.dp):
            for z in range(self.ep):
                there = (d - d % 2 + z // 2) * self.ep + 2 * ((z % 2) ^ u) + (low ^ (d % 2))
                pairs.append((d * self.ep + z, there))
        return [(j, i) for i, j in pairs] if home else pairs

    def piece(self, values, at, count, axis=0):
        return lax.slice_in_dim(values, at * self.capacity, (at + count) * self.capacity, axis=axis)

    def home_slots(self, ids, rank):
        block = jnp.arange(self.micro, dtype=jnp.int32)[:, None]
        if not self.paired:
            return self.work_slots(ids, rank)
        step = ids ^ (2 * block + self.core)
        u = (self.z % 2) ^ (ids // 2)
        return (((step % 2) * 2 + u) * 2 + step // 2) * self.capacity + rank

    def work_slots(self, ids, rank):
        block = jnp.arange(self.micro, dtype=jnp.int32)[:, None]
        step = ids ^ self.z
        groups = self.ep // 2
        inner = block ^ (ids // 2) if self.paired else block
        return ((step % groups * 2 + step // groups) * self.micro + inner) * self.capacity + rank

    def hop(self, values, step):
        return values if step == 0 else swap(values, "ep", step)

    def hops(self, values, group):
        half = values.shape[0] // 2
        return [self.hop(values[h * half : (h + 1) * half], group + h * (self.ep // 2)) for h in (0, 1)]

    def group_of(self, values, group):
        return self.piece(values, group * 2 * self.micro, 2 * self.micro)

    def home_to_expert(self, rows, extra, ahead=()):
        wide = rows.shape[1]
        few = extra.shape[0]
        count = self.micro * self.capacity
        out = []
        last = ()
        for group in range(self.ep // 2):
            got = []
            for u in (0, 1):
                at = (group * 2 + u) * self.micro
                more = self.piece(extra, at, self.micro, 1)
                message = jnp.concatenate(
                    [self.piece(rows, at, self.micro), jnp.pad(more, ((0, 0), (0, wide - count)))], axis=0
                )
                message = after(message, *last)
                if self.paired:
                    got.append(lax.ppermute(message, ("dp", "ep"), self.route(group, u, False)))
                else:
                    got.append(self.hop(message, group + u * (self.ep // 2)))
            last = tuple(got) + tuple(ahead)
            rows_got = [v[:count] for v in got]
            more_got = [v[count:, :count] for v in got]
            if self.paired:
                order = [(u, h) for h in (0, 1) for u in (0, 1)]
                rows_got = [self.piece(rows_got[u], h, 1) for u, h in order]
                more_got = [self.piece(more_got[u], h, 1, 1) for u, h in order]
            out.append((jnp.concatenate(rows_got, axis=0), jnp.concatenate(more_got, axis=1)))
        return out

    def expert_to_home(self, groups):
        messages = []
        for group, (rows, more) in enumerate(groups):
            wide = rows.shape[1]
            for u in (0, 1):
                if self.paired:
                    row = jnp.concatenate([self.piece(rows, 2 * h + u, 1) for h in (0, 1)], axis=0)
                    few = jnp.concatenate([self.piece(more, 2 * h + u, 1, 1) for h in (0, 1)], axis=1)
                else:
                    row, few = self.piece(rows, u * self.micro, self.micro), self.piece(more, u * self.micro, self.micro, 1)
                message = row
                if more.shape[0]:
                    message = jnp.concatenate([row, jnp.pad(few, ((0, 0), (0, wide - few.shape[1])))], axis=0)
                if self.paired:
                    messages.append(lax.ppermute(message, ("dp", "ep"), self.route(group, u, True)))
                else:
                    messages.append(self.hop(message, group + u * (self.ep // 2)))
        return messages

    def opened(self, messages):
        count = self.micro * self.capacity
        return (
            jnp.concatenate([v[:count] for v in messages], axis=0),
            jnp.concatenate([v[count:, :count] for v in messages], axis=1),
        )

    def ids_to_work(self, ids):
        if not self.paired:
            return ids
        values = jnp.swapaxes(ids, 1, 2).astype(jnp.float32)
        out = []
        for turn in (0, 1):
            pairs = []
            for d in range(self.dp):
                for z in range(self.ep):
                    m = (z % 2) ^ turn
                    pairs.append((d * self.ep + z, (d - d % 2 + z // 2) * self.ep + 2 * m + d % 2))
            block = lax.dynamic_index_in_dim(values, (self.z % 2) ^ turn, 0, keepdims=False)
            out.append(lax.ppermute(block, ("dp", "ep"), pairs))
        m = self.z // 2
        both = jnp.stack([jnp.where(m == 0, out[0], out[1]), jnp.where(m == 0, out[1], out[0])])
        return jnp.swapaxes(both, 1, 2).astype(jnp.int32)

    def places(self, lengths):
        counts = jnp.sum(lengths, axis=1).astype(jnp.float32)
        if self.paired:
            m = self.z // 2
            place = self.core * 2 * self.rows + jnp.arange(2 * self.rows, dtype=jnp.int32)
            group = self.d - self.core + self.z % 2
            return place, [lengths[m, group]], counts[m][None]
        place = self.z * self.rows + jnp.arange(self.rows, dtype=jnp.int32)
        return place, [lengths[m, self.d] for m in range(self.micro)], counts

    def gather(self, values):
        if self.paired:
            return jnp.concatenate([values, swap(values, "dp", 1)], axis=0)
        return lax.all_gather(values, "ep", axis=0, tiled=True)

    def key_places(self):
        if self.paired:
            base = jnp.arange(2 * self.rows, dtype=jnp.int32)
            return jnp.concatenate([base + self.core * 2 * self.rows, base + (1 - self.core) * 2 * self.rows])
        return jnp.arange(self.ep * self.rows, dtype=jnp.int32)

    def scatter(self, values):
        if self.paired:
            half = values.shape[1] // 2
            return values[:, :half] + swap(values[:, half:], "dp", 1)
        return lax.psum_scatter(values, "ep", scatter_dimension=1, tiled=True)

    def halo(self, values, width):
        length = values.shape[0]
        if self.paired:
            low = self.core == 0
            edge = jnp.where(low, values[length - width :], values[:width])
            other = swap(edge, "dp", 1)
            zero = jnp.zeros_like(other)
            before, after = jnp.where(low, zero, other), jnp.where(low, other, zero)
        else:
            up = [(i, i + 1) for i in range(self.ep - 1)]
            down = [(j, i) for i, j in up]
            before = lax.ppermute(values[length - width :], "ep", up)
            after = lax.ppermute(values[:width], "ep", down)
        return jnp.concatenate([before, values, after], axis=0)

    def batch_total(self, values):
        if self.paired:
            return butterfly(values, bits_of("dp") + [("ep", 1)])
        return butterfly(values, bits_of("dp") + bits_of("ep"))


def norm_rows(values, gain, shift):
    center = values - jnp.mean(values, axis=-1, keepdims=True)
    spread = jnp.mean(center * center, axis=-1, keepdims=True)
    return center * lax.rsqrt(spread + EPS) * gain + shift


def swish_slope(values):
    squash = jax.nn.sigmoid(values)
    return squash * (1.0 + values * (1.0 - squash))


def ranks(ids, experts):
    rows = ids.shape[1]
    onehot = (ids[..., None] == jnp.arange(experts, dtype=jnp.int32)).astype(jnp.float32)
    below = (jnp.arange(rows)[:, None] > jnp.arange(rows)[None, :]).astype(jnp.float32)
    before = jnp.einsum("rs,bse->bre", below, onehot)
    return jnp.sum(before * onehot, axis=2).astype(jnp.int32)


def tables_of(slot, count):
    spots = jnp.arange(count, dtype=jnp.int32)
    flat = slot.reshape(-1)
    return (
        (spots[:, None] == flat[None, :]).astype(jnp.bfloat16),
        (flat[:, None] == spots[None, :]).astype(jnp.bfloat16),
    )


def pick(table, values):
    return jnp.matmul(table.astype(jnp.float32), values, precision=HIGH)


def pick_columns(values, table):
    return jnp.matmul(values, table.astype(jnp.float32), precision=HIGH)


def product_two(left, right, dot):
    head, rest = parted(left)
    return dot(narrow(head), right) + dot(narrow(rest), right)


def exact_dot(left, right, contract):
    return lax.dot_general(
        left, right, (contract, ((), ())), precision=lax.Precision.HIGHEST, preferred_element_type=jnp.float32
    )


def norm_parts(values):
    center = values - jnp.mean(values, axis=1, keepdims=True)
    scale = lax.rsqrt(jnp.mean(center * center, axis=1, keepdims=True) + EPS)
    return center * scale, scale


def norm_back(grad, gain, normal, scale):
    weighed = grad * gain
    centred = weighed - jnp.mean(weighed, axis=1, keepdims=True)
    return scale * (centred - normal * jnp.mean(weighed * normal, axis=1, keepdims=True))


def gate_parts(hidden, extra, own, norm, router, experts):
    normal, scale = norm_parts(hidden)
    normed = normal * norm[0:1] + norm[1:2]
    lane = lax.broadcasted_iota(jnp.int32, (1, LANES), 1)
    logits = exact_dot(normed, router, ((1,), (0,))) + extra
    logits = jnp.where(lane < experts, logits, -FAR)
    raised = jnp.exp(logits - jnp.max(logits, axis=1, keepdims=True))
    probs = raised / jnp.sum(raised, axis=1, keepdims=True)
    return normal, scale, normed, probs, jnp.sum(probs * own, axis=1, keepdims=True)


def hidden_columns(weight_in):
    wide = min(512, weight_in.shape[1])
    return [pl.ds(at, wide) for at in range(0, weight_in.shape[1], wide)]


def forward_part(hidden, extra, own, norm, router, weight_in, weight_out, pre, experts):
    parts = gate_parts(hidden, extra, own, norm, router, experts)
    result = 0.0
    for now in hidden_columns(weight_in):
        before = product_two(parts[2], weight_in[:, now], dot_nn)
        pre[:, now] = before
        result = result + product_two(before * jax.nn.sigmoid(before), weight_out[now, :], dot_nn)
    return parts, result, hidden + 0.5 * parts[4] * result


def backward_part(grad, result, parts, own, norm, router, weight_in, weight_out, pre, active, grad_pre):
    normal, scale, normed, probs, gate = parts
    grad_result = 0.5 * gate * grad
    grad_gate = 0.5 * jnp.sum(grad * result, axis=1, keepdims=True)
    grad_logits = grad_gate * probs * (own - gate)
    grad_normed = exact_dot(grad_logits, router, ((1,), (1,)))
    for now in hidden_columns(weight_in):
        before = pre[:, now]
        squash = jax.nn.sigmoid(before)
        active[:, now] = before * squash
        slope = squash * (1.0 + before * (1.0 - squash))
        now_grad = product_two(grad_result, weight_out[now, :], dot_nt) * slope
        grad_pre[:, now] = now_grad
        grad_normed = grad_normed + product_two(now_grad, weight_in[:, now], dot_nt)
    sums = [jnp.sum(grad_normed * normal, axis=0, keepdims=True), jnp.sum(grad_normed, axis=0, keepdims=True)]
    return grad + norm_back(grad_normed, norm[0:1], normal, scale), grad_result, grad_logits, sums


def add_rows(out, rows):
    @pl.when(pl.program_id(0) == 0)
    def _():
        out[...] = jnp.zeros_like(out)

    for at, row in enumerate(rows):
        out[at : at + 1, :] += row


def forward_kernel(experts, hidden, extra, own, norm, router, weight_in, weight_out, new, result, pre):
    _, result[...], new[...] = forward_part(
        hidden[...], extra[...], own[...], norm[...], router[...], weight_in, weight_out, pre, experts
    )


def backward_kernel(
    experts, hidden, extra, grad, result, pre, own, norm, router, weight_in, weight_out,
    back, logits, normed, active, grad_result, grad_pre, sums,
):
    parts = gate_parts(hidden[...], extra[...], own[...], norm[...], router[...], experts)
    back[...], grad_result[...], logits[...], rows = backward_part(
        grad[...], result[...], parts, own[...], norm[...], router[...], weight_in, weight_out, pre, active, grad_pre
    )
    normed[...] = parts[2]
    add_rows(sums, rows)


def both_kernel(
    experts, hidden, extra, pull, own, norm, last, router, weight_in, weight_out,
    output, back, logits, normed, active, grad_result, grad_pre, sums, pre,
):
    parts, result, new = forward_part(
        hidden[...], extra[...], own[...], norm[...], router[...], weight_in, weight_out, pre, experts
    )
    lane = lax.broadcasted_iota(jnp.int32, (1, LANES), 1)
    valid = jnp.sum(jnp.where(lane == experts, extra[...], 0.0), axis=1, keepdims=True)
    normal, scale = norm_parts(new)
    output[...] = (normal * last[0:1] + last[1:2]) * valid
    grad = pull[...] * valid
    last_sums = [jnp.sum(grad * normal, axis=0, keepdims=True), jnp.sum(grad, axis=0, keepdims=True)]
    back[...], grad_result[...], logits[...], rows = backward_part(
        norm_back(grad, last[0:1], normal, scale), result, parts, own[...], norm[...], router[...],
        weight_in, weight_out, pre, active, grad_pre,
    )
    normed[...] = parts[2]
    add_rows(sums, rows + last_sums)


def expert_call(kernel, name, experts, by_rows, fixed, widths, sums, hold, products):
    rows, width = by_rows[0].shape
    block = min(256, rows)
    row_spec = lambda wide: pl.BlockSpec((block, wide), lambda i: (i, 0))
    full = lambda v: pl.BlockSpec(v.shape, lambda i: (0, 0))
    out_specs = [row_spec(wide) for wide in widths]
    out_shape = [jax.ShapeDtypeStruct((rows, wide), jnp.float32) for wide in widths]
    if sums:
        out_specs.append(pl.BlockSpec((8, width), lambda i: (0, 0)))
        out_shape.append(jax.ShapeDtypeStruct((8, width), jnp.float32))
    inner = fixed[-2].shape[1]
    return pl.pallas_call(
        functools.partial(kernel, experts),
        grid=(rows // block,),
        in_specs=[row_spec(v.shape[1]) for v in by_rows] + [full(v) for v in fixed],
        out_specs=out_specs,
        out_shape=out_shape,
        scratch_shapes=[pltpu.VMEM((block, inner), jnp.float32)] if hold else [],
        compiler_params=pltpu.CompilerParams(vmem_limit_bytes=48 * 1024 * 1024),
        cost_estimate=BRIEF,
        name=name,
    )(*by_rows, *fixed)


def lanes_of(extra):
    return jnp.pad(extra.T, ((0, 0), (0, LANES - extra.shape[0])))


def weight_kernel(groups, *refs):
    normed, grad_result, active, grad_pre = (refs[k * groups : (k + 1) * groups] for k in range(4))
    inner, outer = refs[4 * groups :]

    def summed(left, right):
        total = 0.0
        for one, two in zip(left, right):
            (a_hi, a_lo), (b_hi, b_lo) = parted(one[...]), parted(two[...])
            a_hi, a_lo, b_hi, b_lo = narrow(a_hi), narrow(a_lo), narrow(b_hi), narrow(b_lo)
            total = total + dot_tn(a_hi, b_hi) + dot_tn(a_lo, b_hi) + dot_tn(a_hi, b_lo)
        return total

    outer[...] = summed(active, grad_result)
    inner[...] = summed(normed, grad_pre)


def expert_weight_grads(kept):
    normed, active, grad_result, grad_pre = zip(*kept)
    rows, width = normed[0].shape
    inner = active[0].shape[1]
    wide = min(512, inner)
    full = pl.BlockSpec((rows, width), lambda i: (0, 0))
    part = pl.BlockSpec((rows, wide), lambda i: (0, i))
    count = len(kept)
    return pl.pallas_call(
        functools.partial(weight_kernel, count),
        grid=(inner // wide,),
        in_specs=[full] * (2 * count) + [part] * (2 * count),
        out_specs=[pl.BlockSpec((width, wide), lambda i: (0, i)), pl.BlockSpec((wide, width), lambda i: (i, 0))],
        out_shape=[
            jax.ShapeDtypeStruct((width, inner), jnp.float32),
            jax.ShapeDtypeStruct((inner, width), jnp.float32),
        ],
        compiler_params=pltpu.CompilerParams(vmem_limit_bytes=48 * 1024 * 1024),
        cost_estimate=pl.CostEstimate(
            flops=12 * count * rows * width * inner, bytes_accessed=16 * count * rows * inner, transcendentals=0
        ),
        name="weights",
    )(*normed, *grad_result, *active, *grad_pre)


def add_up(trees):
    total = trees[0]
    for tree in trees[1:]:
        total = jax.tree.map(jnp.add, total, tree)
    return total


def parted(values):
    head = values.astype(jnp.bfloat16).astype(jnp.float32)
    return head, values - head


def head_lanes(side):
    low = lax.broadcasted_iota(jnp.int32, (1, LANES), 1) < LANES // 2
    turn = lambda v: pltpu.roll(v, LANES // 2, 1)
    at_low = lambda v: v if side == 0 else turn(v)
    at_high = lambda v: turn(v) if side == 0 else v
    both = lambda v, w: jnp.where(low, at_low(v), at_high(w))
    alone = lambda v, rest=0.0: jnp.where(low, at_low(v), rest)
    return both, alone


def dot_nt(left, right):
    return lax.dot_general(left, right, (((1,), (1,)), ((), ())), preferred_element_type=jnp.float32)


def dot_tn(left, right):
    return lax.dot_general(left, right, (((0,), (0,)), ((), ())), preferred_element_type=jnp.float32)


def dot_nn(left, right):
    return lax.dot_general(left, right, (((1,), (0,)), ((), ())), preferred_element_type=jnp.float32)


def narrow(*parts):
    return jnp.concatenate(parts, axis=1).astype(jnp.bfloat16) if len(parts) > 1 else parts[0].astype(jnp.bfloat16)


def attend_kernel(chunk, scale, slopes, dist, q_ref, k_ref, v_ref, out_ref, log_ref, k3, v2, v1, scores):
    pair = pl.program_id(0)
    total = k_ref.shape[0]
    q_hi, q_lo = parted(q_ref[...] * scale)
    k_hi, k_lo = parted(k_ref[...])
    v_hi, v_lo = parted(v_ref[...])
    mixed = []
    for side in (0, 1):
        both, alone = head_lanes(side)
        k3[...] = narrow(both(k_hi, k_hi), alone(k_lo))
        v2[...] = narrow(both(v_hi, v_lo))
        v1[...] = narrow(alone(v_hi))
        q3 = narrow(both(q_hi, q_lo), alone(q_hi))
        slope = slopes[2 * pair + side]
        highest = None
        for at in range(0, total, chunk):
            now = pl.ds(at, chunk)
            score = dot_nt(k3[now], q3) - slope * dist[now]
            scores[now] = score
            top = jnp.max(score, axis=0, keepdims=True)
            highest = top if highest is None else jnp.maximum(highest, top)
        summed, weight = 0.0, 0.0
        for at in range(0, total, chunk):
            now = pl.ds(at, chunk)
            raised = jnp.exp(scores[now] - highest)
            weight = weight + jnp.sum(raised, axis=0, keepdims=True)
            r_hi, r_lo = parted(raised)
            summed = summed + dot_tn(v2[now], narrow(r_hi)) + dot_tn(v1[now], narrow(r_lo))
        mixed.append((summed[: LANES // 2] + summed[LANES // 2 :]) / weight)
        log_ref[0, side : side + 1, :] = highest + jnp.log(weight)
    out_ref[...] = jnp.concatenate(mixed, axis=0).T


def attend_back_kernel(
    chunk, scale, slopes, dist, q_ref, k_ref, v_ref, o_ref, g_ref, log_ref, dq_ref, dkv_ref, ds_ref, k3, v3, k2, k1, hold
):
    pair = pl.program_id(0)
    total = k_ref.shape[0]
    q_hi, q_lo = parted(q_ref[...] * scale)
    k_hi, k_lo = parted(k_ref[...])
    v_hi, v_lo = parted(v_ref[...])
    grad = g_ref[...]
    g_hi, g_lo = parted(grad)
    weighed = grad * o_ref[...]
    lane = lax.broadcasted_iota(jnp.int32, (1, LANES), 1)
    low = lane < LANES // 2
    half = LANES // 2
    grad_query = []
    for side in (0, 1):
        both, alone = head_lanes(side)
        own = low if side == 0 else jnp.logical_not(low)
        centre = -jnp.sum(jnp.where(own, weighed, 0.0), axis=1, keepdims=True)
        c_hi, c_rest = parted(centre)
        c_mid, c_lo = parted(c_rest)
        tail = jnp.where(lane == half, c_hi, jnp.where(lane == half + 1, c_mid, jnp.where(lane == half + 2, c_lo, 0.0)))
        ones = jnp.where(jnp.logical_and(lane >= half, lane < half + 3), 1.0, 0.0)
        k3[...] = narrow(both(k_hi, k_hi), alone(k_lo))
        v3[...] = narrow(both(v_hi, v_hi), alone(v_lo, ones))
        k2[...] = narrow(both(k_hi, k_lo))
        k1[...] = narrow(alone(k_hi))
        q3 = narrow(both(q_hi, q_lo), alone(q_hi))
        q2, q1 = narrow(both(q_hi, q_lo)), narrow(alone(q_hi))
        g3 = narrow(both(g_hi, g_lo), alone(g_hi, tail))
        g2, g1 = narrow(both(g_hi, g_lo)), narrow(alone(g_hi))
        slope = slopes[2 * pair + side]
        logs = log_ref[0, side : side + 1, :]
        slope_grad, query_grad = 0.0, 0.0
        for at in range(0, total, chunk):
            now = pl.ds(at, chunk)
            far = dist[now]
            probs = jnp.exp(dot_nt(k3[now], q3) - slope * far - logs)
            grad_score = probs * dot_nt(v3[now], g3)
            slope_grad = slope_grad + jnp.sum(grad_score * far, axis=0, keepdims=True)
            p_hi, p_lo = parted(probs)
            s_hi, s_lo = parted(grad_score)
            s_hi, s_lo = narrow(s_hi), narrow(s_lo)
            value_grad = dot_nn(narrow(p_hi), g2) + dot_nn(narrow(p_lo), g1)
            key_grad = dot_nn(s_hi, q2) + dot_nn(s_lo, q1)
            query_grad = query_grad + dot_tn(k2[now], s_hi) + dot_tn(k1[now], s_lo)
            value_grad = value_grad + pltpu.roll(value_grad, half, 1)
            key_grad = key_grad + pltpu.roll(key_grad, half, 1)
            if side == 0:
                hold[0, now], hold[1, now] = key_grad, value_grad
            else:
                dkv_ref[0, now] = jnp.where(low, hold[0, now], key_grad)
                dkv_ref[1, now] = jnp.where(low, hold[1, now], value_grad)
        grad_query.append(query_grad[:half] + query_grad[half:])
        ds_ref[0, side : side + 1, :] = slope_grad
    dq_ref[...] = jnp.concatenate(grad_query, axis=0).T * scale


def attend_specs(rows, total, pairs):
    lanes = lambda at: pl.BlockSpec((rows, LANES), lambda i, at=at: (0, at + i))
    wide = lambda at: pl.BlockSpec((total, LANES), lambda i, at=at: (0, at + i))
    return [
        pl.BlockSpec(memory_space=pltpu.SMEM),
        pl.BlockSpec((total, rows), lambda i: (0, 0)),
        lanes(0),
        wide(0),
        wide(pairs),
    ], lanes(0), pl.BlockSpec((1, 8, rows), lambda i: (i, 0, 0))


def attend_params(rows, total, width, passes):
    return dict(
        compiler_params=pltpu.CompilerParams(vmem_limit_bytes=40 * 1024 * 1024),
        cost_estimate=BRIEF,
    )


def attend(packed, both, dist, slopes):
    rows, total = packed.shape[0], both.shape[0]
    width = both.shape[1] // 2
    pairs = width // LANES
    chunk = min(total, 256)
    in_specs, lanes, logs = attend_specs(rows, total, pairs)
    return pl.pallas_call(
        functools.partial(attend_kernel, chunk, (width // slopes.shape[0]) ** -0.5),
        grid=(pairs,),
        in_specs=in_specs,
        out_specs=[lanes, logs],
        out_shape=[
            jax.ShapeDtypeStruct((rows, width), jnp.float32),
            jax.ShapeDtypeStruct((pairs, 8, rows), jnp.float32),
        ],
        scratch_shapes=[
            pltpu.VMEM((total, 2 * LANES), jnp.bfloat16),
            pltpu.VMEM((total, LANES), jnp.bfloat16),
            pltpu.VMEM((total, LANES), jnp.bfloat16),
            pltpu.VMEM((total, rows), jnp.float32),
        ],
        name="attend",
        **attend_params(rows, total, width, 12),
    )(slopes, dist, packed, both, both)


def attend_back(packed, both, dist, slopes, mixed, logs, grad_mixed):
    rows, total = packed.shape[0], both.shape[0]
    width = both.shape[1] // 2
    pairs = width // LANES
    chunk = min(total, 256)
    in_specs, lanes, log_spec = attend_specs(rows, total, pairs)
    dq, dkv, ds = pl.pallas_call(
        functools.partial(attend_back_kernel, chunk, (width // slopes.shape[0]) ** -0.5),
        grid=(pairs,),
        in_specs=in_specs + [lanes, lanes, log_spec],
        out_specs=[lanes, pl.BlockSpec((2, total, LANES), lambda i: (0, 0, i)), log_spec],
        out_shape=[
            jax.ShapeDtypeStruct((rows, width), jnp.float32),
            jax.ShapeDtypeStruct((2, total, width), jnp.float32),
            jax.ShapeDtypeStruct((pairs, 8, rows), jnp.float32),
        ],
        scratch_shapes=[
            pltpu.VMEM((total, 2 * LANES), jnp.bfloat16),
            pltpu.VMEM((total, 2 * LANES), jnp.bfloat16),
            pltpu.VMEM((total, LANES), jnp.bfloat16),
            pltpu.VMEM((total, LANES), jnp.bfloat16),
            pltpu.VMEM((2, total, LANES), jnp.float32),
        ],
        name="attend_back",
        **attend_params(rows, total, width, 30),
    )(slopes, dist, packed, both, both, mixed, grad_mixed, logs)
    return dq, dkv, -jnp.sum(ds[:, :2], axis=2).reshape(-1)


def body(
    frames,
    embedding,
    cotangent,
    expert_ids,
    lengths,
    norm_gain,
    norm_bias,
    router,
    attention_in,
    attention_out,
    slopes,
    conv_point,
    conv_depth,
    batch_gain,
    batch_bias,
    conv_out,
    expert_in,
    expert_out,
):
    packed_weight = attention_in.astype(jnp.float32)
    mixing_weight = attention_out.astype(jnp.float32)
    point_weight = conv_point.astype(jnp.float32)
    project_weight = conv_out.astype(jnp.float32)
    inner_weight = [expert_in[b, 0] for b in (0, 1)]
    outer_weight = [expert_out[b, 0] for b in (0, 1)]
    micro, rows, width = frames.shape
    experts = router.shape[2]
    heads = slopes.shape[0]
    kernel = conv_depth.shape[0]
    half = kernel // 2
    capacity = 2 * rows // experts
    everyone = bits_of("dp") + bits_of("ep")
    layout = Layout(micro, rows, capacity)
    place, part_lengths, counts = layout.places(lengths)
    key_place = layout.key_places()
    parts = len(part_lengths)
    part_rows = micro * rows // parts
    valid_f = jnp.concatenate([(place < length) for length in part_lengths]).astype(jnp.float32)[:, None]
    to_parts = lambda v: v.reshape((parts, part_rows) + v.shape[1:])
    spread = lambda v: jnp.broadcast_to(v[:, None], (parts, part_rows) + v.shape[1:]).reshape(parts * part_rows, -1)

    slots = experts * micro * capacity
    own = (jnp.arange(LANES, dtype=jnp.int32) == layout.z).astype(jnp.float32)[None, :]
    norms = [jnp.stack([norm_gain[i], norm_bias[i]]) for i in range(norm_gain.shape[0])]
    routers = [jnp.pad(router[b], ((0, 0), (0, LANES - experts))) for b in (0, 1)]
    wide = inner_weight[0].shape[1]
    ids = jnp.moveaxis(expert_ids[..., 0], 0, 2)
    rank = [ranks(ids[..., b], experts) for b in (0, 1)]
    home = [tables_of(layout.home_slots(ids[..., b], rank[b]), slots) for b in (0, 1)]
    groups = range(experts // 2)
    home_rows = embedding.reshape(-1, width)
    home_logits = [product(router[b].T, home_rows.T) for b in (0, 1)]
    home_place = layout.z * rows + jnp.arange(rows, dtype=jnp.int32)
    home_valid = (home_place[None, :] < lengths[:, layout.d][:, None]).astype(jnp.float32).reshape(1, -1)
    spare = jnp.zeros((-(experts + 1) % 8, micro * rows), jnp.float32)
    extras = [
        pick_columns(jnp.concatenate([home_logits[b], home_valid, spare], axis=0), home[b][1]) for b in (0, 1)
    ]

    work_ids = layout.ids_to_work(ids)
    sources = layout.home_to_expert(pick(home[0][0], frames.reshape(-1, width)), extras[0], (work_ids,))
    kept_first = []
    back = []
    last = ()
    for group in groups:
        hidden, extra = sources[group]
        hidden, extra = after(hidden, *last), lanes_of(extra)
        fixed = (own, norms[0], routers[0], inner_weight[0], outer_weight[0])
        new, result, pre = expert_call(
            forward_kernel, "forward", experts, (hidden, extra), fixed, (width, width, wide), False, False, 2
        )
        last = (new,)
        kept_first.append(((hidden, extra), (result, pre), fixed))
        back += layout.hops(new, group)
    work = [
        tables_of(layout.work_slots(work_ids[..., b], ranks(work_ids[..., b], experts)), slots) for b in (0, 1)
    ]
    first = pick(work[0][1], jnp.concatenate(back, axis=0))

    def attention_front(values, gain_now, shift_now, weight_now):
        return product(norm_rows(values, gain_now, shift_now), weight_now)

    packed, attention_pull = jax.vjp(attention_front, first, norm_gain[1], norm_bias[1], packed_weight)
    packed, cot_rows = lax.optimization_barrier((packed, cotangent.reshape(-1, width)))
    pulls = layout.home_to_expert(pick(home[1][0], cot_rows), extras[1])
    packed_parts = to_parts(packed)
    apart = jnp.abs(key_place[:, None] - place[None, :]).astype(jnp.float32)
    kept_attention = []
    mixed_parts = []
    for part in range(parts):
        both = layout.gather(packed_parts[part, :, width:])
        dist = jnp.where((key_place < part_lengths[part])[:, None], apart, FAR)
        mixed, logs = attend(packed_parts[part], both, dist, slopes)
        kept_attention.append((both, dist, mixed, logs))
        mixed_parts.append(mixed)
    mixed_all = jnp.concatenate(mixed_parts, axis=0)
    second = first + product(mixed_all, mixing_weight)

    def conv_front(values, gain_now, shift_now, point_now):
        both = product(norm_rows(values, gain_now, shift_now), point_now)
        return both[:, :width] * jax.nn.sigmoid(both[:, width:]) * valid_f

    gated, conv_pull = jax.vjp(conv_front, second, norm_gain[2], norm_bias[2], point_weight)
    padded = [layout.halo(v, half) for v in to_parts(gated)]
    conv_parts = []
    for part in range(parts):
        total = conv_depth[0] * padded[part][0:part_rows]
        for offset in range(1, kernel):
            total = total + conv_depth[offset] * padded[part][offset : offset + part_rows]
        conv_parts.append(total)
    conv = jnp.concatenate(conv_parts, axis=0)
    stats = layout.batch_total(
        jnp.stack([jnp.sum(to_parts(conv * valid_f), axis=1), jnp.sum(to_parts(conv * conv * valid_f), axis=1)], axis=1)
    )
    centre = stats[:, 0] / counts[:, None]
    inverse_dev = lax.rsqrt(stats[:, 1] / counts[:, None] - centre * centre + EPS)
    scaled = (conv - spread(centre)) * spread(inverse_dev)
    shaped = scaled * batch_gain + batch_bias
    swished = jax.nn.silu(shaped)
    third = second + product(swished, project_weight)

    sent = pick(work[1][0], third)
    results, back, kept, small = [], [], [], []
    arrived, last = (), ()
    for group in groups:
        hidden = layout.hops(after(layout.group_of(sent, group), *arrived), group)
        arrived = tuple(hidden)
        pull_now, extra = pulls[group]
        result, grad, grad_logits, normed, active, grad_result, grad_pre, sums = expert_call(
            both_kernel,
            "both",
            experts,
            (jnp.concatenate(after(hidden, *last), axis=0), lanes_of(extra), pull_now),
            (own, norms[3], norms[4], routers[1], inner_weight[1], outer_weight[1]),
            (width, width, LANES, width, wide, width, wide),
            True,
            True,
            4,
        )
        last = (grad,)
        results.append((result, grad_logits[:, : experts + (-experts % 8)].T))
        kept.append((normed, active, grad_result, grad_pre))
        small.append((sums, product(normed.T, grad_logits[:, :experts])))
        back += layout.hops(grad, group)
    sums, router_one = add_up(small)
    gain_three, shift_three, gain_four, shift_four = (sums[k] for k in range(4))
    kept, _ = lax.optimization_barrier((kept, back[:-2]))
    expert_one = lax.psum(expert_weight_grads(kept), "dp")
    grad_third = pick(work[1][1], jnp.concatenate(back, axis=0))
    project_grad = product(swished.T, grad_third)
    grad_shaped = product(grad_third, project_weight.T) * swish_slope(shaped)
    sums = jnp.stack(
        [jnp.sum(to_parts(grad_shaped), axis=1), jnp.sum(to_parts(grad_shaped * scaled), axis=1)], axis=1
    )
    totals = layout.batch_total(sums)
    shift_total, gain_total = totals[:, 0], totals[:, 1]
    results, _ = lax.optimization_barrier((results, totals))
    output_slots, logit_slots = layout.opened(layout.expert_to_home(results))
    output = pick(home[1][1], output_slots).reshape(micro, rows, width)
    logit_one = pick_columns(logit_slots[:experts], home[1][0])
    router_one = router_one + product(logit_one, home_rows).T
    grad_conv = (
        batch_gain
        * spread(inverse_dev)
        * (grad_shaped - valid_f * (spread(shift_total) + scaled * spread(gain_total)) / spread(counts[:, None]))
    )
    depth_grad = 0.0
    gated_parts = []
    for part, now in enumerate(to_parts(grad_conv)):
        grad_pad = layout.halo(now, half)
        total = conv_depth[0] * grad_pad[2 * half : 2 * half + part_rows]
        for offset in range(1, kernel):
            total = total + conv_depth[offset] * grad_pad[2 * half - offset : 2 * half - offset + part_rows]
        gated_parts.append(total)
        depth_grad = depth_grad + jnp.stack(
            [jnp.sum(now * padded[part][offset : offset + part_rows], axis=0) for offset in range(kernel)]
        )
    grad_hidden, gain_two, shift_two, point_grad = conv_pull(jnp.concatenate(gated_parts, axis=0))
    grad_second = grad_third + grad_hidden

    mixing_grad = product(mixed_all.T, grad_second)
    grad_mixed = to_parts(product(grad_second, mixing_weight.T))
    packed_back = []
    slope_grad = 0.0
    for part in range(parts):
        both, dist, mixed, logs = kept_attention[part]
        grad_query, grad_both, slope_now = attend_back(
            packed_parts[part], both, dist, slopes, mixed, logs, grad_mixed[part]
        )
        slope_grad = slope_grad + slope_now
        grad_both = layout.scatter(grad_both)
        packed_back.append(jnp.concatenate([grad_query, grad_both[0], grad_both[1]], axis=1))
    grad_hidden, gain_one, shift_one, packed_grad = attention_pull(jnp.concatenate(packed_back, axis=0))
    grad_first = grad_second + grad_hidden
    early = jnp.concatenate(
        [
            jnp.stack([gain_one, gain_two, gain_three, gain_four, shift_one, shift_two, shift_three, shift_four]),
            router_one.T,
            jnp.pad(slope_grad, (0, width - heads))[None],
            depth_grad,
            jnp.sum(sums, axis=0),
        ],
        axis=0,
    )
    dense = DenseSum(
        [jnp.concatenate([packed_grad, project_grad], axis=1), jnp.concatenate([mixing_grad, point_grad], axis=1)]
    )
    over_dp, over_ep = len(bits_of("dp")), len(bits_of("ep"))

    sent = pick(work[0][0], grad_first)
    sources, kept, small = [], [], []
    arrived, last = (), ()
    for group in groups:
        grad = layout.hops(after(layout.group_of(sent, group), *arrived), group)
        arrived = tuple(grad)
        grad = after(grad, *last)
        if group == 0:
            grad, expert_one = lax.optimization_barrier((dense.step(grad), expert_one))
        if group == 1:
            grad = dense.step(grad)
        (hidden, extra), saved, fixed = kept_first[group]
        new, grad_logits, normed, active, grad_result, grad_pre, sums = expert_call(
            backward_kernel,
            "backward",
            experts,
            (hidden, extra, jnp.concatenate(grad, axis=0)) + saved,
            fixed,
            (width, LANES, width, wide, width, wide),
            True,
            False,
            2,
        )
        if group == 0:
            new = dense.step(new, over_dp - 2)
        if group == 1:
            new = dense.step(new, over_ep - 1)
        last = (new,)
        sources.append((new, grad_logits[:, : experts + (-experts % 8)].T))
        kept.append((normed, active, grad_result, grad_pre))
        small.append((sums, product(normed.T, grad_logits[:, :experts])))
    sums, router_zero = add_up(small)
    gain_zero, shift_zero = sums[0], sums[1]
    expert_zero = lax.psum(expert_weight_grads(kept), "dp")
    sources = dense.step(sources, over_ep + 1)
    frame_messages = layout.expert_to_home(sources)
    wholes = [lax.pad(one[None], 0.0, ((1, 0, 0), (0, 0, 0), (0, 0, 0))) for one in expert_one]
    frame_messages, wholes = dense.step((frame_messages, wholes), over_dp - 1)
    rows_back, logit_slots = layout.opened(frame_messages)
    logit_zero = pick_columns(logit_slots[:experts], home[0][0])
    router_zero = router_zero + product(logit_zero, home_rows).T
    frames_grad = pick(home[0][1], rows_back).reshape(micro, rows, width)
    late = jnp.concatenate([gain_zero[None], shift_zero[None], router_zero.T, early], axis=0)
    one, two = dense.parts
    pieces = [one[:, : 3 * width], one[:, 3 * width :], two[:, :width], two[:, width:]]
    pieces = [join(piece, bits_of("dp")[0]) for piece in pieces]
    late, pieces = lax.optimization_barrier((late, pieces))
    packed_grad, project_grad, mixing_grad, point_grad = pieces
    late = butterfly(late, bits_of("ep") + bits_of("dp"))
    late, early = late[: 2 + experts], late[2 + experts :]
    expert_grads = []
    for zero, whole in zip(expert_zero, wholes):
        expert_grads.append(lax.dynamic_update_slice(whole, zero[None], (0, 0, 0))[:, None])

    at = 8 + experts
    gain_grad = jnp.concatenate([late[:1], early[:4]], axis=0)
    shift_grad = jnp.concatenate([late[1:2], early[4:8]], axis=0)
    router_grad = jnp.stack([late[2 : 2 + experts].T, early[8:at].T])
    return (
        output,
        frames_grad,
        gain_grad,
        shift_grad,
        router_grad,
        packed_grad,
        mixing_grad,
        early[at, :heads],
        point_grad,
        early[at + 1 : at + 1 + kernel],
        early[at + 2 + kernel],
        early[at + 1 + kernel],
        project_grad,
        expert_grads[0],
        expert_grads[1],
    )


def solution(mesh):
    rows = P(None, ("dp", "ep"), None)
    whole = P()
    split = P(None, "ep", None, None)
    return jax.shard_map(
        body,
        mesh=mesh,
        in_specs=(rows, rows, rows, P(None, None, ("dp", "ep"), None)) + (whole,) * 12 + (split, split),
        out_specs=(rows, rows) + (whole,) * 11 + (split, split),
        check_vma=False,
    )
```
